32 devices in a mesh: groups: 2 (over x), dp: 16 (over z, y, core).
Axes of the slice: x: 2, y: 2, z: 4, core: 2. Of those that a mesh axis runs over, the one named last changes fastest.
Arguments:
- hidden: bfloat16 [768, 4096], P(('groups', 'dp')), parts along dimension 0, may hold values from -6 to 6
- in_weight: bfloat16 [4096, 16384], P(None, 'dp'), may hold values from -0.09375 to 0.09375
- dt_weight: bfloat16 [32, 4096], P('dp'), may hold values from -0.09375 to 0.09375
- dt_bias: float32 [32], P('dp'), may hold values from -4 to -2
- decay_rate: float32 [32], P('dp'), may hold values from 0.003 to 0.5
- conv_weight: bfloat16 [4, 12288], P(None, 'dp'), may hold values from -3 to 3
- conv_bias: bfloat16 [12288], P('dp'), may hold values from -3 to 3
- skip: float32 [32], P('dp'), may hold values from 0.5 to 1.5
- norm_gain: bfloat16 [4096], P('dp'), may hold values from 0.099609375 to 1.8984375
- out_weight: bfloat16 [4096, 4096], P('dp'), may hold values from -0.09375 to 0.09375
- state_pool: bfloat16 [1024, 32, 128], P(('groups', 'dp')), parts along dimension 0, may hold values from -2 to 2
- conv_pool: bfloat16 [1024, 3, 96], P(('groups', 'dp')), parts along dimension 0, may hold values from -6 to 6
- hit_page: int32 [4, 32, 4], P('groups'), parts along dimension 0, may hold values from 0 to 511, as said below
- prefix_blocks: int32 [4], P('groups'), parts along dimension 0, may hold values from 1 to 2
- owners: int32 [32], P('groups'), parts along dimension 0, may hold values from 0 to 15, each once
Outputs:
- mixed: bfloat16 [768, 4096], P(('groups', 'dp')), parts along dimension 0
- final_state: float32 [4, 32, 128, 128], P('groups', 'dp'), parts along dimension 0
- final_conv: bfloat16 [4, 3, 12288], P('groups', None, 'dp'), parts along dimension 0
The draws below stay inside these ranges and needn't reach their ends.
There are 2 independent parts, one for each index of `groups`. The reference program is written for one: setup_inputs(seed, part) draws one part's arguments, and reference() takes and returns one part's arrays. A program takes and returns all parts, laid end to end along the dimension named above; an argument that names none is the same for every part. Nothing has to cross between parts.
Inputs may be any that keep to these rules, and one draw needn't show every extreme that they name: All entries differ. Call rows d * 32 to d * 32 + 31 of the pools the block of holder d. For every index e of dp, of the entries hit_page[r, h, p] with h // 2 = e, at most 2 lie in the block of any one holder; in every draw some holder's block holds exactly 2 of them, and some block has all 32 of its rows named.
All inputs are finite; a program needn't handle non-finite values.
Results may differ from the reference program's by a relative error of at most 0.008.
Values may be sent and summed in bfloat16 or wider, within the bound.
No kernel may reach another device: no remote copies, remote signals or barrier semaphores. Data moves between devices by JAX's collectives and lax.ppermute only.
A program may use at most 64 MiB of HBM per device.

```python
import jax
import jax.numpy as jnp
from jax import lax

D = 4096
HEAD_DIM = 128
STATE = 128
CONV = 4
HEAD_DEV = 2
HEADS = 32
REQS = 2
SPAN = 192
BLK = 64
TOKENS = 384
TOK_DEV = 24
PIECES = 4
SLOTS = 32
N_DP = 16


def draw_decay_rate(key, part):
    key = jax.random.fold_in(key, 5)
    spread = jax.random.uniform(key, (HEADS,), jnp.float32)
    return jnp.exp(jnp.log(0.01) + spread * (jnp.log(0.5) - jnp.log(0.01)))


def draw_hit_page(key, part):
    key = jax.random.fold_in(key, 11)
    device_count = HEADS // HEAD_DEV
    hot_count = device_count // 4
    cold_count = device_count - hot_count
    holder_key, shuffle_key = jax.random.split(key, 2)
    holder_order = jax.random.permutation(holder_key, device_count)
    hot_holders = holder_order[:hot_count]
    cold_holders = holder_order[hot_count:]
    receivers = jnp.arange(device_count)
    entries = jnp.arange(device_count)
    paired = entries < 2 * hot_count
    hot_rank = jnp.minimum(entries // 2, hot_count - 1)
    cold_rank = jnp.maximum(entries - 2 * hot_count, 0)
    cold_place = (receivers[:, None] + cold_rank[None, :]) % cold_count
    holder = jnp.where(paired[None, :], hot_holders[hot_rank][None, :], cold_holders[cold_place])
    in_block = jnp.where(paired[None, :], 2 * receivers[:, None] + (entries % 2)[None, :], receivers[:, None] + 0 * entries[None, :])
    pages = holder * SLOTS + in_block
    shuffles = jax.vmap(lambda one_key: jax.random.permutation(one_key, device_count))(jax.random.split(shuffle_key, device_count))
    pages = jnp.take_along_axis(pages, shuffles, axis=1)
    pages = pages.reshape(device_count, REQS, HEAD_DEV, PIECES).transpose(1, 0, 2, 3).reshape(REQS, HEADS, PIECES)
    return pages.astype(jnp.int32)


def block_scale(own_key, shape, shards, low, high):
    def one(axis_at, blocks):
        steps = jax.random.uniform(jax.random.fold_in(jax.random.fold_in(own_key, 6), axis_at), (blocks,), jnp.float32, low / len(shards), high / len(shards))
        return jnp.repeat(jnp.exp(steps), shape[axis_at] // blocks).reshape((-1,) + (1,) * (len(shape) - axis_at - 1))

    gain = one(*shards[0])
    for cut in shards[1:]:
        gain = gain * one(*cut)
    return gain


def centred(key, extent, scale, bound, cuts=(), held_as=jnp.bfloat16):
    values = jax.random.normal(key, extent, jnp.float32) * scale
    if len(cuts) > 0:
        values = block_scale(key, extent, cuts, -0.22, 0.18) * values
    return jnp.clip(values, min=-bound, max=bound).astype(held_as)


def setup_inputs(seed: int = 0, part: int = 0) -> dict:
    seeds = jax.random.split(jax.random.key(seed), 16)
    part_splits = jax.random.split(jax.random.fold_in(seeds[15], part), 16)
    return {
        "hidden": centred(part_splits[0], (TOKENS, D), 1.0, 6.0, ((0, 16),)),
        "in_weight": centred(seeds[1], (D, HEADS * (2 * HEAD_DIM + 2 * STATE)), D ** -0.5, 0.09375, ((1, 16),)),
        "dt_weight": centred(seeds[2], (HEADS, D), D ** -0.5, 0.09375, ((0, 16),)),
        "dt_bias": jnp.clip(-4.0 + 2.0 * jax.random.uniform(seeds[3], (HEADS,), jnp.float32) ** block_scale(seeds[3], (HEADS,), ((0, 16),), -0.2, 0.2), -4.0, -2.0),
        "decay_rate": draw_decay_rate(jax.random.fold_in(seeds[15], 71), part),
        "conv_weight": centred(seeds[5], (CONV, HEADS * (HEAD_DIM + 2 * STATE)), CONV ** -0.5, 3.0, ((1, 16),)),
        "conv_bias": centred(seeds[6], (HEADS * (HEAD_DIM + 2 * STATE),), 0.5, 3.0, ((0, 16),)),
        "skip": jnp.clip(0.5 + 1.0 * jax.random.uniform(seeds[7], (HEADS,), jnp.float32) ** block_scale(seeds[7], (HEADS,), ((0, 16),), -0.2, 0.2), 0.5, 1.5),
        "norm_gain": jnp.clip(1.0 + 0.18 * jax.random.normal(seeds[8], (HEADS * HEAD_DIM,), jnp.float32), 0.099609375, 1.8984375).astype(jnp.bfloat16),
        "out_weight": centred(seeds[9], (HEADS * HEAD_DIM, D), (HEADS * HEAD_DIM) ** -0.5, 0.09375, ((0, 16),)),
        "state_pool": centred(part_splits[10], (N_DP * SLOTS, HEAD_DIM // PIECES, STATE), 0.3, 2.0, ((0, 16),)),
        "conv_pool": centred(part_splits[11], (N_DP * SLOTS, CONV - 1, (HEAD_DIM + 2 * STATE) // PIECES), 1.0, 6.0, ((0, 16),)),
        "hit_page": draw_hit_page(jax.random.fold_in(jax.random.fold_in(seeds[15], part), 71), part),
        "prefix_blocks": jax.random.randint(part_splits[13], (REQS,), 1, SPAN // BLK).astype(jnp.int32),
        "owners": jax.random.permutation(part_splits[14], N_DP).astype(jnp.int32),
    }


EPSILON = 1e-05

def to_front(array):
    return jnp.moveaxis(array, 1, 0)

def reference(hidden, in_weight, dt_weight, dt_bias, decay_rate, conv_weight, conv_bias, skip, norm_gain, out_weight, state_pool, conv_pool, hit_page, prefix_blocks, owners):
    row_width = 2 * HEAD_DIM + 2 * STATE
    channels = HEAD_DIM + 2 * STATE
    projected = jnp.dot(hidden, in_weight, preferred_element_type=jnp.float32).astype(jnp.bfloat16)
    projected = projected.reshape(REQS, SPAN, HEADS, row_width)
    time_step = jax.nn.softplus(jnp.dot(hidden, dt_weight.T, preferred_element_type=jnp.float32) + dt_bias)
    time_step = time_step.reshape(REQS, SPAN, HEADS)
    live_start = (prefix_blocks * BLK).astype(jnp.int32)
    positions = jnp.arange(SPAN, dtype=jnp.int32)
    live_mask = positions[None, :] >= live_start[:, None]
    live_float = live_mask.astype(jnp.float32)
    initial = state_pool[hit_page].astype(jnp.float32).reshape(REQS, HEADS, HEAD_DIM, STATE)
    cached = jnp.transpose(conv_pool[hit_page].astype(jnp.float32), (0, 1, 3, 2, 4)).reshape(REQS, HEADS, CONV - 1, channels)
    conv_input = jnp.where(live_mask[:, :, None, None], projected[..., HEAD_DIM:].astype(jnp.float32), jnp.float32(0.0))
    for lag_row in range(CONV - 1):
        position_hit = positions[None, :] == live_start[:, None] - (CONV - 1) + lag_row
        conv_input = jnp.where(position_hit[:, :, None, None], cached[:, None, :, lag_row, :], conv_input)
    padded = jnp.pad(conv_input, ((0, 0), (CONV - 1, 0), (0, 0), (0, 0)))
    taps = conv_weight.astype(jnp.float32).reshape(CONV, HEADS, channels)
    conv_sum = jnp.broadcast_to(conv_bias.astype(jnp.float32).reshape(HEADS, channels), conv_input.shape)
    for tap_index in range(CONV):
        conv_sum = conv_sum + taps[tap_index] * padded[:, tap_index:tap_index + SPAN]
    conv_out = jax.nn.silu(conv_sum).astype(jnp.bfloat16)
    x_part = conv_out[..., :HEAD_DIM].astype(jnp.float32)
    b_part = conv_out[..., HEAD_DIM:HEAD_DIM + STATE].astype(jnp.float32)
    c_part = conv_out[..., HEAD_DIM + STATE:].astype(jnp.float32)
    step_size = time_step * live_float[:, :, None]
    decays = jnp.exp(-decay_rate * step_size)

    def advance(carried, step_inputs):
        decay_now, size_now, x_now, b_now, c_now = step_inputs
        carried = decay_now[:, :, None, None] * carried + (size_now[:, :, None] * x_now)[..., None] * b_now[:, :, None, :]
        return (carried, jnp.einsum('rhpn,rhn->rhp', carried, c_now, precision=lax.Precision.HIGHEST))
    final_state, outputs = lax.scan(advance, initial, (to_front(decays), to_front(step_size), to_front(x_part), to_front(b_part), to_front(c_part)))
    outputs = jnp.moveaxis(outputs, 0, 1) + skip[:, None] * x_part
    gate_part = projected[..., :HEAD_DIM].astype(jnp.float32)
    gated = outputs * jax.nn.silu(gate_part)
    inverse_rms = lax.rsqrt(lax.optimization_barrier(jnp.mean(gated * gated, axis=-1, keepdims=True)) + EPSILON)
    normed = (gated * inverse_rms * norm_gain.astype(jnp.float32).reshape(HEADS, HEAD_DIM) * live_float[:, :, None, None]).astype(jnp.bfloat16)
    summed = jnp.dot(normed.reshape(TOKENS, HEADS * HEAD_DIM), out_weight, preferred_element_type=jnp.float32).astype(jnp.bfloat16)
    mixed = jnp.zeros((N_DP, TOK_DEV, D), jnp.bfloat16).at[owners].set(summed.reshape(N_DP, TOK_DEV, D)).reshape(TOKENS, D)
    final_conv = projected[:, SPAN - (CONV - 1):, :, HEAD_DIM:].reshape(REQS, CONV - 1, HEADS * channels)
    return (mixed, final_state, final_conv)
```

```python
import jax
import jax.numpy as jnp
import numpy as np
from jax import lax
from jax.sharding import PartitionSpec as P

HEAD_DIM = 128
STATE = 128
CONV = 4
REQS = 2
SPAN = 192
BLK = 64


EPSILON = 1e-05


def split_pair(values):
    upper_part = values.astype(jnp.bfloat16)
    lower_part = (values - upper_part.astype(jnp.float32)).astype(jnp.bfloat16)
    return (upper_part, lower_part)


def ring_order(chip_count):
    if chip_count <= 8:
        return list(range(0, chip_count, 2)) + list(range(chip_count - 1, 0, -2))
    return list(range(chip_count))


def gather_plan(chip_count, order, live_chip):
    half = chip_count // 2
    up_load = [0] * chip_count
    down_load = [0] * chip_count
    up_reach = [0] * chip_count
    down_reach = [0] * chip_count
    live_places = [p for p in range(chip_count) if live_chip[order[p]]]
    for p in live_places:
        for hop in range(half - 1):
            up_load[(p + hop) % chip_count] += 1
            down_load[(p - hop) % chip_count] += 1
        up_reach[p] = half - 1
        down_reach[p] = half - 1
    for p in live_places:
        up_last = (p + half - 1) % chip_count
        down_last = (p - half + 1) % chip_count
        if up_load[up_last] <= down_load[down_last]:
            up_load[up_last] += 1
            up_reach[p] = half
        else:
            down_load[down_last] += 1
            down_reach[p] = half
    return up_reach, down_reach


def hop_pairs(order, places, shift):
    count = len(order)
    return [
        (2 * order[p] + core, 2 * order[(p + shift) % count] + core)
        for p in places
        for core in range(2)
    ]


def other_core(array, device_count):
    return lax.ppermute(array, "dp", [(d, d ^ 1) for d in range(device_count)])


def offer_pages(page_ids, state_pool, conv_pool, my_index, per_peer):
    pool_slots = state_pool.shape[0]
    holders = page_ids // pool_slots
    in_slot = page_ids % pool_slots
    order_ids = jnp.arange(page_ids.shape[1])
    same_holder = holders[:, :, None] == holders[:, None, :]
    earlier = order_ids[None, :] < order_ids[:, None]
    holder_rank = jnp.sum((same_holder & earlier[None]).astype(jnp.int32), axis=2)
    chosen = (holders == my_index)[:, None, :] & (
        holder_rank[:, None, :] == jnp.arange(per_peer)[None, :, None]
    )
    picked = jnp.sum(jnp.where(chosen, in_slot[:, None, :], 0), axis=2)
    present = jnp.any(chosen, axis=2)
    ssm_pages = jnp.where(
        present[:, :, None, None], state_pool[picked], jnp.zeros((), state_pool.dtype)
    )
    conv_pages = jnp.where(
        present[:, :, None, None], conv_pool[picked], jnp.zeros((), conv_pool.dtype)
    )
    my_rows = lax.dynamic_index_in_dim(
        holders * per_peer + holder_rank, my_index, 0, keepdims=False
    )
    return (ssm_pages, conv_pages, my_rows)


def body(
    hidden,
    in_weight,
    dt_weight,
    dt_bias,
    decay_rate,
    conv_weight,
    conv_bias,
    skip,
    norm_gain,
    out_weight,
    state_pool,
    conv_pool,
    hit_page,
    prefix_blocks,
    owners,
):
    device_count = lax.axis_size("dp")
    my_index = lax.axis_index("dp")
    heads_dev = dt_weight.shape[0]
    piece_count = hit_page.shape[2]
    per_peer = 2
    row_width = 2 * HEAD_DIM + 2 * STATE
    channels = HEAD_DIM + 2 * STATE
    rows_dev = hidden.shape[0]
    total_rows = rows_dev * device_count
    chip_count = device_count // 2
    half = chip_count // 2
    order = ring_order(chip_count)
    place_of = {chip: p for p, chip in enumerate(order)}
    live_chip = [
        any((d * rows_dev) % SPAN + rows_dev > BLK for d in (2 * chip, 2 * chip + 1))
        for chip in range(chip_count)
    ]
    up_reach, down_reach = gather_plan(chip_count, order, live_chip)
    held_rows = other_core(out_weight, device_count)
    up_block = hidden
    down_block = hidden
    stages = [[hidden, other_core(hidden, device_count)]]
    kept = [[(0, 0), (0, 1)]]
    for step in range(1, half + 1):
        up_from = [p for p in range(chip_count) if up_reach[(p - step + 1) % chip_count] >= step]
        down_from = [
            p for p in range(chip_count) if down_reach[(p + step - 1) % chip_count] >= step
        ]
        up_block = lax.ppermute(up_block, "dp", hop_pairs(order, up_from, 1))
        down_block = lax.ppermute(down_block, "dp", hop_pairs(order, down_from, -1))
        if step < half:
            stages.append(
                [
                    up_block,
                    down_block,
                    other_core(up_block, device_count),
                    other_core(down_block, device_count),
                ]
            )
            kept.append([(-step, 0), (step, 0), (-step, 1), (step, 1)])
        else:
            last_block = up_block + down_block
            stages.append([last_block, other_core(last_block, device_count)])
            kept.append([(step, 0), (step, 1)])
    dt_columns = dt_weight.T
    main_parts = []
    rate_parts = []
    for stage in stages:
        joined = jnp.concatenate(stage, axis=0)
        main_parts.append(jnp.dot(joined, in_weight, preferred_element_type=jnp.float32))
        rate_parts.append(jnp.dot(joined, dt_columns, preferred_element_type=jnp.float32))
    slots = [slot for group in kept for slot in group]
    where_is = np.zeros((device_count, device_count), np.int32)
    for device in range(device_count):
        p = place_of[device // 2]
        for at, (offset, other) in enumerate(slots):
            block = 2 * order[(p + offset) % chip_count] + ((device % 2) ^ other)
            where_is[device, block] = at
    my_slots = lax.dynamic_index_in_dim(jnp.asarray(where_is), my_index, 0, keepdims=False)
    main_blocks = jnp.concatenate(main_parts, axis=0).reshape(device_count, rows_dev, -1)
    rate_blocks = jnp.concatenate(rate_parts, axis=0).reshape(device_count, rows_dev, -1)
    main_part = jnp.take(main_blocks, my_slots, axis=0).reshape(total_rows, -1)
    rate_part = jnp.take(rate_blocks, my_slots, axis=0).reshape(total_rows, -1)
    projected_all = jnp.concatenate([main_part, rate_part], axis=1)
    projected = (
        projected_all[:, : heads_dev * row_width]
        .astype(jnp.bfloat16)
        .reshape(REQS, SPAN, heads_dev, row_width)
    )
    time_step = jax.nn.softplus(projected_all[:, heads_dev * row_width :] + dt_bias).reshape(
        REQS, SPAN, heads_dev
    )
    by_device = hit_page.reshape(REQS, device_count, heads_dev * piece_count).transpose(1, 0, 2)
    ssm_pages, conv_pages, my_rows = offer_pages(
        by_device.reshape(device_count, REQS * heads_dev * piece_count),
        state_pool,
        conv_pool,
        my_index,
        per_peer,
    )
    state_rows = state_pool.shape[1]
    piece_channels = conv_pool.shape[2]
    conv_wide = jnp.pad(conv_pages, ((0, 0), (0, 0), (0, 0), (0, STATE - piece_channels)))
    offered = jnp.concatenate([ssm_pages, conv_wide], axis=2)
    received = lax.all_to_all(offered, "dp", split_axis=0, concat_axis=0, tiled=True)
    pages = jnp.take(received.reshape((-1,) + received.shape[2:]), my_rows, axis=0)
    initial_pages = pages[:, :state_rows]
    cached_pages = pages[:, state_rows:, :piece_channels]
    initial_bf = initial_pages.reshape(REQS, heads_dev, HEAD_DIM, STATE)
    initial = initial_bf.astype(jnp.float32)
    cached = (
        jnp.transpose(
            cached_pages.reshape(REQS, heads_dev, piece_count, CONV - 1, channels // piece_count),
            (0, 1, 3, 2, 4),
        )
        .reshape(REQS, heads_dev, CONV - 1, channels)
        .astype(jnp.float32)
    )
    live_start = prefix_blocks * BLK
    positions = jnp.arange(SPAN, dtype=jnp.int32)
    live_mask = positions[None, :] >= live_start[:, None]
    live_float = live_mask.astype(jnp.float32)
    conv_input = jnp.where(
        live_mask[:, :, None, None], projected[..., HEAD_DIM:].astype(jnp.float32), jnp.float32(0.0)
    )
    for lag_row in range(CONV - 1):
        position_hit = positions[None, :] == live_start[:, None] - (CONV - 1) + lag_row
        conv_input = jnp.where(
            position_hit[:, :, None, None], cached[:, None, :, lag_row, :], conv_input
        )
    padded = jnp.pad(conv_input, ((0, 0), (CONV - 1, 0), (0, 0), (0, 0)))
    taps = conv_weight.astype(jnp.float32).reshape(CONV, heads_dev, channels)
    conv_sum = jnp.broadcast_to(
        conv_bias.astype(jnp.float32).reshape(heads_dev, channels), conv_input.shape
    )
    for tap_index in range(CONV):
        conv_sum = conv_sum + taps[tap_index] * padded[:, tap_index : tap_index + SPAN]
    conv_out = jax.nn.silu(conv_sum).astype(jnp.bfloat16)
    x_part = conv_out[..., :HEAD_DIM]
    b_part = conv_out[..., HEAD_DIM : HEAD_DIM + STATE]
    c_part = conv_out[..., HEAD_DIM + STATE :]
    x_float = x_part.astype(jnp.float32)
    c_float = c_part.astype(jnp.float32)
    step_size = time_step * live_float[:, :, None]
    cumulative = jnp.cumsum(-decay_rate * step_size, axis=1)
    scores = jnp.einsum("rthn,rshn->rhts", c_part, b_part, preferred_element_type=jnp.float32)
    cum_heads = jnp.moveaxis(cumulative, 2, 1)
    gaps = cum_heads[..., :, None] - cum_heads[..., None, :]
    causal = jnp.arange(SPAN)[:, None] >= jnp.arange(SPAN)[None, :]
    weights = (
        jnp.where(causal, jnp.exp(jnp.where(causal, gaps, 0.0)), 0.0)
        * scores
        * jnp.moveaxis(step_size, 2, 1)[:, :, None, :]
    )
    weight_upper, weight_lower = split_pair(weights)
    inner = jnp.einsum("rhts,rshp->rthp", weight_upper, x_part, preferred_element_type=jnp.float32)
    inner = inner + jnp.einsum(
        "rhts,rshp->rthp", weight_lower, x_part, preferred_element_type=jnp.float32
    )
    reader_upper, reader_lower = split_pair(c_float * jnp.exp(cumulative)[..., None])
    outer = jnp.einsum(
        "rthn,rhpn->rthp", reader_upper, initial_bf, preferred_element_type=jnp.float32
    )
    outer = outer + jnp.einsum(
        "rthn,rhpn->rthp", reader_lower, initial_bf, preferred_element_type=jnp.float32
    )
    span_tail = cumulative[:, -1, :]
    to_end = jnp.exp(span_tail[:, None, :] - cumulative) * step_size
    input_upper, input_lower = split_pair(to_end[..., None] * x_float)
    added_state = jnp.einsum(
        "rshp,rshn->rhpn", input_upper, b_part, preferred_element_type=jnp.float32
    )
    added_state = added_state + jnp.einsum(
        "rshp,rshn->rhpn", input_lower, b_part, preferred_element_type=jnp.float32
    )
    final_state = jnp.exp(span_tail)[:, :, None, None] * initial + added_state
    outputs = inner + outer + skip[:, None] * x_float
    gate_part = projected[..., :HEAD_DIM].astype(jnp.float32)
    gated = outputs * jax.nn.silu(gate_part)
    inverse_rms = lax.rsqrt(jnp.mean(gated * gated, axis=-1, keepdims=True) + EPSILON)
    normed = (
        gated
        * inverse_rms
        * norm_gain.astype(jnp.float32).reshape(heads_dev, HEAD_DIM)
        * live_float[:, :, None, None]
    ).astype(jnp.bfloat16)
    normed_rows = normed.reshape(device_count, rows_dev, heads_dev * HEAD_DIM)
    owner_match = owners[None, :] == jnp.arange(device_count)[:, None]
    source_block = jnp.sum(jnp.where(owner_match, jnp.arange(device_count)[None, :], 0), axis=1)
    targets = np.zeros((device_count, 2, chip_count), np.int32)
    for device in range(device_count):
        p = place_of[device // 2]
        for offset in range(chip_count):
            chip = order[(p + offset) % chip_count]
            targets[device, 0, offset] = 2 * chip + device % 2
            targets[device, 1, offset] = 2 * chip + 1 - device % 2
    my_targets = lax.dynamic_index_in_dim(jnp.asarray(targets), my_index, 0, keepdims=False)
    mine = jnp.take(normed_rows, jnp.take(source_block, my_targets[0]), axis=0)
    theirs = other_core(
        jnp.take(normed_rows, jnp.take(source_block, my_targets[1]), axis=0), device_count
    )
    both = jnp.concatenate([mine, theirs], axis=2).reshape(chip_count * rows_dev, -1)
    chip_weight = jnp.concatenate([out_weight, held_rows], axis=0)
    shares = jnp.dot(both, chip_weight, preferred_element_type=jnp.float32)
    shares = shares.reshape(chip_count, rows_dev, -1)
    cut = shares.shape[2] // 2
    every = list(range(chip_count))
    up_pairs = hop_pairs(order, every, 1)
    down_pairs = hop_pairs(order, every, -1)
    up_sum = lax.ppermute(shares[half, :, :cut].astype(jnp.bfloat16), "dp", up_pairs)
    down_sum = lax.ppermute(shares[half, :, cut:].astype(jnp.bfloat16), "dp", down_pairs)
    for step in range(half - 1, 0, -1):
        up_share = shares[step]
        down_share = shares[chip_count - step]
        if step == half - 1:
            up_next = jnp.concatenate(
                [up_share[:, :cut] + up_sum.astype(jnp.float32), up_share[:, cut:]], axis=1
            )
            down_next = jnp.concatenate(
                [down_share[:, :cut], down_share[:, cut:] + down_sum.astype(jnp.float32)], axis=1
            )
        else:
            up_next = up_share + up_sum.astype(jnp.float32)
            down_next = down_share + down_sum.astype(jnp.float32)
        up_sum = lax.ppermute(up_next.astype(jnp.bfloat16), "dp", up_pairs)
        down_sum = lax.ppermute(down_next.astype(jnp.bfloat16), "dp", down_pairs)
    mixed = (shares[0] + up_sum.astype(jnp.float32) + down_sum.astype(jnp.float32)).astype(
        jnp.bfloat16
    )
    final_conv = projected[:, SPAN - (CONV - 1) :, :, HEAD_DIM:].reshape(
        REQS, CONV - 1, heads_dev * channels
    )
    return (mixed, final_state, final_conv)


def solution(mesh):
    return jax.shard_map(
        body,
        mesh=mesh,
        in_specs=(
            P(("groups", "dp"), None),
            P(None, "dp"),
            P("dp", None),
            P("dp"),
            P("dp"),
            P(None, "dp"),
            P("dp"),
            P("dp"),
            P("dp"),
            P("dp", None),
            P(("groups", "dp"), None, None),
            P(("groups", "dp"), None, None),
            P("groups", None, None),
            P("groups"),
            P("groups"),
        ),
        out_specs=(
            P(("groups", "dp"), None),
            P("groups", "dp", None, None),
            P("groups", None, "dp"),
        ),
        check_vma=False,
    )
```

```python
import functools

import jax
import jax.numpy as jnp
import numpy as np
from jax import lax
from jax.experimental import pallas as pl
from jax.experimental.pallas import tpu as pltpu
from jax.sharding import PartitionSpec as P

HEAD_DIM = 128
STATE = 128
CONV = 4
REQS = 2
SPAN = 192
BLK = 64


EPSILON = 1e-05


def ring_order(chip_count):
    if chip_count <= 8:
        return list(range(0, chip_count, 2)) + list(range(chip_count - 1, 0, -2))
    return list(range(chip_count))


def gather_plan(chip_count, order, live_chip):
    half = chip_count // 2
    up_load = [0] * chip_count
    down_load = [0] * chip_count
    up_reach = [0] * chip_count
    down_reach = [0] * chip_count
    live_places = [p for p in range(chip_count) if live_chip[order[p]]]
    for p in live_places:
        for hop in range(half - 1):
            up_load[(p + hop) % chip_count] += 1
            down_load[(p - hop) % chip_count] += 1
        up_reach[p] = half - 1
        down_reach[p] = half - 1
    for p in live_places:
        up_last = (p + half - 1) % chip_count
        down_last = (p - half + 1) % chip_count
        if up_load[up_last] <= down_load[down_last]:
            up_load[up_last] += 1
            up_reach[p] = half
        else:
            down_load[down_last] += 1
            down_reach[p] = half
    return up_reach, down_reach


def hop_pairs(order, places, shift):
    count = len(order)
    return [
        (2 * order[p] + core, 2 * order[(p + shift) % count] + core)
        for p in places
        for core in range(2)
    ]


def other_core(array, device_count):
    return lax.ppermute(array, "dp", [(d, d ^ 1) for d in range(device_count)])


def offer_kernel(
    per_peer, entries, my_ref, ids_ref, state_ref, conv_ref, out_ref
):
    pool_slots, state_rows, _ = state_ref.shape
    lag_rows, piece_channels = conv_ref.shape[1:]
    receivers = out_ref.shape[0]
    my_index = my_ref[0]
    out_ref[...] = jnp.zeros_like(out_ref)

    def one_receiver(receiver, _):
        def one_entry(entry, used):
            page = ids_ref[receiver * entries + entry]
            slot = page - my_index * pool_slots
            held = jnp.logical_and(slot >= 0, slot < pool_slots)

            @pl.when(jnp.logical_and(held, used < per_peer))
            def _():
                out_ref[receiver, used, :state_rows, :] = state_ref[slot]
                out_ref[receiver, used, state_rows:, :piece_channels] = conv_ref[slot]

            return used + held.astype(jnp.int32)

        lax.fori_loop(0, entries, one_entry, jnp.int32(0))
        return 0

    lax.fori_loop(0, receivers, one_receiver, 0)


def mix_kernel(
    sizes,
    ids_ref,
    slot_ref,
    target_ref,
    owner_ref,
    prefix_ref,
    skip_ref,
    main_ref,
    rate_ref,
    page_ref,
    bias_ref,
    decay_ref,
    taps_ref,
    conv_bias_ref,
    gain_ref,
    state_ref,
    conv_ref,
    mine_ref,
    theirs_ref,
    rows_s,
    rate_s,
    input_s,
    normed_s,
    initial_s,
    inverse_s,
    used_s,
):
    heads_dev, piece_count, pool_slots, per_peer = sizes
    blocks, rows_dev, _ = main_ref.shape
    live_rows = SPAN - BLK
    lead = 8
    state_rows = HEAD_DIM // piece_count
    channels = HEAD_DIM + 2 * STATE
    row_width = HEAD_DIM + channels
    piece_channels = channels // piece_count
    blocks_req = blocks // REQS

    def clear(holder, _):
        used_s[holder] = 0
        return 0

    lax.fori_loop(0, blocks, clear, 0)

    def invert(block, _):
        inverse_s[owner_ref[block]] = block
        return 0

    lax.fori_loop(0, blocks, invert, 0)

    pieces_of = []
    for r in range(REQS):
        for j in range(blocks_req):
            start = j * rows_dev
            low, high = max(start, BLK), start + rows_dev
            if high > BLK:
                pieces_of.append((r, r * blocks_req + j, low - start, low - BLK, high - BLK))
    for r, block, skipped, low, high in pieces_of:
        at = slot_ref[block]
        rows_s[r, lead + low : lead + high, :] = main_ref[at, skipped:, :]
        rate_s[r, low:high, :] = rate_ref[at, skipped:, :]
    normed_s[...] = jnp.zeros_like(normed_s)

    wide = (live_rows, 128)
    later = lax.broadcasted_iota(jnp.int32, (live_rows, live_rows), 0)
    sooner = lax.broadcasted_iota(jnp.int32, (live_rows, live_rows), 1)
    causal = later >= sooner
    ones = causal.astype(jnp.float32)
    position = lax.broadcasted_iota(jnp.int32, wide, 0) + BLK
    lead_position = lax.broadcasted_iota(jnp.int32, (live_rows + lead, channels), 0) + BLK - lead
    spread_row = lax.broadcasted_iota(jnp.int32, (piece_count * 128, channels), 0)
    spread_col = lax.broadcasted_iota(jnp.int32, (piece_count * 128, channels), 1)
    spread = (
        ((spread_row // 128) * piece_channels + spread_row % 128 == spread_col)
        & (spread_row % 128 < piece_channels)
    ).astype(jnp.bfloat16)

    for r in range(REQS):
        live_start = prefix_ref[r] * BLK
        live = position >= live_start
        rate = rate_s[r] + bias_ref[...]
        step = jnp.where(live, jax.nn.softplus(rate), 0.0)
        drop = -decay_ref[...] * step
        total = jnp.dot(
            ones, drop, preferred_element_type=jnp.float32, precision=lax.Precision.HIGHEST
        )
        total_t = total.T
        step_t = step.T
        from_start = jnp.exp(total)
        span_tail = total[live_rows - 1 : live_rows, :]
        to_end = jnp.exp(span_tail - total) * step
        kept = jnp.exp(span_tail)
        for h in range(heads_dev):
            lags = []
            for p in range(piece_count):
                entry = (r * heads_dev + h) * piece_count + p
                holder = lax.div(ids_ref[entry], pool_slots)
                rank = used_s[holder]
                used_s[holder] = rank + 1
                at = holder * per_peer + rank
                initial_s[p * state_rows : (p + 1) * state_rows, :] = page_ref[
                    at, :state_rows, :
                ].astype(jnp.float32)
                lags.append(page_ref[at, state_rows:, :])
            initial = initial_s[...]
            lag_lanes = jnp.concatenate(lags, axis=1)
            cached = jnp.dot(lag_lanes, spread, preferred_element_type=jnp.float32)
            first = h * row_width
            c0 = h * channels
            raw = rows_s[r, :, first + HEAD_DIM : first + row_width]
            raw = raw.astype(jnp.bfloat16).astype(jnp.float32)
            inputs = jnp.where(lead_position >= live_start, raw, 0.0)
            for lag in range(CONV - 1):
                inputs = jnp.where(
                    lead_position == live_start - (CONV - 1) + lag,
                    cached[lag : lag + 1, :],
                    inputs,
                )
            input_s[...] = inputs
            conv_ref[r, :, c0 : c0 + channels] = rows_s[
                r,
                live_rows + lead - (CONV - 1) : live_rows + lead,
                first + HEAD_DIM : first + row_width,
            ].astype(jnp.bfloat16)
            summed = jnp.broadcast_to(
                conv_bias_ref[:, c0 : c0 + channels].astype(jnp.float32), (live_rows, channels)
            )
            for tap in range(CONV):
                begin = lead - (CONV - 1) + tap
                summed = summed + taps_ref[tap : tap + 1, c0 : c0 + channels].astype(
                    jnp.float32
                ) * input_s[begin : begin + live_rows, :]
            mixed_in = (summed * jax.nn.sigmoid(summed)).astype(jnp.bfloat16)
            x_part = mixed_in[:, :HEAD_DIM]
            b_part = mixed_in[:, HEAD_DIM : HEAD_DIM + STATE]
            c_part = mixed_in[:, HEAD_DIM + STATE :]
            x_float = x_part.astype(jnp.float32)
            last = (((1,), (1,)), ((), ()))
            scores = lax.dot_general(c_part, b_part, last, preferred_element_type=jnp.float32)
            gaps = jnp.where(causal, total[:, h : h + 1] - total_t[h : h + 1, :], 0.0)
            weights = jnp.where(causal, jnp.exp(gaps) * scores * step_t[h : h + 1, :], 0.0)
            outputs = jnp.dot(
                weights.astype(jnp.bfloat16), x_part, preferred_element_type=jnp.float32
            )
            reader = (c_part.astype(jnp.float32) * from_start[:, h : h + 1]).astype(jnp.bfloat16)
            outputs = outputs + lax.dot_general(
                reader, initial.astype(jnp.bfloat16), last, preferred_element_type=jnp.float32
            )
            outputs = outputs + skip_ref[h] * x_float
            entering = (x_float * to_end[:, h : h + 1]).astype(jnp.bfloat16)
            added = lax.dot_general(
                entering,
                b_part,
                (((0,), (0,)), ((), ())),
                preferred_element_type=jnp.float32,
            )
            state_ref[r, h] = kept[:, h : h + 1] * initial + added
            gate = rows_s[r, lead:, first : first + HEAD_DIM]
            gate = gate.astype(jnp.bfloat16).astype(jnp.float32)
            gated = outputs * (gate * jax.nn.sigmoid(gate))
            scale = lax.rsqrt(jnp.mean(gated * gated, axis=1, keepdims=True) + EPSILON)
            gain = gain_ref[:, h * HEAD_DIM : (h + 1) * HEAD_DIM].astype(jnp.float32)
            normed = jnp.where(live, gated * scale * gain, 0.0)
            for rr, block, skipped, low, high in pieces_of:
                if rr == r:
                    normed_s[block, skipped:, h * HEAD_DIM : (h + 1) * HEAD_DIM] = normed[low:high]

    for at in range(mine_ref.shape[0]):
        mine_ref[at] = normed_s[inverse_s[target_ref[0, at]]].astype(jnp.bfloat16)
        theirs_ref[at] = normed_s[inverse_s[target_ref[1, at]]].astype(jnp.bfloat16)


def body(
    hidden,
    in_weight,
    dt_weight,
    dt_bias,
    decay_rate,
    conv_weight,
    conv_bias,
    skip,
    norm_gain,
    out_weight,
    state_pool,
    conv_pool,
    hit_page,
    prefix_blocks,
    owners,
):
    device_count = lax.axis_size("dp")
    my_index = lax.axis_index("dp")
    heads_dev = dt_weight.shape[0]
    piece_count = hit_page.shape[2]
    per_peer = 2
    row_width = 2 * HEAD_DIM + 2 * STATE
    channels = HEAD_DIM + 2 * STATE
    rows_dev = hidden.shape[0]
    by_device = hit_page.reshape(REQS, device_count, heads_dev * piece_count).transpose(1, 0, 2)
    entries = REQS * heads_dev * piece_count
    page_ids = by_device.reshape(device_count * entries)
    state_rows = state_pool.shape[1]
    smem = pl.BlockSpec(memory_space=pltpu.SMEM)
    vmem = pl.BlockSpec(memory_space=pltpu.VMEM)
    offered = pl.pallas_call(
        functools.partial(offer_kernel, per_peer, entries),
        out_shape=jax.ShapeDtypeStruct(
            (device_count, per_peer, state_rows + CONV - 1, STATE), state_pool.dtype
        ),
        in_specs=[smem, smem, vmem, vmem],
        out_specs=vmem,
        name="offer_pages",
    )(my_index.reshape(1).astype(jnp.int32), page_ids, state_pool, conv_pool)
    received = lax.all_to_all(offered, "dp", split_axis=0, concat_axis=0, tiled=True)
    received = received.reshape((-1,) + received.shape[2:])
    chip_count = device_count // 2
    half = chip_count // 2
    order = ring_order(chip_count)
    place_of = {chip: p for p, chip in enumerate(order)}
    live_chip = [
        any((d * rows_dev) % SPAN + rows_dev > BLK for d in (2 * chip, 2 * chip + 1))
        for chip in range(chip_count)
    ]
    up_reach, down_reach = gather_plan(chip_count, order, live_chip)
    held_rows = other_core(out_weight, device_count)
    up_block = hidden
    down_block = hidden
    stages = [[hidden, other_core(hidden, device_count)]]
    kept = [[(0, 0), (0, 1)]]
    for step in range(1, half + 1):
        up_from = [p for p in range(chip_count) if up_reach[(p - step + 1) % chip_count] >= step]
        down_from = [
            p for p in range(chip_count) if down_reach[(p + step - 1) % chip_count] >= step
        ]
        up_block = lax.ppermute(up_block, "dp", hop_pairs(order, up_from, 1))
        down_block = lax.ppermute(down_block, "dp", hop_pairs(order, down_from, -1))
        if step < half:
            stages.append(
                [
                    up_block,
                    down_block,
                    other_core(up_block, device_count),
                    other_core(down_block, device_count),
                ]
            )
            kept.append([(-step, 0), (step, 0), (-step, 1), (step, 1)])
        else:
            last_block = up_block + down_block
            stages.append([last_block, other_core(last_block, device_count)])
            kept.append([(step, 0), (step, 1)])
    dt_columns = jnp.pad(dt_weight, ((0, 128 - heads_dev), (0, 0))).T
    main_parts = []
    rate_parts = []
    for stage in stages:
        joined = jnp.concatenate(stage, axis=0)
        main_parts.append(jnp.dot(joined, in_weight, preferred_element_type=jnp.float32))
        rate_parts.append(jnp.dot(joined, dt_columns, preferred_element_type=jnp.float32))
    slots = [slot for group in kept for slot in group]
    where_is = np.zeros((device_count, device_count), np.int32)
    for device in range(device_count):
        p = place_of[device // 2]
        for at, (offset, other) in enumerate(slots):
            block = 2 * order[(p + offset) % chip_count] + ((device % 2) ^ other)
            where_is[device, block] = at
    my_slots = lax.dynamic_index_in_dim(jnp.asarray(where_is), my_index, 0, keepdims=False)
    main_blocks = jnp.concatenate(main_parts, axis=0).reshape(device_count, rows_dev, -1)
    rate_blocks = jnp.concatenate(rate_parts, axis=0).reshape(device_count, rows_dev, -1)
    targets = np.zeros((device_count, 2, chip_count), np.int32)
    for device in range(device_count):
        p = place_of[device // 2]
        for offset in range(chip_count):
            chip = order[(p + offset) % chip_count]
            targets[device, 0, offset] = 2 * chip + device % 2
            targets[device, 1, offset] = 2 * chip + 1 - device % 2
    my_targets = lax.dynamic_index_in_dim(jnp.asarray(targets), my_index, 0, keepdims=False)
    my_ids = lax.dynamic_slice(page_ids, (my_index * entries,), (entries,))
    lanes = (0, 128 - heads_dev)
    live_rows = SPAN - BLK
    normed_block = jax.ShapeDtypeStruct(
        (chip_count, rows_dev, heads_dev * HEAD_DIM), jnp.bfloat16
    )
    final_state, final_conv, mine, theirs = pl.pallas_call(
        functools.partial(
            mix_kernel, (heads_dev, piece_count, state_pool.shape[0], per_peer)
        ),
        out_shape=[
            jax.ShapeDtypeStruct((REQS, heads_dev, HEAD_DIM, STATE), jnp.float32),
            jax.ShapeDtypeStruct((REQS, CONV - 1, heads_dev * channels), jnp.bfloat16),
            normed_block,
            normed_block,
        ],
        in_specs=[smem] * 6 + [vmem] * 8,
        out_specs=[vmem] * 4,
        scratch_shapes=[
            pltpu.VMEM((REQS, live_rows + 8, heads_dev * row_width), jnp.float32),
            pltpu.VMEM((REQS, live_rows, 128), jnp.float32),
            pltpu.VMEM((live_rows + 8, channels), jnp.float32),
            pltpu.VMEM((device_count, rows_dev, heads_dev * HEAD_DIM), jnp.float32),
            pltpu.VMEM((HEAD_DIM, STATE), jnp.float32),
            pltpu.SMEM((device_count,), jnp.int32),
            pltpu.SMEM((device_count,), jnp.int32),
        ],
        compiler_params=pltpu.CompilerParams(vmem_limit_bytes=32 * 1024 * 1024),
        name="mixer",
    )(
        my_ids,
        my_slots,
        my_targets,
        owners,
        prefix_blocks,
        skip,
        main_blocks,
        rate_blocks,
        received,
        jnp.pad(dt_bias, lanes).reshape(1, 128),
        jnp.pad(decay_rate, lanes).reshape(1, 128),
        conv_weight,
        conv_bias.reshape(1, -1),
        norm_gain.reshape(1, -1),
    )
    theirs = other_core(theirs, device_count)
    both = jnp.concatenate([mine, theirs], axis=2).reshape(chip_count * rows_dev, -1)
    chip_weight = jnp.concatenate([out_weight, held_rows], axis=0)
    shares = jnp.dot(both, chip_weight, preferred_element_type=jnp.float32)
    shares = shares.reshape(chip_count, rows_dev, -1)
    cut = shares.shape[2] // 2
    every = list(range(chip_count))
    up_pairs = hop_pairs(order, every, 1)
    down_pairs = hop_pairs(order, every, -1)
    up_sum = lax.ppermute(shares[half, :, :cut].astype(jnp.bfloat16), "dp", up_pairs)
    down_sum = lax.ppermute(shares[half, :, cut:].astype(jnp.bfloat16), "dp", down_pairs)
    for step in range(half - 1, 0, -1):
        up_share = shares[step]
        down_share = shares[chip_count - step]
        if step == half - 1:
            up_next = jnp.concatenate(
                [up_share[:, :cut] + up_sum.astype(jnp.float32), up_share[:, cut:]], axis=1
            )
            down_next = jnp.concatenate(
                [down_share[:, :cut], down_share[:, cut:] + down_sum.astype(jnp.float32)], axis=1
            )
        else:
            up_next = up_share + up_sum.astype(jnp.float32)
            down_next = down_share + down_sum.astype(jnp.float32)
        up_sum = lax.ppermute(up_next.astype(jnp.bfloat16), "dp", up_pairs)
        down_sum = lax.ppermute(down_next.astype(jnp.bfloat16), "dp", down_pairs)
    mixed = (shares[0] + up_sum.astype(jnp.float32) + down_sum.astype(jnp.float32)).astype(
        jnp.bfloat16
    )
    return (mixed, final_state, final_conv)


def solution(mesh):
    return jax.shard_map(
        body,
        mesh=mesh,
        in_specs=(
            P(("groups", "dp"), None),
            P(None, "dp"),
            P("dp", None),
            P("dp"),
            P("dp"),
            P(None, "dp"),
            P("dp"),
            P("dp"),
            P("dp"),
            P("dp", None),
            P(("groups", "dp"), None, None),
            P(("groups", "dp"), None, None),
            P("groups", None, None),
            P("groups"),
            P("groups"),
        ),
        out_specs=(
            P(("groups", "dp"), None),
            P("groups", "dp", None, None),
            P("groups", None, "dp"),
        ),
        check_vma=False,
    )
```

```python
import functools

import jax
import jax.numpy as jnp
import numpy as np
from jax import lax
from jax.experimental import pallas as pl
from jax.experimental.pallas import tpu as pltpu
from jax.sharding import PartitionSpec as P

HEAD_DIM = 128
STATE = 128
CONV = 4
REQS = 2
SPAN = 192
BLK = 64


EPSILON = 1e-05
PER_PEER = 2


def ring_order(chip_count):
    if chip_count <= 8:
        return list(range(0, chip_count, 2)) + list(range(chip_count - 1, 0, -2))
    return list(range(chip_count))


def hop_pairs(order, shift):
    count = len(order)
    return [
        (2 * order[p] + core, 2 * order[(p + shift) % count] + core)
        for p in range(count)
        for core in range(2)
    ]


def other_core(array, device_count):
    return lax.ppermute(array, "dp", [(d, d ^ 1) for d in range(device_count)])


def offer_kernel(entries, my_ref, ids_ref, state_ref, conv_ref, out_ref, slot_s, conv_s, lag_s):
    pool_slots, state_rows, _ = state_ref.shape
    lag_rows = conv_ref.shape[0]
    piece_channels = conv_ref.shape[2]
    receivers = out_ref.shape[0]
    heads_dev = ids_ref.shape[2] // receivers
    first = my_ref[0] * pool_slots
    conv_s[...] = jnp.zeros_like(conv_s)
    conv_s[:, :, :piece_channels] = conv_ref[...].astype(jnp.float32)
    lag_s[...] = jnp.zeros_like(lag_s)

    def one_receiver(receiver, _):
        used = jnp.int32(0)
        for r in range(REQS):
            for h in range(heads_dev):
                for p in range(ids_ref.shape[1]):
                    slot = ids_ref[r, p, receiver * heads_dev + h] - first
                    slot_s[used] = slot
                    held = jnp.logical_and(slot >= 0, slot < pool_slots)
                    used = used + held.astype(jnp.int32)
        for place in range(PER_PEER):
            slot = jnp.clip(slot_s[place], 0, pool_slots - 1)
            out_ref[receiver, place * state_rows : (place + 1) * state_rows, :] = state_ref[slot]
            for lag in range(lag_rows):
                row = 8 * place + lag
                lag_s[receiver, row : row + 1, :] = conv_s[lag, pl.ds(slot, 1), :]
        return 0

    lax.fori_loop(0, receivers, one_receiver, 0)
    out_ref[:, PER_PEER * state_rows :, :] = lag_s[...].astype(out_ref.dtype)


def stage_kernel(layout, *refs):
    parts = sum(layout)
    block_refs = refs[:parts]
    weight_ref, rate_weight_ref, main_ref, rate_ref, joined_s = refs[parts:]
    rows = main_ref.shape[0] // len(layout)
    at = 0
    for block, count in enumerate(layout):
        left = 0
        for _ in range(count):
            part = block_refs[at]
            width = part.shape[1]
            joined_s[block * rows : (block + 1) * rows, left : left + width] = part[...]
            left += width
            at += 1
    joined = joined_s[...]
    rate_ref[...] = lax.dot_general(
        joined,
        rate_weight_ref[...],
        (((1,), (1,)), ((), ())),
        preferred_element_type=jnp.float32,
    )
    tile = 256

    def one_tile(index, _):
        columns = pl.ds(pl.multiple_of(index * tile, tile), tile)
        main_ref[:, columns] = jnp.dot(
            joined_s[...], weight_ref[:, columns], preferred_element_type=jnp.float32
        )
        return 0

    lax.fori_loop(0, main_ref.shape[1] // tile, one_tile, 0)


def stage(blocks, rows, in_weight, rate_weight):
    layout = tuple(len(block) for block in blocks)
    total = len(blocks) * rows
    depth, width = in_weight.shape
    vmem = pl.BlockSpec(memory_space=pltpu.VMEM)
    return pl.pallas_call(
        functools.partial(stage_kernel, layout),
        out_shape=[
            jax.ShapeDtypeStruct((total, width), jnp.float32),
            jax.ShapeDtypeStruct((total, rate_weight.shape[0]), jnp.float32),
        ],
        in_specs=[vmem] * (sum(layout) + 2),
        out_specs=[vmem] * 2,
        scratch_shapes=[pltpu.VMEM((total, depth), jnp.bfloat16)],
        compiler_params=pltpu.CompilerParams(vmem_limit_bytes=16 * 1024 * 1024),
        cost_estimate=pl.CostEstimate(
            flops=2 * 256 * depth * width, bytes_accessed=2 * depth * width, transcendentals=0
        ),
        name="stage",
    )(*[part for block in blocks for part in block], in_weight, rate_weight)


def first_kernel(half, mine_ref, theirs_ref, weight_ref, held_ref, up_a, up_b, down_a, down_b):
    cut = up_a.shape[1]
    for at, left, out in (
        (half, 0, up_a),
        (half, cut, down_b),
        (half - 1, cut, up_b),
        (half + 1, 0, down_a),
    ):
        total = jnp.dot(
            mine_ref[at], weight_ref[:, left : left + cut], preferred_element_type=jnp.float32
        )
        total = total + jnp.dot(
            theirs_ref[at], held_ref[:, left : left + cut], preferred_element_type=jnp.float32
        )
        out[...] = total.astype(out.dtype)


def onward_kernel(offset, left, share_ref, arrived_ref, out_ref):
    width = out_ref.shape[1]
    share = share_ref[offset, :, left : left + width]
    out_ref[...] = (share + arrived_ref[...].astype(jnp.float32)).astype(out_ref.dtype)


def last_kernel(share_ref, up_a, up_b, down_a, down_b, out_ref):
    cut = up_a.shape[1]
    for left, up, down in ((0, up_a, down_a), (cut, up_b, down_b)):
        total = share_ref[0, :, left : left + cut] + up[...].astype(jnp.float32)
        total = total + down[...].astype(jnp.float32)
        out_ref[:, left : left + cut] = total.astype(out_ref.dtype)


def mix_kernel(
    sizes,
    ids_ref,
    slot_ref,
    target_ref,
    owner_ref,
    prefix_ref,
    skip_ref,
    page_ref,
    bias_ref,
    decay_ref,
    taps_ref,
    conv_bias_ref,
    gain_ref,
    *rest,
):
    heads_dev, piece_count, pool_slots, stages = sizes
    main_refs, rate_refs, rest = rest[:stages], rest[stages : 2 * stages], rest[2 * stages :]
    state_ref, conv_ref, mine_ref, theirs_ref = rest[:4]
    placed_s, placed_rate_s, rows_s, rate_s, input_s, normed_s, initial_s, page_s = rest[4:12]
    inverse_s, used_s = rest[12:]
    blocks, rows_dev, _ = placed_s.shape
    live_rows = SPAN - BLK
    lead = 8
    state_rows = HEAD_DIM // piece_count
    channels = HEAD_DIM + 2 * STATE
    row_width = HEAD_DIM + channels
    piece_channels = channels // piece_count
    blocks_req = blocks // REQS

    def clear(holder, _):
        used_s[holder] = 0
        return 0

    lax.fori_loop(0, blocks, clear, 0)

    def invert(block, _):
        inverse_s[owner_ref[block]] = block
        return 0

    lax.fori_loop(0, blocks, invert, 0)

    page_s[...] = page_ref[...].astype(jnp.float32)

    pieces_of = []
    for r in range(REQS):
        for j in range(blocks_req):
            start = j * rows_dev
            low, high = max(start, BLK), start + rows_dev
            if high > BLK:
                pieces_of.append((r, r * blocks_req + j, low - start, low - BLK, high - BLK))
    slot = 0
    for main_ref, rate_ref in zip(main_refs, rate_refs, strict=True):
        for top in range(0, main_ref.shape[0], rows_dev):
            block = slot_ref[slot]
            placed_s[block] = main_ref[top : top + rows_dev, :]
            placed_rate_s[block] = rate_ref[top : top + rows_dev, :]
            slot += 1
    for r, block, skipped, low, high in pieces_of:
        rows_s[r, lead + low : lead + high, :] = placed_s[block, skipped:, :]
        rate_s[r, low:high, :] = placed_rate_s[block, skipped:, :]
    normed_s[...] = jnp.zeros_like(normed_s)

    wide = (live_rows, 128)
    later = lax.broadcasted_iota(jnp.int32, (live_rows, live_rows), 0)
    sooner = lax.broadcasted_iota(jnp.int32, (live_rows, live_rows), 1)
    causal = later >= sooner
    ones = causal.astype(jnp.float32)
    position = lax.broadcasted_iota(jnp.int32, wide, 0) + BLK
    lead_position = lax.broadcasted_iota(jnp.int32, (live_rows + lead, channels), 0) + BLK - lead
    spread_row = lax.broadcasted_iota(jnp.int32, (piece_count * 128, channels), 0)
    spread_col = lax.broadcasted_iota(jnp.int32, (piece_count * 128, channels), 1)
    spread = (
        ((spread_row // 128) * piece_channels + spread_row % 128 == spread_col)
        & (spread_row % 128 < piece_channels)
    ).astype(jnp.bfloat16)

    for r in range(REQS):
        live_start = prefix_ref[r] * BLK
        live = position >= live_start
        rate = rate_s[r] + bias_ref[...]
        step = jnp.where(live, jax.nn.softplus(rate), 0.0)
        drop = -decay_ref[...] * step
        total = jnp.dot(
            ones, drop, preferred_element_type=jnp.float32, precision=lax.Precision.HIGHEST
        )
        total_t = total.T
        step_t = step.T
        from_start = jnp.exp(total)
        span_tail = total[live_rows - 1 : live_rows, :]
        to_end = jnp.exp(span_tail - total) * step
        kept = jnp.exp(span_tail)
        for h in range(heads_dev):
            lags = []
            for p in range(piece_count):
                entry = (r * heads_dev + h) * piece_count + p
                holder = lax.div(ids_ref[entry], pool_slots)
                rank = used_s[holder]
                used_s[holder] = rank + 1
                state_at = pl.ds(pl.multiple_of(rank * state_rows, state_rows), state_rows)
                lag_at = pl.ds(pl.multiple_of(PER_PEER * state_rows + 8 * rank, 8), 8)
                initial_s[p * state_rows : (p + 1) * state_rows, :] = page_s[holder, state_at, :]
                lags.append(page_s[holder, lag_at, :].astype(jnp.bfloat16))
            initial = initial_s[...]
            lag_lanes = jnp.concatenate(lags, axis=1)
            cached = jnp.dot(lag_lanes, spread, preferred_element_type=jnp.float32)
            first = h * row_width
            c0 = h * channels
            raw = rows_s[r, :, first + HEAD_DIM : first + row_width]
            raw = raw.astype(jnp.bfloat16).astype(jnp.float32)
            inputs = jnp.where(lead_position >= live_start, raw, 0.0)
            for lag in range(CONV - 1):
                inputs = jnp.where(
                    lead_position == live_start - (CONV - 1) + lag,
                    cached[lag : lag + 1, :],
                    inputs,
                )
            input_s[...] = inputs
            conv_ref[r, :, c0 : c0 + channels] = rows_s[
                r,
                live_rows + lead - (CONV - 1) : live_rows + lead,
                first + HEAD_DIM : first + row_width,
            ].astype(jnp.bfloat16)
            summed = jnp.broadcast_to(
                conv_bias_ref[:, c0 : c0 + channels].astype(jnp.float32), (live_rows, channels)
            )
            for tap in range(CONV):
                begin = lead - (CONV - 1) + tap
                summed = summed + taps_ref[tap : tap + 1, c0 : c0 + channels].astype(
                    jnp.float32
                ) * input_s[begin : begin + live_rows, :]
            mixed_in = (summed * jax.nn.sigmoid(summed)).astype(jnp.bfloat16)
            x_part = mixed_in[:, :HEAD_DIM]
            b_part = mixed_in[:, HEAD_DIM : HEAD_DIM + STATE]
            c_part = mixed_in[:, HEAD_DIM + STATE :]
            x_float = x_part.astype(jnp.float32)
            last = (((1,), (1,)), ((), ()))
            scores = lax.dot_general(c_part, b_part, last, preferred_element_type=jnp.float32)
            gaps = jnp.where(causal, total[:, h : h + 1] - total_t[h : h + 1, :], 0.0)
            weights = jnp.where(causal, jnp.exp(gaps) * scores * step_t[h : h + 1, :], 0.0)
            outputs = jnp.dot(
                weights.astype(jnp.bfloat16), x_part, preferred_element_type=jnp.float32
            )
            reader = (c_part.astype(jnp.float32) * from_start[:, h : h + 1]).astype(jnp.bfloat16)
            outputs = outputs + lax.dot_general(
                reader, initial.astype(jnp.bfloat16), last, preferred_element_type=jnp.float32
            )
            outputs = outputs + skip_ref[h] * x_float
            entering = (x_float * to_end[:, h : h + 1]).astype(jnp.bfloat16)
            added = lax.dot_general(
                entering,
                b_part,
                (((0,), (0,)), ((), ())),
                preferred_element_type=jnp.float32,
            )
            state_ref[r, h] = kept[:, h : h + 1] * initial + added
            gate = rows_s[r, lead:, first : first + HEAD_DIM]
            gate = gate.astype(jnp.bfloat16).astype(jnp.float32)
            gated = outputs * (gate * jax.nn.sigmoid(gate))
            scale = lax.rsqrt(jnp.mean(gated * gated, axis=1, keepdims=True) + EPSILON)
            gain = gain_ref[:, h * HEAD_DIM : (h + 1) * HEAD_DIM].astype(jnp.float32)
            normed = jnp.where(live, gated * scale * gain, 0.0)
            for rr, block, skipped, low, high in pieces_of:
                if rr == r:
                    normed_s[block, skipped:, h * HEAD_DIM : (h + 1) * HEAD_DIM] = normed[low:high]

    for at in range(mine_ref.shape[0]):
        mine_ref[at] = normed_s[inverse_s[target_ref[0, at]]].astype(jnp.bfloat16)
        theirs_ref[at] = normed_s[inverse_s[target_ref[1, at]]].astype(jnp.bfloat16)


def body(
    hidden,
    in_weight,
    dt_weight,
    dt_bias,
    decay_rate,
    conv_weight,
    conv_bias,
    skip,
    norm_gain,
    out_weight,
    state_pool,
    conv_pool,
    hit_page,
    prefix_blocks,
    owners,
):
    device_count = lax.axis_size("dp")
    my_index = lax.axis_index("dp")
    heads_dev = dt_weight.shape[0]
    piece_count = hit_page.shape[2]
    row_width = 2 * HEAD_DIM + 2 * STATE
    channels = HEAD_DIM + 2 * STATE
    rows_dev = hidden.shape[0]
    entries = REQS * heads_dev * piece_count
    pool_slots, state_rows, _ = state_pool.shape
    smem = pl.BlockSpec(memory_space=pltpu.SMEM)
    vmem = pl.BlockSpec(memory_space=pltpu.VMEM)

    chip_count = device_count // 2
    half = chip_count // 2
    order = ring_order(chip_count)
    place_of = {chip: p for p, chip in enumerate(order)}
    up_pairs = hop_pairs(order, 1)
    down_pairs = hop_pairs(order, -1)

    page_rows = PER_PEER * state_rows + 8 * PER_PEER
    offered = pl.pallas_call(
        functools.partial(offer_kernel, entries),
        out_shape=jax.ShapeDtypeStruct((device_count, page_rows, STATE), state_pool.dtype),
        in_specs=[smem, smem, vmem, vmem],
        out_specs=vmem,
        scratch_shapes=[
            pltpu.SMEM((entries + 1,), jnp.int32),
            pltpu.VMEM((CONV - 1, pool_slots, STATE), jnp.float32),
            pltpu.VMEM((device_count, 8 * PER_PEER, STATE), jnp.float32),
        ],
        name="offer_pages",
    )(
        my_index.reshape(1).astype(jnp.int32),
        jnp.swapaxes(hit_page, 1, 2),
        state_pool,
        jnp.swapaxes(conv_pool, 0, 1),
    )
    received = lax.all_to_all(offered, "dp", split_axis=0, concat_axis=0, tiled=True)
    by_device = hit_page.reshape(REQS, device_count, heads_dev * piece_count)
    my_ids = lax.dynamic_slice(
        by_device, (0, my_index, 0), (REQS, 1, heads_dev * piece_count)
    ).reshape(entries)

    held_rows = other_core(out_weight, device_count)
    rate_weight = jnp.pad(dt_weight, ((0, 128 - heads_dev), (0, 0)))
    weight_here = pltpu.with_memory_space_constraint(in_weight, pltpu.VMEM)
    up_block = hidden
    down_block = hidden
    cut = hidden.shape[1] // 2
    stages = [[[hidden], [other_core(hidden, device_count)]]]
    slots = [(0, 0), (0, 1)]
    for step in range(1, half):
        up_block = lax.ppermute(up_block, "dp", up_pairs)
        down_block = lax.ppermute(down_block, "dp", down_pairs)
        up_other = other_core(up_block, device_count)
        down_other = other_core(down_block, device_count)
        stages.append([[up_block], [down_block], [up_other], [down_other]])
        slots += [(-step, 0), (step, 0), (-step, 1), (step, 1)]
    up_part = lax.ppermute(up_block[:, :cut], "dp", up_pairs)
    down_part = lax.ppermute(down_block[:, cut:], "dp", down_pairs)
    stages.append(
        [
            [up_part, down_part],
            [other_core(up_part, device_count), other_core(down_part, device_count)],
        ]
    )
    slots += [(half, 0), (half, 1)]
    staged = [stage(blocks, rows_dev, weight_here, rate_weight) for blocks in stages]
    mains = [main for main, _ in staged]
    rates = [rate for _, rate in staged]

    block_of = np.zeros((device_count, device_count), np.int32)
    targets = np.zeros((device_count, 2, chip_count), np.int32)
    for device in range(device_count):
        p = place_of[device // 2]
        for at, (offset, other) in enumerate(slots):
            block_of[device, at] = 2 * order[(p + offset) % chip_count] + ((device % 2) ^ other)
        for offset in range(chip_count):
            chip = order[(p + offset) % chip_count]
            targets[device, 0, offset] = 2 * chip + device % 2
            targets[device, 1, offset] = 2 * chip + 1 - device % 2
    my_blocks = lax.dynamic_index_in_dim(jnp.asarray(block_of), my_index, 0, keepdims=False)
    my_targets = lax.dynamic_index_in_dim(jnp.asarray(targets), my_index, 0, keepdims=False)
    lanes = (0, 128 - heads_dev)
    live_rows = SPAN - BLK
    normed_block = jax.ShapeDtypeStruct(
        (chip_count, rows_dev, heads_dev * HEAD_DIM), jnp.bfloat16
    )
    final_state, final_conv, mine, theirs = pl.pallas_call(
        functools.partial(
            mix_kernel, (heads_dev, piece_count, pool_slots, len(mains))
        ),
        out_shape=[
            jax.ShapeDtypeStruct((REQS, heads_dev, HEAD_DIM, STATE), jnp.float32),
            jax.ShapeDtypeStruct((REQS, CONV - 1, heads_dev * channels), jnp.bfloat16),
            normed_block,
            normed_block,
        ],
        in_specs=[smem] * 6 + [vmem] * (6 + 2 * len(mains)),
        out_specs=[vmem] * 4,
        scratch_shapes=[
            pltpu.VMEM((device_count, rows_dev, heads_dev * row_width), jnp.float32),
            pltpu.VMEM((device_count, rows_dev, 128), jnp.float32),
            pltpu.VMEM((REQS, live_rows + 8, heads_dev * row_width), jnp.float32),
            pltpu.VMEM((REQS, live_rows, 128), jnp.float32),
            pltpu.VMEM((live_rows + 8, channels), jnp.float32),
            pltpu.VMEM((device_count, rows_dev, heads_dev * HEAD_DIM), jnp.float32),
            pltpu.VMEM((HEAD_DIM, STATE), jnp.float32),
            pltpu.VMEM(received.shape, jnp.float32),
            pltpu.SMEM((device_count,), jnp.int32),
            pltpu.SMEM((device_count,), jnp.int32),
        ],
        compiler_params=pltpu.CompilerParams(vmem_limit_bytes=20 * 1024 * 1024),
        name="mixer",
    )(
        my_ids,
        my_blocks,
        my_targets,
        owners,
        prefix_blocks,
        skip,
        received,
        jnp.pad(dt_bias, lanes).reshape(1, 128),
        jnp.pad(decay_rate, lanes).reshape(1, 128),
        conv_weight,
        conv_bias.reshape(1, -1),
        norm_gain.reshape(1, -1),
        *mains,
        *rates,
    )
    theirs = other_core(theirs, device_count)
    width = out_weight.shape[1]
    chunk = jax.ShapeDtypeStruct((rows_dev, width // 2), jnp.bfloat16)
    up_a, up_b, down_a, down_b = pl.pallas_call(
        functools.partial(first_kernel, half),
        out_shape=[chunk] * 4,
        in_specs=[vmem] * 4,
        out_specs=[vmem] * 4,
        compiler_params=pltpu.CompilerParams(vmem_limit_bytes=16 * 1024 * 1024),
        cost_estimate=pl.CostEstimate(
            flops=2 * 256 * 512 * width, bytes_accessed=1024 * width, transcendentals=0
        ),
        name="first_sums",
    )(mine, theirs, out_weight, held_rows)
    both = jnp.concatenate([mine, theirs], axis=2).reshape(chip_count * rows_dev, -1)
    chip_weight = jnp.concatenate([out_weight, held_rows], axis=0)
    shares = jnp.dot(both, chip_weight, preferred_element_type=jnp.float32)
    shares = shares.reshape(chip_count, rows_dev, width)

    def onward(offset, left, arrived):
        return pl.pallas_call(
            functools.partial(onward_kernel, offset, left),
            out_shape=chunk,
            in_specs=[vmem] * 2,
            out_specs=vmem,
            compiler_params=pltpu.CompilerParams(vmem_limit_bytes=8 * 1024 * 1024),
            cost_estimate=add_cost,
            name="onward",
        )(shares, arrived)

    cut = width // 2
    add_cost = pl.CostEstimate(
        flops=rows_dev * cut, bytes_accessed=8 * rows_dev * cut, transcendentals=0
    )
    up_a = lax.ppermute(up_a, "dp", up_pairs)
    down_b = lax.ppermute(down_b, "dp", down_pairs)
    up_b = lax.ppermute(up_b, "dp", up_pairs)
    down_a = lax.ppermute(down_a, "dp", down_pairs)
    for step in range(half - 1, 0, -1):
        up_a = lax.ppermute(onward(step, 0, up_a), "dp", up_pairs)
        down_b = lax.ppermute(onward(chip_count - step, cut, down_b), "dp", down_pairs)
        if step > 1:
            up_b = lax.ppermute(onward(step - 1, cut, up_b), "dp", up_pairs)
            down_a = lax.ppermute(onward(chip_count - step + 1, 0, down_a), "dp", down_pairs)
    mixed = pl.pallas_call(
        last_kernel,
        out_shape=jax.ShapeDtypeStruct((rows_dev, width), jnp.bfloat16),
        in_specs=[vmem] * 5,
        out_specs=vmem,
        compiler_params=pltpu.CompilerParams(vmem_limit_bytes=8 * 1024 * 1024),
        cost_estimate=add_cost,
        name="last_sums",
    )(shares, up_a, up_b, down_a, down_b)
    return (mixed, final_state, final_conv)


def solution(mesh):
    return jax.shard_map(
        body,
        mesh=mesh,
        in_specs=(
            P(("groups", "dp"), None),
            P(None, "dp"),
            P("dp", None),
            P("dp"),
            P("dp"),
            P(None, "dp"),
            P("dp"),
            P("dp"),
            P("dp"),
            P("dp", None),
            P(("groups", "dp"), None, None),
            P(("groups", "dp"), None, None),
            P("groups", None, None),
            P("groups"),
            P("groups"),
        ),
        out_specs=(
            P(("groups", "dp"), None),
            P("groups", "dp", None, None),
            P("groups", None, "dp"),
        ),
        check_vma=False,
    )
```

```python
import functools

import jax
import jax.numpy as jnp
from jax import lax
from jax.experimental import pallas as pl
from jax.experimental.pallas import tpu as pltpu
from jax.sharding import PartitionSpec as P

HEAD_DIM = 128
STATE = 128
CONV = 4
REQS = 2
SPAN = 192
BLK = 64


EPSILON = 1e-05
PER_PEER = 2
VMEM_LIMIT = 16 * 1024 * 1024


def folded(chip_count):
    return chip_count <= 8


def chip_at(place, chip_count):
    if not folded(chip_count):
        return place
    back = 2 * (chip_count - 1 - place) + 1
    if isinstance(place, int):
        return 2 * place if place < chip_count // 2 else back
    return jnp.where(place < chip_count // 2, 2 * place, back)


def place_of(chip, chip_count):
    if not folded(chip_count):
        return chip
    return jnp.where(chip % 2 == 0, chip // 2, chip_count - 1 - chip // 2)


def stream(array, chip_count):
    pairs = []
    for place in range(chip_count):
        for core in range(2):
            onto = (place + 1 - 2 * core) % chip_count
            pairs.append((2 * chip_at(place, chip_count) + core, 2 * chip_at(onto, chip_count) + core))
    return lax.ppermute(array, "dp", pairs)


def other_core(array, chip_count):
    return lax.ppermute(array, "dp", [(d, d ^ 1) for d in range(2 * chip_count)])


def kernel_call(kernel, outs, operands, scratch, name, flops=0, smem=0):
    several = isinstance(outs, list)
    whole = pl.BlockSpec(memory_space=pltpu.VMEM)
    scalars = pl.BlockSpec(memory_space=pltpu.SMEM)
    return pl.pallas_call(
        kernel,
        out_shape=outs,
        in_specs=[scalars] * smem + [whole] * (len(operands) - smem),
        out_specs=[whole] * len(outs) if several else whole,
        scratch_shapes=scratch,
        compiler_params=pltpu.CompilerParams(vmem_limit_bytes=VMEM_LIMIT),
        cost_estimate=pl.CostEstimate(flops=flops, bytes_accessed=1 << 20, transcendentals=0),
        name=name,
    )(*operands)


def offer_kernel(entries, my_ref, ids_ref, state_ref, conv_ref, out_ref, slot_s, conv_s, lag_s):
    pool_slots, state_rows, _ = state_ref.shape
    lag_rows = conv_ref.shape[0]
    piece_channels = conv_ref.shape[2]
    receivers = out_ref.shape[0]
    heads_dev = ids_ref.shape[2] // receivers
    first = my_ref[0] * pool_slots
    conv_s[...] = jnp.zeros_like(conv_s)
    conv_s[:, :, :piece_channels] = conv_ref[...].astype(jnp.float32)
    lag_s[...] = jnp.zeros_like(lag_s)

    def one_receiver(receiver, _):
        used = jnp.int32(0)
        for r in range(REQS):
            for h in range(heads_dev):
                for p in range(ids_ref.shape[1]):
                    slot = ids_ref[r, p, receiver * heads_dev + h] - first
                    slot_s[used] = slot
                    held = jnp.logical_and(slot >= 0, slot < pool_slots)
                    used = used + held.astype(jnp.int32)
        for place in range(PER_PEER):
            slot = jnp.clip(slot_s[place], 0, pool_slots - 1)
            out_ref[receiver, place * state_rows : (place + 1) * state_rows, :] = state_ref[slot]
            for lag in range(lag_rows):
                row = 8 * place + lag
                lag_s[receiver, row : row + 1, :] = conv_s[lag, pl.ds(slot, 1), :]
        return 0

    lax.fori_loop(0, receivers, one_receiver, 0)
    out_ref[:, PER_PEER * state_rows :, :] = lag_s[...].astype(out_ref.dtype)


def column_tiles(width, body):
    tile = min(512, width)

    def one_tile(index, _):
        body(pl.ds(pl.multiple_of(index * tile, tile), tile))
        return 0

    lax.fori_loop(0, width // tile, one_tile, 0)


def stage_kernel(count, *refs):
    block_refs = refs[:count]
    weight_ref, rate_weight_ref, out_ref, joined_s = refs[count:]
    rows = block_refs[0].shape[0]
    width = weight_ref.shape[1]
    for at, block_ref in enumerate(block_refs):
        joined_s[at * rows : (at + 1) * rows, :] = block_ref[...]
    out_ref[:, width:] = jnp.dot(
        joined_s[...], rate_weight_ref[...], preferred_element_type=jnp.float32
    )

    def body(columns):
        out_ref[:, columns] = jnp.dot(
            joined_s[...], weight_ref[:, columns], preferred_element_type=jnp.float32
        )

    column_tiles(width, body)


def stage(blocks, weight, rate_weight):
    rows, depth = blocks[0].shape
    total = rows * len(blocks)
    width = weight.shape[1] + rate_weight.shape[1]
    return kernel_call(
        functools.partial(stage_kernel, len(blocks)),
        jax.ShapeDtypeStruct((total, width), jnp.float32),
        [*blocks, weight, rate_weight],
        [pltpu.VMEM((total, depth), jnp.bfloat16)],
        "stage",
        flops=2 * 256 * depth * width,
    )


def part_kernel(mine_ref, weight_ref, out_ref):
    def body(columns):
        out_ref[:, columns] = jnp.dot(
            mine_ref[...], weight_ref[:, columns], preferred_element_type=jnp.float32
        )

    column_tiles(out_ref.shape[1], body)


def first_kernel(rows, part_ref, theirs_ref, held_ref, first_ref, second_ref):
    def body(columns):
        total = part_ref[: 2 * rows, columns] + jnp.dot(
            theirs_ref[: 2 * rows, :], held_ref[:, columns], preferred_element_type=jnp.float32
        )
        first_ref[:, columns] = total[:rows].astype(first_ref.dtype)
        second_ref[:, columns] = total[rows:].astype(second_ref.dtype)

    column_tiles(held_ref.shape[1], body)


def rest_kernel(rows, part_ref, theirs_ref, held_ref, out_ref):
    def body(columns):
        out_ref[:, columns] = part_ref[2 * rows :, columns] + jnp.dot(
            theirs_ref[2 * rows :, :], held_ref[:, columns], preferred_element_type=jnp.float32
        )

    column_tiles(held_ref.shape[1], body)


def add_kernel(top, share_ref, *refs):
    out_ref = refs[-1]
    total = share_ref[top : top + out_ref.shape[0], :]
    for arrived_ref in refs[:-1]:
        total = total + arrived_ref[...].astype(jnp.float32)
    out_ref[...] = total.astype(out_ref.dtype)


def gather_slots(half):
    slots = [(0, 0), (0, 1)]
    for step in range(1, half):
        slots += [(-step, 0), (-step, 1), (step, 1), (step, 0)]
    return slots + [(-half, 0), (half, 1)]


def send_slots(half):
    slots = []
    for step in range(half, 0, -1):
        slots.append((step, 0))
        if step > 1:
            slots.append((step - 1, 1))
    return slots + [(0, 0)]


def mix_kernel(sizes, scalar_ref, page_id_ref, number_ref, page_ref, param_ref, *rest):
    heads_dev, piece_count, pool_slots, stages = sizes
    stage_refs, rest = rest[:stages], rest[stages:]
    state_ref, conv_ref, mine_ref, theirs_ref = rest[:4]
    placed_s, rows_s, rate_s, input_s, normed_s, initial_s, page_s, inverse_s, used_s = rest[4:]
    blocks, rows_dev, _ = placed_s.shape
    live_rows = SPAN - BLK
    lead = 8
    state_rows = HEAD_DIM // piece_count
    channels = HEAD_DIM + 2 * STATE
    row_width = HEAD_DIM + channels
    piece_channels = channels // piece_count
    blocks_req = blocks // REQS

    chip_count = blocks // 2
    half = chip_count // 2
    my_index = scalar_ref[0]
    core = my_index % 2
    place = place_of(my_index // 2, chip_count)
    owner_at = 1 + REQS

    def device_at(distance, flip):
        onto = place + jnp.where(core == 0, distance, -distance) + chip_count
        chip = chip_at(lax.rem(onto, chip_count), chip_count)
        return 2 * chip + (core if flip == 0 else 1 - core)

    def clear(holder, _):
        used_s[holder] = 0
        return 0

    lax.fori_loop(0, blocks, clear, 0)

    def invert(block, _):
        inverse_s[scalar_ref[owner_at + block]] = block
        return 0

    lax.fori_loop(0, blocks, invert, 0)

    page_s[...] = page_ref[...].astype(jnp.float32)

    pieces_of = []
    for r in range(REQS):
        for j in range(blocks_req):
            start = j * rows_dev
            low, high = max(start, BLK), start + rows_dev
            if high > BLK:
                pieces_of.append((r, r * blocks_req + j, low - start, low - BLK, high - BLK))
    slots = gather_slots(half)
    at = 0
    for stage_ref in stage_refs:
        for top in range(0, stage_ref.shape[0], rows_dev):
            placed_s[device_at(*slots[at])] = stage_ref[top : top + rows_dev, :]
            at += 1
    for r, block, skipped, low, high in pieces_of:
        rows_s[r, lead + low : lead + high, :] = placed_s[block, skipped:, : rows_s.shape[2]]
        rate_s[r, low:high, :] = placed_s[block, skipped:, rows_s.shape[2] :]
    normed_s[...] = jnp.zeros_like(normed_s)

    wide = (live_rows, 128)
    later = lax.broadcasted_iota(jnp.int32, (live_rows, live_rows), 0)
    sooner = lax.broadcasted_iota(jnp.int32, (live_rows, live_rows), 1)
    causal = later >= sooner
    ones = causal.astype(jnp.float32)
    position = lax.broadcasted_iota(jnp.int32, wide, 0) + BLK
    lead_position = lax.broadcasted_iota(jnp.int32, (live_rows + lead, channels), 0) + BLK - lead
    spread_row = lax.broadcasted_iota(jnp.int32, (piece_count * 128, channels), 0)
    spread_col = lax.broadcasted_iota(jnp.int32, (piece_count * 128, channels), 1)
    spread = (
        ((spread_row // 128) * piece_channels + spread_row % 128 == spread_col)
        & (spread_row % 128 < piece_channels)
    ).astype(jnp.bfloat16)

    lane = lax.broadcasted_iota(jnp.int32, (1, 128), 1)
    bias_lanes = jnp.zeros((1, 128), jnp.float32)
    decay_lanes = jnp.zeros((1, 128), jnp.float32)
    for h in range(heads_dev):
        bias_lanes = jnp.where(lane == h, number_ref[h], bias_lanes)
        decay_lanes = jnp.where(lane == h, number_ref[heads_dev + h], decay_lanes)

    for r in range(REQS):
        live_start = scalar_ref[1 + r] * BLK
        live = position >= live_start
        rate = rate_s[r] + bias_lanes
        step = jnp.where(live, jax.nn.softplus(rate), 0.0)
        drop = -decay_lanes * step
        total = jnp.dot(
            ones, drop, preferred_element_type=jnp.float32, precision=lax.Precision.HIGHEST
        )
        total_t = total.T
        step_t = step.T
        from_start = jnp.exp(total)
        span_tail = total[live_rows - 1 : live_rows, :]
        to_end = jnp.exp(span_tail - total) * step
        kept = jnp.exp(span_tail)
        for h in range(heads_dev):
            lags = []
            for p in range(piece_count):
                page = page_id_ref[r, p, my_index * heads_dev + h]
                holder = lax.div(page, pool_slots)
                rank = used_s[holder]
                used_s[holder] = rank + 1
                state_at = pl.ds(pl.multiple_of(rank * state_rows, state_rows), state_rows)
                lag_at = pl.ds(pl.multiple_of(PER_PEER * state_rows + 8 * rank, 8), 8)
                initial_s[p * state_rows : (p + 1) * state_rows, :] = page_s[holder, state_at, :]
                lags.append(page_s[holder, lag_at, :].astype(jnp.bfloat16))
            initial = initial_s[...]
            lag_lanes = jnp.concatenate(lags, axis=1)
            cached = jnp.dot(lag_lanes, spread, preferred_element_type=jnp.float32)
            first = h * row_width
            c0 = h * channels
            raw = rows_s[r, :, first + HEAD_DIM : first + row_width]
            raw = raw.astype(jnp.bfloat16).astype(jnp.float32)
            inputs = jnp.where(lead_position >= live_start, raw, 0.0)
            for lag in range(CONV - 1):
                inputs = jnp.where(
                    lead_position == live_start - (CONV - 1) + lag,
                    cached[lag : lag + 1, :],
                    inputs,
                )
            input_s[...] = inputs
            conv_ref[r, :, c0 : c0 + channels] = rows_s[
                r,
                live_rows + lead - (CONV - 1) : live_rows + lead,
                first + HEAD_DIM : first + row_width,
            ].astype(jnp.bfloat16)
            summed = jnp.broadcast_to(
                param_ref[CONV : CONV + 1, c0 : c0 + channels].astype(jnp.float32), (live_rows, channels)
            )
            for tap in range(CONV):
                begin = lead - (CONV - 1) + tap
                summed = summed + param_ref[tap : tap + 1, c0 : c0 + channels].astype(
                    jnp.float32
                ) * input_s[begin : begin + live_rows, :]
            mixed_in = (summed * jax.nn.sigmoid(summed)).astype(jnp.bfloat16)
            x_part = mixed_in[:, :HEAD_DIM]
            b_part = mixed_in[:, HEAD_DIM : HEAD_DIM + STATE]
            c_part = mixed_in[:, HEAD_DIM + STATE :]
            x_float = x_part.astype(jnp.float32)
            last = (((1,), (1,)), ((), ()))
            scores = lax.dot_general(c_part, b_part, last, preferred_element_type=jnp.float32)
            gaps = jnp.where(causal, total[:, h : h + 1] - total_t[h : h + 1, :], 0.0)
            weights = jnp.where(causal, jnp.exp(gaps) * scores * step_t[h : h + 1, :], 0.0)
            outputs = jnp.dot(
                weights.astype(jnp.bfloat16), x_part, preferred_element_type=jnp.float32
            )
            reader = (c_part.astype(jnp.float32) * from_start[:, h : h + 1]).astype(jnp.bfloat16)
            outputs = outputs + lax.dot_general(
                reader, initial.astype(jnp.bfloat16), last, preferred_element_type=jnp.float32
            )
            outputs = outputs + number_ref[2 * heads_dev + h] * x_float
            entering = (x_float * to_end[:, h : h + 1]).astype(jnp.bfloat16)
            added = lax.dot_general(
                entering,
                b_part,
                (((0,), (0,)), ((), ())),
                preferred_element_type=jnp.float32,
            )
            state_ref[r, h] = kept[:, h : h + 1] * initial + added
            gate = rows_s[r, lead:, first : first + HEAD_DIM]
            gate = gate.astype(jnp.bfloat16).astype(jnp.float32)
            gated = outputs * (gate * jax.nn.sigmoid(gate))
            scale = lax.rsqrt(jnp.mean(gated * gated, axis=1, keepdims=True) + EPSILON)
            gain = param_ref[CONV + 1 : CONV + 2, h * HEAD_DIM : (h + 1) * HEAD_DIM]
            gain = gain.astype(jnp.float32)
            normed = jnp.where(live, gated * scale * gain, 0.0)
            for rr, block, skipped, low, high in pieces_of:
                if rr == r:
                    normed_s[block, skipped:, h * HEAD_DIM : (h + 1) * HEAD_DIM] = normed[low:high]

    for at, (distance, flip) in enumerate(send_slots(half)):
        rows = slice(at * rows_dev, (at + 1) * rows_dev)
        mine_ref[rows, :] = normed_s[inverse_s[device_at(distance, flip)]].astype(jnp.bfloat16)
        theirs_ref[rows, :] = normed_s[inverse_s[device_at(-distance, 1 - flip)]].astype(
            jnp.bfloat16
        )


def body(
    hidden,
    in_weight,
    dt_weight,
    dt_bias,
    decay_rate,
    conv_weight,
    conv_bias,
    skip,
    norm_gain,
    out_weight,
    state_pool,
    conv_pool,
    hit_page,
    prefix_blocks,
    owners,
):
    device_count = lax.axis_size("dp")
    my_index = lax.axis_index("dp").astype(jnp.int32).reshape(1)
    heads_dev = dt_weight.shape[0]
    piece_count = hit_page.shape[2]
    row_width = 2 * HEAD_DIM + 2 * STATE
    channels = HEAD_DIM + 2 * STATE
    rows_dev = hidden.shape[0]
    pool_slots, state_rows, _ = state_pool.shape
    chip_count = device_count // 2
    half = chip_count // 2
    page_ids = jnp.swapaxes(hit_page, 1, 2)

    held = other_core(out_weight, chip_count)
    own_type = hidden
    other_type = other_core(hidden, chip_count)

    page_rows = PER_PEER * state_rows + 8 * PER_PEER
    entries = REQS * heads_dev * piece_count
    offered = kernel_call(
        functools.partial(offer_kernel, entries),
        jax.ShapeDtypeStruct((device_count, page_rows, STATE), state_pool.dtype),
        [my_index, page_ids, state_pool, jnp.swapaxes(conv_pool, 0, 1)],
        [
            pltpu.SMEM((entries + 1,), jnp.int32),
            pltpu.VMEM((CONV - 1, pool_slots, STATE), jnp.float32),
            pltpu.VMEM((device_count, 8 * PER_PEER, STATE), jnp.float32),
        ],
        "offer_pages",
        smem=2,
    )
    received = lax.all_to_all(offered, "dp", split_axis=0, concat_axis=0, tiled=True)

    rate_weight = jnp.pad(dt_weight.T, ((0, 0), (0, 128 - heads_dev)))
    weight_here = pltpu.with_memory_space_constraint(in_weight, pltpu.VMEM)
    stages = [[own_type, other_type]]
    for step in range(1, half):
        own_type = stream(own_type, chip_count)
        other_type = stream(other_type, chip_count)
        stages.append(
            [
                own_type,
                other_type,
                other_core(own_type, chip_count),
                other_core(other_type, chip_count),
            ]
        )
    own_type = stream(own_type, chip_count)
    stages.append([own_type, other_core(own_type, chip_count)])
    staged = [stage(blocks, weight_here, rate_weight) for blocks in stages]

    live_rows = SPAN - BLK
    scalars = jnp.concatenate([my_index, prefix_blocks, owners])
    numbers = jnp.concatenate([dt_bias, decay_rate, skip])
    wide = conv_weight.shape[1]
    params = jnp.concatenate(
        [
            conv_weight,
            conv_bias.reshape(1, wide),
            jnp.pad(norm_gain, (0, wide - norm_gain.shape[0])).reshape(1, wide),
        ]
    )
    normed_rows = jax.ShapeDtypeStruct((chip_count * rows_dev, heads_dev * HEAD_DIM), jnp.bfloat16)
    final_state, final_conv, mine, theirs = kernel_call(
        functools.partial(mix_kernel, (heads_dev, piece_count, pool_slots, len(staged))),
        [
            jax.ShapeDtypeStruct((REQS, heads_dev, HEAD_DIM, STATE), jnp.float32),
            jax.ShapeDtypeStruct((REQS, CONV - 1, heads_dev * channels), jnp.bfloat16),
            normed_rows,
            normed_rows,
        ],
        [scalars, page_ids, numbers, received, params, *staged],
        [
            pltpu.VMEM((device_count, rows_dev, heads_dev * row_width + 128), jnp.float32),
            pltpu.VMEM((REQS, live_rows + 8, heads_dev * row_width), jnp.float32),
            pltpu.VMEM((REQS, live_rows, 128), jnp.float32),
            pltpu.VMEM((live_rows + 8, channels), jnp.float32),
            pltpu.VMEM((device_count, rows_dev, heads_dev * HEAD_DIM), jnp.float32),
            pltpu.VMEM((HEAD_DIM, STATE), jnp.float32),
            pltpu.VMEM(received.shape, jnp.float32),
            pltpu.SMEM((device_count,), jnp.int32),
            pltpu.SMEM((device_count,), jnp.int32),
        ],
        "mixer",
        flops=1 << 30,
        smem=3,
    )

    theirs = other_core(theirs, chip_count)
    width = out_weight.shape[1]
    total_rows = chip_count * rows_dev
    block = jax.ShapeDtypeStruct((rows_dev, width), jnp.bfloat16)
    part = kernel_call(
        part_kernel,
        jax.ShapeDtypeStruct((total_rows, width), jnp.float32),
        [mine, out_weight],
        [],
        "sums_part",
        flops=1 << 30,
    )
    first, second = kernel_call(
        functools.partial(first_kernel, rows_dev),
        [block, block],
        [part, theirs, held],
        [],
        "sums_first",
        flops=1 << 30,
    )
    own_sum = stream(first, chip_count)
    other_sum = stream(second, chip_count)
    shares = kernel_call(
        functools.partial(rest_kernel, rows_dev),
        jax.ShapeDtypeStruct((total_rows - 2 * rows_dev, width), jnp.float32),
        [part, theirs, held],
        [],
        "sums_rest",
        flops=1 << 30,
    )

    def onward(at, *arrived):
        top = (at - 2) * rows_dev
        return kernel_call(
            functools.partial(add_kernel, top), block, [shares, *arrived], [], "onward"
        )

    slots = send_slots(half)
    for at in range(2, len(slots) - 1):
        if slots[at][1] == 0:
            own_sum = stream(onward(at, own_sum), chip_count)
        else:
            other_sum = stream(onward(at, other_sum), chip_count)
    crossed = other_core(other_sum, chip_count)
    mixed = onward(len(slots) - 1, own_sum, crossed)
    return (mixed, final_state, final_conv)


def solution(mesh):
    return jax.shard_map(
        body,
        mesh=mesh,
        in_specs=(
            P(("groups", "dp"), None),
            P(None, "dp"),
            P("dp", None),
            P("dp"),
            P("dp"),
            P(None, "dp"),
            P("dp"),
            P("dp"),
            P("dp"),
            P("dp", None),
            P(("groups", "dp"), None, None),
            P(("groups", "dp"), None, None),
            P("groups", None, None),
            P("groups"),
            P("groups"),
        ),
        out_specs=(
            P(("groups", "dp"), None),
            P("groups", "dp", None, None),
            P("groups", None, "dp"),
        ),
        check_vma=False,
    )
```

```python
import functools

import jax
import jax.numpy as jnp
from jax import lax
from jax.experimental import pallas as pl
from jax.experimental.pallas import tpu as pltpu
from jax.sharding import PartitionSpec as P

HEAD_DIM = 128
STATE = 128
CONV = 4
REQS = 2
SPAN = 192
BLK = 64


EPSILON = 1e-05
PER_PEER = 2
VMEM_LIMIT = 16 * 1024 * 1024
VMEM_ALL = 60 * 1024 * 1024


def folded(chip_count):
    return chip_count <= 8


def chip_at(place, chip_count):
    if not folded(chip_count):
        return place
    back = 2 * (chip_count - 1 - place) + 1
    if isinstance(place, int):
        return 2 * place if place < chip_count // 2 else back
    return jnp.where(place < chip_count // 2, 2 * place, back)


def place_of(chip, chip_count):
    if not folded(chip_count):
        return chip
    return jnp.where(chip % 2 == 0, chip // 2, chip_count - 1 - chip // 2)


def stream(array, chip_count):
    pairs = []
    for place in range(chip_count):
        for core in range(2):
            onto = (place + 1 - 2 * core) % chip_count
            pairs.append((2 * chip_at(place, chip_count) + core, 2 * chip_at(onto, chip_count) + core))
    return lax.ppermute(array, "dp", pairs)


def other_core(array, chip_count):
    return lax.ppermute(array, "dp", [(d, d ^ 1) for d in range(2 * chip_count)])


def kernel_call(kernel, outs, operands, scratch, name, flops=0, smem=0, limit=VMEM_LIMIT):
    several = isinstance(outs, list)
    whole = pl.BlockSpec(memory_space=pltpu.VMEM)
    scalars = pl.BlockSpec(memory_space=pltpu.SMEM)
    return pl.pallas_call(
        kernel,
        out_shape=outs,
        in_specs=[scalars] * smem + [whole] * (len(operands) - smem),
        out_specs=[whole] * len(outs) if several else whole,
        scratch_shapes=scratch,
        compiler_params=pltpu.CompilerParams(vmem_limit_bytes=limit),
        cost_estimate=pl.CostEstimate(flops=flops, bytes_accessed=1 << 20, transcendentals=0),
        name=name,
    )(*operands)


def offer_kernel(entries, my_ref, ids_ref, state_ref, conv_ref, out_ref, slot_s, conv_s, lag_s):
    pool_slots, state_rows, _ = state_ref.shape
    lag_rows = conv_ref.shape[0]
    piece_channels = conv_ref.shape[2]
    receivers = out_ref.shape[0]
    heads_dev = ids_ref.shape[2] // receivers
    first = my_ref[0] * pool_slots
    conv_s[...] = jnp.zeros_like(conv_s)
    conv_s[:, :, :piece_channels] = conv_ref[...].astype(jnp.float32)
    lag_s[...] = jnp.zeros_like(lag_s)

    def one_receiver(receiver, _):
        used = jnp.int32(0)
        for r in range(REQS):
            for h in range(heads_dev):
                for p in range(ids_ref.shape[1]):
                    slot = ids_ref[r, p, receiver * heads_dev + h] - first
                    slot_s[used] = slot
                    held = jnp.logical_and(slot >= 0, slot < pool_slots)
                    used = used + held.astype(jnp.int32)
        for place in range(PER_PEER):
            slot = jnp.clip(slot_s[place], 0, pool_slots - 1)
            out_ref[receiver, place * state_rows : (place + 1) * state_rows, :] = state_ref[slot]
            for lag in range(lag_rows):
                row = 8 * place + lag
                lag_s[receiver, row : row + 1, :] = conv_s[lag, pl.ds(slot, 1), :]
        return 0

    lax.fori_loop(0, receivers, one_receiver, 0)
    out_ref[:, PER_PEER * state_rows :, :] = lag_s[...].astype(out_ref.dtype)


def column_tiles(width, body):
    tile = min(512, width)

    def one_tile(index, _):
        body(pl.ds(pl.multiple_of(index * tile, tile), tile))
        return 0

    lax.fori_loop(0, width // tile, one_tile, 0)


def load_kernel(*refs):
    count = (len(refs) - 1) // 2
    sems = refs[-1]
    copies = [
        pltpu.make_async_copy(refs[at], refs[count + at], sems.at[at]) for at in range(count)
    ]
    for copy in copies:
        copy.start()
    for copy in copies:
        copy.wait()


def load(*arrays):
    return pl.pallas_call(
        load_kernel,
        out_shape=[jax.ShapeDtypeStruct(a.shape, a.dtype) for a in arrays],
        in_specs=[pl.BlockSpec(memory_space=pltpu.HBM)] * len(arrays),
        out_specs=[pl.BlockSpec(memory_space=pltpu.VMEM)] * len(arrays),
        scratch_shapes=[pltpu.SemaphoreType.DMA((len(arrays),))],
        compiler_params=pltpu.CompilerParams(vmem_limit_bytes=VMEM_LIMIT),
        cost_estimate=pl.CostEstimate(flops=0, bytes_accessed=8 << 20, transcendentals=0),
        name="load",
    )(*[pltpu.with_memory_space_constraint(a, pltpu.HBM) for a in arrays])


def stage_kernel(count, *refs):
    block_refs = refs[:count]
    weight_ref, rate_weight_ref, out_ref, joined_s = refs[count:]
    rows = block_refs[0].shape[0]
    width = weight_ref.shape[1]
    for at, block_ref in enumerate(block_refs):
        joined_s[at * rows : (at + 1) * rows, :] = block_ref[...]
    rates = rate_weight_ref.shape[0]
    out_ref[:, width:] = jnp.zeros((out_ref.shape[0], out_ref.shape[1] - width), jnp.float32)
    out_ref[:, width : width + rates] = lax.dot_general(
        joined_s[...],
        rate_weight_ref[...],
        (((1,), (1,)), ((), ())),
        preferred_element_type=jnp.float32,
    )

    def body(columns):
        out_ref[:, columns] = jnp.dot(
            joined_s[...], weight_ref[:, columns], preferred_element_type=jnp.float32
        )

    column_tiles(width, body)


def stage(blocks, weight, rate_weight):
    rows, depth = blocks[0].shape
    total = rows * len(blocks)
    width = weight.shape[1] + 128
    return kernel_call(
        functools.partial(stage_kernel, len(blocks)),
        jax.ShapeDtypeStruct((total, width), jnp.float32),
        [*blocks, weight, rate_weight],
        [pltpu.VMEM((total, depth), jnp.bfloat16)],
        "stage",
        flops=2 * 256 * depth * width,
    )


def part_kernel(mine_ref, weight_ref, out_ref):
    def body(columns):
        out_ref[:, columns] = jnp.dot(
            mine_ref[...], weight_ref[:, columns], preferred_element_type=jnp.float32
        )

    column_tiles(out_ref.shape[1], body)


def first_kernel(rows, part_ref, theirs_ref, held_ref, first_ref, second_ref):
    def body(columns):
        total = part_ref[: 2 * rows, columns] + jnp.dot(
            theirs_ref[: 2 * rows, :], held_ref[:, columns], preferred_element_type=jnp.float32
        )
        first_ref[:, columns] = total[:rows].astype(first_ref.dtype)
        second_ref[:, columns] = total[rows:].astype(second_ref.dtype)

    column_tiles(held_ref.shape[1], body)


def rest_kernel(rows, part_ref, theirs_ref, held_ref, out_ref):
    def body(columns):
        out_ref[:, columns] = part_ref[2 * rows :, columns] + jnp.dot(
            theirs_ref[2 * rows :, :], held_ref[:, columns], preferred_element_type=jnp.float32
        )

    column_tiles(held_ref.shape[1], body)


def add_kernel(top, share_ref, *refs):
    out_ref = refs[-1]
    total = share_ref[top : top + out_ref.shape[0], :]
    for arrived_ref in refs[:-1]:
        total = total + arrived_ref[...].astype(jnp.float32)
    out_ref[...] = total.astype(out_ref.dtype)


def gather_slots(half):
    slots = [(0, 0), (0, 1)]
    for step in range(1, half):
        slots += [(-step, 0), (-step, 1), (step, 1), (step, 0)]
    return slots + [(-half, 0), (half, 1)]


def send_slots(half):
    slots = []
    for step in range(half, 0, -1):
        slots.append((step, 0))
        if step > 1:
            slots.append((step - 1, 1))
    return slots + [(0, 0)]


def mix_kernel(sizes, scalar_ref, page_id_ref, number_ref, page_ref, *rest):
    heads_dev, piece_count, pool_slots, stages = sizes
    taps_ref, conv_bias_ref, gain_ref = rest[:3]
    stage_refs, rest = rest[3 : 3 + stages], rest[3 + stages :]
    conv_bias = conv_bias_ref[...].astype(jnp.float32).reshape(1, -1)
    gains = gain_ref[...].astype(jnp.float32).reshape(1, -1)
    state_ref, conv_ref, mine_ref, theirs_ref = rest[:4]
    placed_s, rows_s, rate_s, input_s, normed_s, initial_s, page_s, inverse_s, used_s = rest[4:]
    blocks, rows_dev, _ = placed_s.shape
    live_rows = SPAN - BLK
    lead = 8
    state_rows = HEAD_DIM // piece_count
    channels = HEAD_DIM + 2 * STATE
    row_width = HEAD_DIM + channels
    piece_channels = channels // piece_count
    blocks_req = blocks // REQS

    chip_count = blocks // 2
    half = chip_count // 2
    my_index = scalar_ref[0]
    core = my_index % 2
    place = place_of(my_index // 2, chip_count)
    owner_at = 1 + REQS

    def device_at(distance, flip):
        onto = place + jnp.where(core == 0, distance, -distance) + chip_count
        chip = chip_at(lax.rem(onto, chip_count), chip_count)
        return 2 * chip + (core if flip == 0 else 1 - core)

    def clear(holder, _):
        used_s[holder] = 0
        return 0

    lax.fori_loop(0, blocks, clear, 0)

    def invert(block, _):
        inverse_s[scalar_ref[owner_at + block]] = block
        return 0

    lax.fori_loop(0, blocks, invert, 0)

    page_s[...] = page_ref[...].astype(jnp.float32)

    pieces_of = []
    for r in range(REQS):
        for j in range(blocks_req):
            start = j * rows_dev
            low, high = max(start, BLK), start + rows_dev
            if high > BLK:
                pieces_of.append((r, r * blocks_req + j, low - start, low - BLK, high - BLK))
    slots = gather_slots(half)
    at = 0
    for stage_ref in stage_refs:
        for top in range(0, stage_ref.shape[0], rows_dev):
            placed_s[device_at(*slots[at])] = stage_ref[top : top + rows_dev, :]
            at += 1
    for r, block, skipped, low, high in pieces_of:
        rows_s[r, lead + low : lead + high, :] = placed_s[block, skipped:, : rows_s.shape[2]]
        rate_s[r, low:high, :] = placed_s[block, skipped:, rows_s.shape[2] :]
    normed_s[...] = jnp.zeros_like(normed_s)

    wide = (live_rows, 128)
    later = lax.broadcasted_iota(jnp.int32, (live_rows, live_rows), 0)
    sooner = lax.broadcasted_iota(jnp.int32, (live_rows, live_rows), 1)
    causal = later >= sooner
    ones = causal.astype(jnp.float32)
    position = lax.broadcasted_iota(jnp.int32, wide, 0) + BLK
    lead_position = lax.broadcasted_iota(jnp.int32, (live_rows + lead, channels), 0) + BLK - lead
    spread_row = lax.broadcasted_iota(jnp.int32, (piece_count * 128, channels), 0)
    spread_col = lax.broadcasted_iota(jnp.int32, (piece_count * 128, channels), 1)
    spread = (
        ((spread_row // 128) * piece_channels + spread_row % 128 == spread_col)
        & (spread_row % 128 < piece_channels)
    ).astype(jnp.bfloat16)

    lane = lax.broadcasted_iota(jnp.int32, (1, 128), 1)
    bias_lanes = jnp.zeros((1, 128), jnp.float32)
    decay_lanes = jnp.zeros((1, 128), jnp.float32)
    for h in range(heads_dev):
        bias_lanes = jnp.where(lane == h, number_ref[h], bias_lanes)
        decay_lanes = jnp.where(lane == h, number_ref[heads_dev + h], decay_lanes)

    for r in range(REQS):
        live_start = scalar_ref[1 + r] * BLK
        live = position >= live_start
        rate = rate_s[r] + bias_lanes
        step = jnp.where(live, jax.nn.softplus(rate), 0.0)
        drop = -decay_lanes * step
        total = jnp.dot(
            ones, drop, preferred_element_type=jnp.float32, precision=lax.Precision.HIGHEST
        )
        total_t = total.T
        step_t = step.T
        from_start = jnp.exp(total)
        span_tail = total[live_rows - 1 : live_rows, :]
        to_end = jnp.exp(span_tail - total) * step
        kept = jnp.exp(span_tail)
        for h in range(heads_dev):
            lags = []
            for p in range(piece_count):
                page = page_id_ref[r, p, my_index * heads_dev + h]
                holder = lax.div(page, pool_slots)
                rank = used_s[holder]
                used_s[holder] = rank + 1
                state_at = pl.ds(pl.multiple_of(rank * state_rows, state_rows), state_rows)
                lag_at = pl.ds(pl.multiple_of(PER_PEER * state_rows + 8 * rank, 8), 8)
                initial_s[p * state_rows : (p + 1) * state_rows, :] = page_s[holder, state_at, :]
                lags.append(page_s[holder, lag_at, :].astype(jnp.bfloat16))
            initial = initial_s[...]
            lag_lanes = jnp.concatenate(lags, axis=1)
            cached = jnp.dot(lag_lanes, spread, preferred_element_type=jnp.float32)
            first = h * row_width
            c0 = h * channels
            raw = rows_s[r, :, first + HEAD_DIM : first + row_width]
            raw = raw.astype(jnp.bfloat16).astype(jnp.float32)
            inputs = jnp.where(lead_position >= live_start, raw, 0.0)
            for lag in range(CONV - 1):
                inputs = jnp.where(
                    lead_position == live_start - (CONV - 1) + lag,
                    cached[lag : lag + 1, :],
                    inputs,
                )
            input_s[...] = inputs
            conv_ref[r, :, c0 : c0 + channels] = rows_s[
                r,
                live_rows + lead - (CONV - 1) : live_rows + lead,
                first + HEAD_DIM : first + row_width,
            ].astype(jnp.bfloat16)
            summed = jnp.broadcast_to(
                conv_bias[:, c0 : c0 + channels], (live_rows, channels)
            )
            for tap in range(CONV):
                begin = lead - (CONV - 1) + tap
                summed = summed + taps_ref[tap : tap + 1, c0 : c0 + channels].astype(
                    jnp.float32
                ) * input_s[begin : begin + live_rows, :]
            mixed_in = (summed * jax.nn.sigmoid(summed)).astype(jnp.bfloat16)
            x_part = mixed_in[:, :HEAD_DIM]
            b_part = mixed_in[:, HEAD_DIM : HEAD_DIM + STATE]
            c_part = mixed_in[:, HEAD_DIM + STATE :]
            x_float = x_part.astype(jnp.float32)
            last = (((1,), (1,)), ((), ()))
            scores = lax.dot_general(c_part, b_part, last, preferred_element_type=jnp.float32)
            gaps = jnp.where(causal, total[:, h : h + 1] - total_t[h : h + 1, :], 0.0)
            weights = jnp.where(causal, jnp.exp(gaps) * scores * step_t[h : h + 1, :], 0.0)
            outputs = jnp.dot(
                weights.astype(jnp.bfloat16), x_part, preferred_element_type=jnp.float32
            )
            reader = (c_part.astype(jnp.float32) * from_start[:, h : h + 1]).astype(jnp.bfloat16)
            outputs = outputs + lax.dot_general(
                reader, initial.astype(jnp.bfloat16), last, preferred_element_type=jnp.float32
            )
            outputs = outputs + number_ref[2 * heads_dev + h] * x_float
            entering = (x_float * to_end[:, h : h + 1]).astype(jnp.bfloat16)
            added = lax.dot_general(
                entering,
                b_part,
                (((0,), (0,)), ((), ())),
                preferred_element_type=jnp.float32,
            )
            state_ref[r, h] = kept[:, h : h + 1] * initial + added
            gate = rows_s[r, lead:, first : first + HEAD_DIM]
            gate = gate.astype(jnp.bfloat16).astype(jnp.float32)
            gated = outputs * (gate * jax.nn.sigmoid(gate))
            scale = lax.rsqrt(jnp.mean(gated * gated, axis=1, keepdims=True) + EPSILON)
            gain = gains[:, h * HEAD_DIM : (h + 1) * HEAD_DIM]
            normed = jnp.where(live, gated * scale * gain, 0.0)
            for rr, block, skipped, low, high in pieces_of:
                if rr == r:
                    normed_s[block, skipped:, h * HEAD_DIM : (h + 1) * HEAD_DIM] = normed[low:high]

    for at, (distance, flip) in enumerate(send_slots(half)):
        rows = slice(at * rows_dev, (at + 1) * rows_dev)
        mine_ref[rows, :] = normed_s[inverse_s[device_at(distance, flip)]].astype(jnp.bfloat16)
        theirs_ref[rows, :] = normed_s[inverse_s[device_at(-distance, 1 - flip)]].astype(
            jnp.bfloat16
        )


def body(
    hidden,
    in_weight,
    dt_weight,
    dt_bias,
    decay_rate,
    conv_weight,
    conv_bias,
    skip,
    norm_gain,
    out_weight,
    state_pool,
    conv_pool,
    hit_page,
    prefix_blocks,
    owners,
):
    device_count = lax.axis_size("dp")
    my_index = lax.axis_index("dp").astype(jnp.int32).reshape(1)
    heads_dev = dt_weight.shape[0]
    piece_count = hit_page.shape[2]
    row_width = 2 * HEAD_DIM + 2 * STATE
    channels = HEAD_DIM + 2 * STATE
    rows_dev = hidden.shape[0]
    pool_slots, state_rows, _ = state_pool.shape
    chip_count = device_count // 2
    half = chip_count // 2
    page_ids = jnp.swapaxes(hit_page, 1, 2)

    held = other_core(out_weight, chip_count)
    own_type = hidden
    other_type = other_core(hidden, chip_count)

    first_other, state_here = lax.optimization_barrier((other_type, state_pool))
    other_type = first_other
    page_rows = PER_PEER * state_rows + 8 * PER_PEER
    entries = REQS * heads_dev * piece_count
    offered = kernel_call(
        functools.partial(offer_kernel, entries),
        jax.ShapeDtypeStruct((device_count, page_rows, STATE), state_pool.dtype),
        [my_index, page_ids, state_here, jnp.swapaxes(conv_pool, 0, 1)],
        [
            pltpu.SMEM((entries + 1,), jnp.int32),
            pltpu.VMEM((CONV - 1, pool_slots, STATE), jnp.float32),
            pltpu.VMEM((device_count, 8 * PER_PEER, STATE), jnp.float32),
        ],
        "offer_pages",
        smem=2,
        limit=VMEM_ALL,
    )
    received = lax.all_to_all(offered, "dp", split_axis=0, concat_axis=0, tiled=True)

    staged = []
    pending = []
    for step in range(1, half):
        own_type = stream(own_type, chip_count)
        other_type = stream(other_type, chip_count)
        if step == 1:
            own_type, other_type, received = lax.optimization_barrier(
                (own_type, other_type, received)
            )
        crossed = other_core(own_type, chip_count)
        if step == 1:
            own_here, weight_here, rates_here, crossed = lax.optimization_barrier(
                (hidden, in_weight, dt_weight, crossed)
            )
            own_here, weight_here, rates_here = load(own_here, weight_here, rates_here)
            pending = [own_here, first_other]
        pending += [own_type, other_type, crossed, other_core(other_type, chip_count)]
        if len(pending) >= 6 or step == half - 1:
            staged.append(stage(pending, weight_here, rates_here))
            pending = []
    own_type = stream(own_type, chip_count)
    last = [own_type, other_core(own_type, chip_count)]
    staged.append(stage(last, weight_here, rates_here))

    live_rows = SPAN - BLK
    scalars = jnp.concatenate([my_index, prefix_blocks, owners])
    numbers = jnp.concatenate([dt_bias, decay_rate, skip])
    normed_rows = jax.ShapeDtypeStruct((chip_count * rows_dev, heads_dev * HEAD_DIM), jnp.bfloat16)
    final_state, final_conv, mine, theirs = kernel_call(
        functools.partial(mix_kernel, (heads_dev, piece_count, pool_slots, len(staged))),
        [
            jax.ShapeDtypeStruct((REQS, heads_dev, HEAD_DIM, STATE), jnp.float32),
            jax.ShapeDtypeStruct((REQS, CONV - 1, heads_dev * channels), jnp.bfloat16),
            normed_rows,
            normed_rows,
        ],
        [
            scalars,
            page_ids,
            numbers,
            received,
            conv_weight,
            conv_bias,
            norm_gain,
            *staged,
        ],
        [
            pltpu.VMEM((device_count, rows_dev, heads_dev * row_width + 128), jnp.float32),
            pltpu.VMEM((REQS, live_rows + 8, heads_dev * row_width), jnp.float32),
            pltpu.VMEM((REQS, live_rows, 128), jnp.float32),
            pltpu.VMEM((live_rows + 8, channels), jnp.float32),
            pltpu.VMEM((device_count, rows_dev, heads_dev * HEAD_DIM), jnp.float32),
            pltpu.VMEM((HEAD_DIM, STATE), jnp.float32),
            pltpu.VMEM(received.shape, jnp.float32),
            pltpu.SMEM((device_count,), jnp.int32),
            pltpu.SMEM((device_count,), jnp.int32),
        ],
        "mixer",
        flops=1 << 30,
        smem=3,
    )

    theirs = other_core(theirs, chip_count)
    width = out_weight.shape[1]
    total_rows = chip_count * rows_dev
    block = jax.ShapeDtypeStruct((rows_dev, width), jnp.bfloat16)
    part = kernel_call(
        part_kernel,
        jax.ShapeDtypeStruct((total_rows, width), jnp.float32),
        [mine, out_weight],
        [],
        "sums_part",
        flops=1 << 30,
    )
    first, second = kernel_call(
        functools.partial(first_kernel, rows_dev),
        [block, block],
        [part, theirs, held],
        [],
        "sums_first",
        flops=1 << 30,
    )
    own_sum = stream(first, chip_count)
    other_sum = stream(second, chip_count)
    shares = kernel_call(
        functools.partial(rest_kernel, rows_dev),
        jax.ShapeDtypeStruct((total_rows - 2 * rows_dev, width), jnp.float32),
        [part, theirs, held],
        [],
        "sums_rest",
        flops=1 << 30,
    )

    def onward(at, *arrived):
        top = (at - 2) * rows_dev
        return kernel_call(
            functools.partial(add_kernel, top), block, [shares, *arrived], [], "onward"
        )

    slots = send_slots(half)
    for at in range(2, len(slots) - 1):
        if slots[at][1] == 0:
            own_sum = stream(onward(at, own_sum), chip_count)
        else:
            other_sum = stream(onward(at, other_sum), chip_count)
    crossed = other_core(other_sum, chip_count)
    mixed = onward(len(slots) - 1, own_sum, crossed)
    return (mixed, final_state, final_conv)


def solution(mesh):
    return jax.shard_map(
        body,
        mesh=mesh,
        in_specs=(
            P(("groups", "dp"), None),
            P(None, "dp"),
            P("dp", None),
            P("dp"),
            P("dp"),
            P(None, "dp"),
            P("dp"),
            P("dp"),
            P("dp"),
            P("dp", None),
            P(("groups", "dp"), None, None),
            P(("groups", "dp"), None, None),
            P("groups", None, None),
            P("groups"),
            P("groups"),
        ),
        out_specs=(
            P(("groups", "dp"), None),
            P("groups", "dp", None, None),
            P("groups", None, "dp"),
        ),
        check_vma=False,
    )
```

```python
import functools

import jax
import jax.numpy as jnp
from jax import lax
from jax.experimental import pallas as pl
from jax.experimental.pallas import tpu as pltpu
from jax.sharding import PartitionSpec as P

HEAD_DIM = 128
STATE = 128
CONV = 4
REQS = 2
SPAN = 192
BLK = 64


EPSILON = 1e-05
PER_PEER = 2
VMEM_LIMIT = 16 * 1024 * 1024
VMEM_ALL = 60 * 1024 * 1024


def folded(chip_count):
    return chip_count <= 8


def chip_at(place, chip_count):
    if not folded(chip_count):
        return place
    back = 2 * (chip_count - 1 - place) + 1
    if isinstance(place, int):
        return 2 * place if place < chip_count // 2 else back
    return jnp.where(place < chip_count // 2, 2 * place, back)


def place_of(chip, chip_count):
    if not folded(chip_count):
        return chip
    return jnp.where(chip % 2 == 0, chip // 2, chip_count - 1 - chip // 2)


def stream(array, chip_count):
    pairs = []
    for place in range(chip_count):
        for core in range(2):
            onto = (place + 1 - 2 * core) % chip_count
            pairs.append((2 * chip_at(place, chip_count) + core, 2 * chip_at(onto, chip_count) + core))
    return lax.ppermute(array, "dp", pairs)


def other_core(array, chip_count):
    return lax.ppermute(array, "dp", [(d, d ^ 1) for d in range(2 * chip_count)])


def kernel_call(kernel, outs, operands, scratch, name, flops=0, smem=0, limit=VMEM_LIMIT):
    several = isinstance(outs, list)
    whole = pl.BlockSpec(memory_space=pltpu.VMEM)
    scalars = pl.BlockSpec(memory_space=pltpu.SMEM)
    return pl.pallas_call(
        kernel,
        out_shape=outs,
        in_specs=[scalars] * smem + [whole] * (len(operands) - smem),
        out_specs=[whole] * len(outs) if several else whole,
        scratch_shapes=scratch,
        compiler_params=pltpu.CompilerParams(vmem_limit_bytes=limit),
        cost_estimate=pl.CostEstimate(flops=flops, bytes_accessed=8 << 20, transcendentals=0),
        name=name,
    )(*operands)


def offer_kernel(entries, my_ref, ids_ref, *refs):
    state_refs, conv_refs, (out_ref, slot_s, conv_s, lag_s) = refs[:2], refs[2:4], refs[4:]
    pool_slots, state_rows, _ = state_refs[0].shape
    lag_rows = conv_refs[0].shape[0]
    piece_channels = conv_refs[0].shape[2]
    receivers = out_ref.shape[0]
    heads_dev = ids_ref.shape[2] // (2 * receivers)
    page_rows = out_ref.shape[1] // 2
    my_index = my_ref[0]
    core = my_index % 2
    conv_s[...] = jnp.zeros_like(conv_s)
    lag_s[...] = jnp.zeros_like(lag_s)
    for other in range(2):
        conv_s[other, :, :, :piece_channels] = conv_refs[other][...].astype(jnp.float32)

    def one_receiver(receiver, _):
        first_head = (2 * receiver + core) * heads_dev
        for other in range(2):
            first = (my_index + (1 - 2 * core) * other) * pool_slots
            used = jnp.int32(0)
            for r in range(REQS):
                for h in range(heads_dev):
                    for p in range(ids_ref.shape[1]):
                        slot = ids_ref[r, p, first_head + h] - first
                        slot_s[used] = slot
                        held = jnp.logical_and(slot >= 0, slot < pool_slots)
                        used = used + held.astype(jnp.int32)
            for place in range(PER_PEER):
                slot = jnp.clip(slot_s[place], 0, pool_slots - 1)
                top = other * page_rows + place * state_rows
                out_ref[receiver, top : top + state_rows, :] = state_refs[other][slot]
                for lag in range(lag_rows):
                    row = 8 * place + lag
                    lag_s[other, receiver, row : row + 1, :] = conv_s[
                        other, lag, pl.ds(slot, 1), :
                    ]
        return 0

    lax.fori_loop(0, receivers, one_receiver, 0)
    for other in range(2):
        top = other * page_rows + PER_PEER * state_rows
        out_ref[:, top : (other + 1) * page_rows, :] = lag_s[other].astype(out_ref.dtype)


def column_tiles(width, body):
    tile = min(512, width)

    def one_tile(index, _):
        body(pl.ds(pl.multiple_of(index * tile, tile), tile))
        return 0

    lax.fori_loop(0, width // tile, one_tile, 0)


def load_kernel(*refs):
    count = (len(refs) - 1) // 2
    sems = refs[-1]
    copies = [
        pltpu.make_async_copy(refs[at], refs[count + at], sems.at[at]) for at in range(count)
    ]
    for copy in copies:
        copy.start()
    for copy in copies:
        copy.wait()


def load(*arrays):
    return pl.pallas_call(
        load_kernel,
        out_shape=[jax.ShapeDtypeStruct(a.shape, a.dtype) for a in arrays],
        in_specs=[pl.BlockSpec(memory_space=pltpu.HBM)] * len(arrays),
        out_specs=[pl.BlockSpec(memory_space=pltpu.VMEM)] * len(arrays),
        scratch_shapes=[pltpu.SemaphoreType.DMA((len(arrays),))],
        compiler_params=pltpu.CompilerParams(vmem_limit_bytes=VMEM_LIMIT),
        cost_estimate=pl.CostEstimate(flops=0, bytes_accessed=8 << 20, transcendentals=0),
        name="load",
    )(*[pltpu.with_memory_space_constraint(a, pltpu.HBM) for a in arrays])


def stage_kernel(count, *refs):
    block_refs = refs[:count]
    weight_ref, rate_weight_ref, out_ref, joined_s = refs[count:]
    rows = block_refs[0].shape[0]
    width = weight_ref.shape[1]
    for at, block_ref in enumerate(block_refs):
        joined_s[at * rows : (at + 1) * rows, :] = block_ref[...]
    rates = rate_weight_ref.shape[0]
    out_ref[:, width:] = jnp.zeros((out_ref.shape[0], out_ref.shape[1] - width), jnp.float32)
    out_ref[:, width : width + rates] = lax.dot_general(
        joined_s[...],
        rate_weight_ref[...],
        (((1,), (1,)), ((), ())),
        preferred_element_type=jnp.float32,
    )

    def body(columns):
        out_ref[:, columns] = jnp.dot(
            joined_s[...], weight_ref[:, columns], preferred_element_type=jnp.float32
        )

    column_tiles(width, body)


def stage(blocks, weight, rate_weight):
    rows, depth = blocks[0].shape
    total = rows * len(blocks)
    width = weight.shape[1] + 128
    return kernel_call(
        functools.partial(stage_kernel, len(blocks)),
        jax.ShapeDtypeStruct((total, width), jnp.float32),
        [*blocks, weight, rate_weight],
        [pltpu.VMEM((total, depth), jnp.bfloat16)],
        "stage",
        flops=2 * 256 * depth * width,
    )


def part_kernel(mine_ref, weight_ref, out_ref):
    def body(columns):
        out_ref[:, columns] = jnp.dot(
            mine_ref[...], weight_ref[:, columns], preferred_element_type=jnp.float32
        )

    column_tiles(out_ref.shape[1], body)


def first_kernel(rows, part_ref, theirs_ref, held_ref, first_ref, second_ref):
    def body(columns):
        total = part_ref[: 2 * rows, columns] + jnp.dot(
            theirs_ref[: 2 * rows, :], held_ref[:, columns], preferred_element_type=jnp.float32
        )
        first_ref[:, columns] = total[:rows].astype(first_ref.dtype)
        second_ref[:, columns] = total[rows:].astype(second_ref.dtype)

    column_tiles(held_ref.shape[1], body)


def rest_kernel(rows, part_ref, theirs_ref, held_ref, out_ref):
    def body(columns):
        out_ref[:, columns] = part_ref[2 * rows :, columns] + jnp.dot(
            theirs_ref[2 * rows :, :], held_ref[:, columns], preferred_element_type=jnp.float32
        )

    column_tiles(held_ref.shape[1], body)


def add_kernel(top, share_ref, *refs):
    out_ref = refs[-1]
    total = share_ref[top : top + out_ref.shape[0], :]
    for arrived_ref in refs[:-1]:
        total = total + arrived_ref[...].astype(jnp.float32)
    out_ref[...] = total.astype(out_ref.dtype)


def gather_slots(half):
    slots = [(0, 0), (0, 1)]
    for step in range(1, half):
        slots += [(-step, 0), (-step, 1), (step, 1), (step, 0)]
    return slots + [(-half, 0), (half, 1)]


def send_slots(half):
    slots = []
    for step in range(half, 0, -1):
        slots.append((step, 0))
        if step > 1:
            slots.append((step - 1, 1))
    return slots + [(0, 0)]


def mix_kernel(sizes, scalar_ref, page_id_ref, number_ref, page_ref, *rest):
    heads_dev, piece_count, pool_slots, stages = sizes
    taps_ref, conv_bias_ref, gain_ref = rest[:3]
    stage_refs, rest = rest[3 : 3 + stages], rest[3 + stages :]
    conv_bias = conv_bias_ref[...].astype(jnp.float32).reshape(1, -1)
    gains = gain_ref[...].astype(jnp.float32).reshape(1, -1)
    state_ref, conv_ref, mine_ref, theirs_ref = rest[:4]
    placed_s, rows_s, rate_s, input_s, normed_s, initial_s, page_s, inverse_s, used_s = rest[4:]
    blocks, rows_dev, _ = placed_s.shape
    live_rows = SPAN - BLK
    lead = 8
    state_rows = HEAD_DIM // piece_count
    channels = HEAD_DIM + 2 * STATE
    row_width = HEAD_DIM + channels
    piece_channels = channels // piece_count
    blocks_req = blocks // REQS

    chip_count = blocks // 2
    half = chip_count // 2
    my_index = scalar_ref[0]
    core = my_index % 2
    place = place_of(my_index // 2, chip_count)
    owner_at = 1 + REQS

    def device_at(distance, flip):
        onto = place + jnp.where(core == 0, distance, -distance) + chip_count
        chip = chip_at(lax.rem(onto, chip_count), chip_count)
        return 2 * chip + (core if flip == 0 else 1 - core)

    def clear(holder, _):
        used_s[holder] = 0
        return 0

    lax.fori_loop(0, blocks, clear, 0)

    def invert(block, _):
        inverse_s[scalar_ref[owner_at + block]] = block
        return 0

    lax.fori_loop(0, blocks, invert, 0)

    page_s[...] = page_ref[...].astype(jnp.float32)

    pieces_of = []
    for r in range(REQS):
        for j in range(blocks_req):
            start = j * rows_dev
            low, high = max(start, BLK), start + rows_dev
            if high > BLK:
                pieces_of.append((r, r * blocks_req + j, low - start, low - BLK, high - BLK))
    slots = gather_slots(half)
    at = 0
    for stage_ref in stage_refs:
        for top in range(0, stage_ref.shape[0], rows_dev):
            placed_s[device_at(*slots[at])] = stage_ref[top : top + rows_dev, :]
            at += 1
    for r, block, skipped, low, high in pieces_of:
        rows_s[r, lead + low : lead + high, :] = placed_s[block, skipped:, : rows_s.shape[2]]
        rate_s[r, low:high, :] = placed_s[block, skipped:, rows_s.shape[2] :]
    normed_s[...] = jnp.zeros_like(normed_s)

    wide = (live_rows, 128)
    later = lax.broadcasted_iota(jnp.int32, (live_rows, live_rows), 0)
    sooner = lax.broadcasted_iota(jnp.int32, (live_rows, live_rows), 1)
    causal = later >= sooner
    ones = causal.astype(jnp.float32)
    position = lax.broadcasted_iota(jnp.int32, wide, 0) + BLK
    lead_position = lax.broadcasted_iota(jnp.int32, (live_rows + lead, channels), 0) + BLK - lead
    spread_row = lax.broadcasted_iota(jnp.int32, (piece_count * 128, channels), 0)
    spread_col = lax.broadcasted_iota(jnp.int32, (piece_count * 128, channels), 1)
    spread = (
        ((spread_row // 128) * piece_channels + spread_row % 128 == spread_col)
        & (spread_row % 128 < piece_channels)
    ).astype(jnp.bfloat16)

    lane = lax.broadcasted_iota(jnp.int32, (1, 128), 1)
    bias_lanes = jnp.zeros((1, 128), jnp.float32)
    decay_lanes = jnp.zeros((1, 128), jnp.float32)
    for h in range(heads_dev):
        bias_lanes = jnp.where(lane == h, number_ref[h], bias_lanes)
        decay_lanes = jnp.where(lane == h, number_ref[heads_dev + h], decay_lanes)

    for r in range(REQS):
        live_start = scalar_ref[1 + r] * BLK
        live = position >= live_start
        rate = rate_s[r] + bias_lanes
        step = jnp.where(live, jax.nn.softplus(rate), 0.0)
        drop = -decay_lanes * step
        total = jnp.dot(
            ones, drop, preferred_element_type=jnp.float32, precision=lax.Precision.HIGHEST
        )
        total_t = total.T
        step_t = step.T
        from_start = jnp.exp(total)
        span_tail = total[live_rows - 1 : live_rows, :]
        to_end = jnp.exp(span_tail - total) * step
        kept = jnp.exp(span_tail)
        for h in range(heads_dev):
            lags = []
            for p in range(piece_count):
                page = page_id_ref[r, p, my_index * heads_dev + h]
                holder = lax.div(page, pool_slots)
                rank = used_s[holder]
                used_s[holder] = rank + 1
                top = jnp.where(holder % 2 == core, 0, page_s.shape[1] // 2)
                state_at = pl.multiple_of(top + rank * state_rows, 8)
                lag_at = pl.multiple_of(top + PER_PEER * state_rows + 8 * rank, 8)
                initial_s[p * state_rows : (p + 1) * state_rows, :] = page_s[
                    holder // 2, pl.ds(state_at, state_rows), :
                ]
                lags.append(page_s[holder // 2, pl.ds(lag_at, 8), :].astype(jnp.bfloat16))
            initial = initial_s[...]
            lag_lanes = jnp.concatenate(lags, axis=1)
            cached = jnp.dot(lag_lanes, spread, preferred_element_type=jnp.float32)
            first = h * row_width
            c0 = h * channels
            raw = rows_s[r, :, first + HEAD_DIM : first + row_width]
            raw = raw.astype(jnp.bfloat16).astype(jnp.float32)
            inputs = jnp.where(lead_position >= live_start, raw, 0.0)
            for lag in range(CONV - 1):
                inputs = jnp.where(
                    lead_position == live_start - (CONV - 1) + lag,
                    cached[lag : lag + 1, :],
                    inputs,
                )
            input_s[...] = inputs
            conv_ref[r, :, c0 : c0 + channels] = rows_s[
                r,
                live_rows + lead - (CONV - 1) : live_rows + lead,
                first + HEAD_DIM : first + row_width,
            ].astype(jnp.bfloat16)
            summed = jnp.broadcast_to(
                conv_bias[:, c0 : c0 + channels], (live_rows, channels)
            )
            for tap in range(CONV):
                begin = lead - (CONV - 1) + tap
                summed = summed + taps_ref[tap : tap + 1, c0 : c0 + channels].astype(
                    jnp.float32
                ) * input_s[begin : begin + live_rows, :]
            mixed_in = (summed * jax.nn.sigmoid(summed)).astype(jnp.bfloat16)
            x_part = mixed_in[:, :HEAD_DIM]
            b_part = mixed_in[:, HEAD_DIM : HEAD_DIM + STATE]
            c_part = mixed_in[:, HEAD_DIM + STATE :]
            x_float = x_part.astype(jnp.float32)
            last = (((1,), (1,)), ((), ()))
            scores = lax.dot_general(c_part, b_part, last, preferred_element_type=jnp.float32)
            gaps = jnp.where(causal, total[:, h : h + 1] - total_t[h : h + 1, :], 0.0)
            weights = jnp.where(causal, jnp.exp(gaps) * scores * step_t[h : h + 1, :], 0.0)
            outputs = jnp.dot(
                weights.astype(jnp.bfloat16), x_part, preferred_element_type=jnp.float32
            )
            reader = (c_part.astype(jnp.float32) * from_start[:, h : h + 1]).astype(jnp.bfloat16)
            outputs = outputs + lax.dot_general(
                reader, initial.astype(jnp.bfloat16), last, preferred_element_type=jnp.float32
            )
            outputs = outputs + number_ref[2 * heads_dev + h] * x_float
            entering = (x_float * to_end[:, h : h + 1]).astype(jnp.bfloat16)
            added = lax.dot_general(
                entering,
                b_part,
                (((0,), (0,)), ((), ())),
                preferred_element_type=jnp.float32,
            )
            state_ref[r, h] = kept[:, h : h + 1] * initial + added
            gate = rows_s[r, lead:, first : first + HEAD_DIM]
            gate = gate.astype(jnp.bfloat16).astype(jnp.float32)
            gated = outputs * (gate * jax.nn.sigmoid(gate))
            scale = lax.rsqrt(jnp.mean(gated * gated, axis=1, keepdims=True) + EPSILON)
            gain = gains[:, h * HEAD_DIM : (h + 1) * HEAD_DIM]
            normed = jnp.where(live, gated * scale * gain, 0.0)
            for rr, block, skipped, low, high in pieces_of:
                if rr == r:
                    normed_s[block, skipped:, h * HEAD_DIM : (h + 1) * HEAD_DIM] = normed[low:high]

    for at, (distance, flip) in enumerate(send_slots(half)):
        rows = slice(at * rows_dev, (at + 1) * rows_dev)
        mine_ref[rows, :] = normed_s[inverse_s[device_at(distance, flip)]].astype(jnp.bfloat16)
        theirs_ref[rows, :] = normed_s[inverse_s[device_at(-distance, 1 - flip)]].astype(
            jnp.bfloat16
        )


def body(
    hidden,
    in_weight,
    dt_weight,
    dt_bias,
    decay_rate,
    conv_weight,
    conv_bias,
    skip,
    norm_gain,
    out_weight,
    state_pool,
    conv_pool,
    hit_page,
    prefix_blocks,
    owners,
):
    device_count = lax.axis_size("dp")
    my_index = lax.axis_index("dp").astype(jnp.int32).reshape(1)
    heads_dev = dt_weight.shape[0]
    piece_count = hit_page.shape[2]
    row_width = 2 * HEAD_DIM + 2 * STATE
    channels = HEAD_DIM + 2 * STATE
    rows_dev = hidden.shape[0]
    pool_slots, state_rows, _ = state_pool.shape
    chip_count = device_count // 2
    half = chip_count // 2
    page_ids = jnp.swapaxes(hit_page, 1, 2)

    other_type = other_core(hidden, chip_count)
    conv_pool = jnp.swapaxes(conv_pool, 0, 1)
    state_there = other_core(state_pool, chip_count)
    conv_there = other_core(conv_pool, chip_count)
    held = other_core(out_weight, chip_count)

    page_rows = PER_PEER * state_rows + 8 * PER_PEER
    entries = REQS * heads_dev * piece_count
    offered = kernel_call(
        functools.partial(offer_kernel, entries),
        jax.ShapeDtypeStruct((chip_count, 2 * page_rows, STATE), state_pool.dtype),
        [
            my_index,
            page_ids,
            *[
                pltpu.with_memory_space_constraint(pool, pltpu.HBM)
                for pool in (state_pool, state_there, conv_pool, conv_there)
            ],
        ],
        [
            pltpu.SMEM((entries + 1,), jnp.int32),
            pltpu.VMEM((2, CONV - 1, pool_slots, STATE), jnp.float32),
            pltpu.VMEM((2, chip_count, 8 * PER_PEER, STATE), jnp.float32),
        ],
        "offer_pages",
        smem=2,
        limit=VMEM_ALL,
    )
    first_other = other_type
    own_type = stream(hidden, chip_count)
    other_type = stream(other_type, chip_count)
    offered, own_type, other_type = lax.optimization_barrier((offered, own_type, other_type))
    same_type = [[2 * chip + core for chip in range(chip_count)] for core in range(2)]
    received = lax.all_to_all(
        offered, "dp", split_axis=0, concat_axis=0, axis_index_groups=same_type, tiled=True
    )

    staged = []
    pending = []
    for step in range(1, half):
        if step > 1:
            own_type = stream(own_type, chip_count)
            other_type = stream(other_type, chip_count)
        crossed = other_core(own_type, chip_count)
        if step == 1:
            received, own_here, weight_here, rates_here, crossed = lax.optimization_barrier(
                (received, hidden, in_weight, dt_weight, crossed)
            )
            own_here, weight_here, rates_here = load(own_here, weight_here, rates_here)
            pending = [own_here, first_other]
        pending += [own_type, other_type, crossed, other_core(other_type, chip_count)]
        if len(pending) >= 6 or step == half - 1:
            staged.append(stage(pending, weight_here, rates_here))
            pending = []
    own_type = stream(own_type, chip_count)
    last = [own_type, other_core(own_type, chip_count)]
    staged.append(stage(last, weight_here, rates_here))

    live_rows = SPAN - BLK
    scalars = jnp.concatenate([my_index, prefix_blocks, owners])
    numbers = jnp.concatenate([dt_bias, decay_rate, skip])
    normed_rows = jax.ShapeDtypeStruct((chip_count * rows_dev, heads_dev * HEAD_DIM), jnp.bfloat16)
    final_state, final_conv, mine, theirs = kernel_call(
        functools.partial(mix_kernel, (heads_dev, piece_count, pool_slots, len(staged))),
        [
            jax.ShapeDtypeStruct((REQS, heads_dev, HEAD_DIM, STATE), jnp.float32),
            jax.ShapeDtypeStruct((REQS, CONV - 1, heads_dev * channels), jnp.bfloat16),
            normed_rows,
            normed_rows,
        ],
        [
            scalars,
            page_ids,
            numbers,
            received,
            conv_weight,
            conv_bias,
            norm_gain,
            *staged,
        ],
        [
            pltpu.VMEM((device_count, rows_dev, heads_dev * row_width + 128), jnp.float32),
            pltpu.VMEM((REQS, live_rows + 8, heads_dev * row_width), jnp.float32),
            pltpu.VMEM((REQS, live_rows, 128), jnp.float32),
            pltpu.VMEM((live_rows + 8, channels), jnp.float32),
            pltpu.VMEM((device_count, rows_dev, heads_dev * HEAD_DIM), jnp.float32),
            pltpu.VMEM((HEAD_DIM, STATE), jnp.float32),
            pltpu.VMEM(received.shape, jnp.float32),
            pltpu.SMEM((device_count,), jnp.int32),
            pltpu.SMEM((device_count,), jnp.int32),
        ],
        "mixer",
        flops=1 << 30,
        smem=3,
    )

    theirs = other_core(theirs, chip_count)
    width = out_weight.shape[1]
    total_rows = chip_count * rows_dev
    block = jax.ShapeDtypeStruct((rows_dev, width), jnp.bfloat16)
    part = kernel_call(
        part_kernel,
        jax.ShapeDtypeStruct((total_rows, width), jnp.float32),
        [mine, out_weight],
        [],
        "sums_part",
        flops=1 << 30,
    )
    first, second = kernel_call(
        functools.partial(first_kernel, rows_dev),
        [block, block],
        [part, theirs, held],
        [],
        "sums_first",
        flops=1 << 30,
    )
    own_sum = stream(first, chip_count)
    other_sum = stream(second, chip_count)
    shares = kernel_call(
        functools.partial(rest_kernel, rows_dev),
        jax.ShapeDtypeStruct((total_rows - 2 * rows_dev, width), jnp.float32),
        [part, theirs, held],
        [],
        "sums_rest",
        flops=1 << 30,
    )

    def onward(at, *arrived):
        top = (at - 2) * rows_dev
        return kernel_call(
            functools.partial(add_kernel, top), block, [shares, *arrived], [], "onward"
        )

    slots = send_slots(half)
    for at in range(2, len(slots) - 1):
        if slots[at][1] == 0:
            own_sum = stream(onward(at, own_sum), chip_count)
        else:
            other_sum = stream(onward(at, other_sum), chip_count)
    crossed = other_core(other_sum, chip_count)
    mixed = onward(len(slots) - 1, own_sum, crossed)
    return (mixed, final_state, final_conv)


def solution(mesh):
    return jax.shard_map(
        body,
        mesh=mesh,
        in_specs=(
            P(("groups", "dp"), None),
            P(None, "dp"),
            P("dp", None),
            P("dp"),
            P("dp"),
            P(None, "dp"),
            P("dp"),
            P("dp"),
            P("dp"),
            P("dp", None),
            P(("groups", "dp"), None, None),
            P(("groups", "dp"), None, None),
            P("groups", None, None),
            P("groups"),
            P("groups"),
        ),
        out_specs=(
            P(("groups", "dp"), None),
            P("groups", "dp", None, None),
            P("groups", None, "dp"),
        ),
        check_vma=False,
    )
```

```python
import functools

import jax
import jax.numpy as jnp
from jax import lax
from jax.experimental import pallas as pl
from jax.experimental.pallas import tpu as pltpu
from jax.sharding import PartitionSpec as P

HEAD_DIM = 128
STATE = 128
CONV = 4
REQS = 2
SPAN = 192
BLK = 64


EPSILON = 1e-05
PER_PEER = 2
VMEM_LIMIT = 16 * 1024 * 1024
VMEM_ALL = 60 * 1024 * 1024


def folded(chip_count):
    return chip_count <= 8


def chip_at(place, chip_count):
    if not folded(chip_count):
        return place
    back = 2 * (chip_count - 1 - place) + 1
    if isinstance(place, int):
        return 2 * place if place < chip_count // 2 else back
    return jnp.where(place < chip_count // 2, 2 * place, back)


def place_of(chip, chip_count):
    if not folded(chip_count):
        return chip
    return jnp.where(chip % 2 == 0, chip // 2, chip_count - 1 - chip // 2)


def stream(array, chip_count):
    pairs = []
    for place in range(chip_count):
        for core in range(2):
            onto = (place + 1 - 2 * core) % chip_count
            pairs.append((2 * chip_at(place, chip_count) + core, 2 * chip_at(onto, chip_count) + core))
    return lax.ppermute(array, "dp", pairs)


def other_core(array, chip_count):
    return lax.ppermute(array, "dp", [(d, d ^ 1) for d in range(2 * chip_count)])


def kernel_call(kernel, outs, operands, scratch, name, flops=0, smem=0, limit=VMEM_LIMIT):
    several = isinstance(outs, list)
    whole = pl.BlockSpec(memory_space=pltpu.VMEM)
    scalars = pl.BlockSpec(memory_space=pltpu.SMEM)
    return pl.pallas_call(
        kernel,
        out_shape=outs,
        in_specs=[scalars] * smem + [whole] * (len(operands) - smem),
        out_specs=[whole] * len(outs) if several else whole,
        scratch_shapes=scratch,
        compiler_params=pltpu.CompilerParams(vmem_limit_bytes=limit),
        cost_estimate=pl.CostEstimate(flops=flops, bytes_accessed=8 << 20, transcendentals=0),
        name=name,
    )(*operands)


def offer_kernel(entries, my_ref, ids_ref, state_ref, conv_ref, out_ref, slot_s, conv_s, lag_s):
    pool_slots, state_rows, _ = state_ref.shape
    lag_rows = conv_ref.shape[0]
    piece_channels = conv_ref.shape[2]
    receivers = out_ref.shape[0]
    heads_dev = ids_ref.shape[2] // receivers
    first = my_ref[0] * pool_slots
    conv_s[...] = jnp.zeros_like(conv_s)
    conv_s[:, :, :piece_channels] = conv_ref[...].astype(jnp.float32)
    lag_s[...] = jnp.zeros_like(lag_s)

    def one_receiver(receiver, _):
        used = jnp.int32(0)
        for r in range(REQS):
            for h in range(heads_dev):
                for p in range(ids_ref.shape[1]):
                    slot = ids_ref[r, p, receiver * heads_dev + h] - first
                    slot_s[used] = slot
                    held = jnp.logical_and(slot >= 0, slot < pool_slots)
                    used = used + held.astype(jnp.int32)
        for place in range(PER_PEER):
            slot = jnp.clip(slot_s[place], 0, pool_slots - 1)
            out_ref[receiver, place * state_rows : (place + 1) * state_rows, :] = state_ref[slot]
            for lag in range(lag_rows):
                row = 8 * place + lag
                lag_s[receiver, row : row + 1, :] = conv_s[lag, pl.ds(slot, 1), :]
        return 0

    lax.fori_loop(0, receivers, one_receiver, 0)
    out_ref[:, PER_PEER * state_rows :, :] = lag_s[...].astype(out_ref.dtype)


def column_tiles(width, body):
    tile = min(512, width)

    def one_tile(index, _):
        body(pl.ds(pl.multiple_of(index * tile, tile), tile))
        return 0

    lax.fori_loop(0, width // tile, one_tile, 0)


def join_blocks(block_refs, rate_weight_ref, out_ref, joined_s, width):
    rows = block_refs[0].shape[0]
    for at, block_ref in enumerate(block_refs):
        joined_s[at * rows : (at + 1) * rows, :] = block_ref[...]
    rates = rate_weight_ref.shape[0]
    out_ref[:, width:] = jnp.zeros((out_ref.shape[0], out_ref.shape[1] - width), jnp.float32)
    out_ref[:, width : width + rates] = lax.dot_general(
        joined_s[...],
        rate_weight_ref[...],
        (((1,), (1,)), ((), ())),
        preferred_element_type=jnp.float32,
    )


def stage_kernel(count, *refs):
    block_refs = refs[:count]
    weight_ref, rate_weight_ref, out_ref, joined_s = refs[count:]
    width = weight_ref.shape[1]
    join_blocks(block_refs, rate_weight_ref, out_ref, joined_s, width)

    def body(columns):
        out_ref[:, columns] = jnp.dot(
            joined_s[...], weight_ref[:, columns], preferred_element_type=jnp.float32
        )

    column_tiles(width, body)


def first_stage_kernel(count, tile, *refs):
    block_refs = refs[:count]
    weight_ref, rate_weight_ref, out_ref, held_ref, joined_s, sems = refs[count:]
    width = weight_ref.shape[1]
    copies = []
    for at, left in enumerate(range(0, width, tile)):
        columns = pl.ds(left, tile)
        copies.append(
            pltpu.make_async_copy(
                weight_ref.at[:, columns], held_ref.at[:, columns], sems.at[at]
            )
        )
    for copy in copies:
        copy.start()
    join_blocks(block_refs, rate_weight_ref, out_ref, joined_s, width)
    for at, left in enumerate(range(0, width, tile)):
        copies[at].wait()
        out_ref[:, left : left + tile] = jnp.dot(
            joined_s[...], held_ref[:, left : left + tile], preferred_element_type=jnp.float32
        )


def from_hbm(array):
    return pltpu.with_memory_space_constraint(array, pltpu.HBM)


def stage(blocks, weight, rate_weight, first=False):
    rows, depth = blocks[0].shape
    total = rows * len(blocks)
    out = jax.ShapeDtypeStruct((total, weight.shape[1] + 128), jnp.float32)
    joined = pltpu.VMEM((total, depth), jnp.bfloat16)
    if not first:
        return kernel_call(
            functools.partial(stage_kernel, len(blocks)),
            out,
            [*blocks, weight, rate_weight],
            [joined],
            "stage",
            flops=2 * 256 * depth * weight.shape[1],
        )
    whole = pl.BlockSpec(memory_space=pltpu.VMEM)
    tile = min(256, weight.shape[1])
    return pl.pallas_call(
        functools.partial(first_stage_kernel, len(blocks), tile),
        out_shape=[out, jax.ShapeDtypeStruct(weight.shape, weight.dtype)],
        in_specs=[whole] * len(blocks) + [pl.BlockSpec(memory_space=pltpu.HBM), whole],
        out_specs=[whole] * 2,
        scratch_shapes=[joined, pltpu.SemaphoreType.DMA((weight.shape[1] // tile,))],
        compiler_params=pltpu.CompilerParams(vmem_limit_bytes=VMEM_LIMIT),
        cost_estimate=pl.CostEstimate(
            flops=2 * 256 * depth * weight.shape[1], bytes_accessed=8 << 20, transcendentals=0
        ),
        name="first_stage",
    )(*blocks, from_hbm(weight), rate_weight)


def part_kernel(mine_ref, weight_ref, out_ref):
    def body(columns):
        out_ref[:, columns] = jnp.dot(
            mine_ref[...], weight_ref[:, columns], preferred_element_type=jnp.float32
        )

    column_tiles(out_ref.shape[1], body)


def first_kernel(rows, part_ref, theirs_ref, held_ref, first_ref, second_ref):
    def body(columns):
        total = part_ref[: 2 * rows, columns] + jnp.dot(
            theirs_ref[: 2 * rows, :], held_ref[:, columns], preferred_element_type=jnp.float32
        )
        first_ref[:, columns] = total[:rows].astype(first_ref.dtype)
        second_ref[:, columns] = total[rows:].astype(second_ref.dtype)

    column_tiles(held_ref.shape[1], body)


def rest_kernel(rows, part_ref, theirs_ref, held_ref, out_ref):
    def body(columns):
        out_ref[:, columns] = part_ref[2 * rows :, columns] + jnp.dot(
            theirs_ref[2 * rows :, :], held_ref[:, columns], preferred_element_type=jnp.float32
        )

    column_tiles(held_ref.shape[1], body)


def add_kernel(top, share_ref, *refs):
    out_ref = refs[-1]
    total = share_ref[top : top + out_ref.shape[0], :]
    for arrived_ref in refs[:-1]:
        total = total + arrived_ref[...].astype(jnp.float32)
    out_ref[...] = total.astype(out_ref.dtype)


def gather_slots(half):
    slots = [(0, 0), (0, 1)]
    for step in range(1, half):
        slots += [(-step, 0), (-step, 1), (step, 1), (step, 0)]
    return slots + [(-half, 0), (half, 1)]


def send_slots(half):
    slots = []
    for step in range(half, 0, -1):
        slots.append((step, 0))
        if step > 1:
            slots.append((step - 1, 1))
    return slots + [(0, 0)]


def mix_kernel(sizes, scalar_ref, page_id_ref, number_ref, page_ref, *rest):
    heads_dev, piece_count, pool_slots, stages = sizes
    taps_ref, conv_bias_ref, gain_ref = rest[:3]
    stage_refs, rest = rest[3 : 3 + stages], rest[3 + stages :]
    conv_bias = conv_bias_ref[...].astype(jnp.float32).reshape(1, -1)
    gains = gain_ref[...].astype(jnp.float32).reshape(1, -1)
    state_ref, conv_ref, mine_ref, theirs_ref = rest[:4]
    placed_s, rows_s, rate_s, input_s, normed_s, initial_s, page_s, inverse_s, used_s = rest[4:]
    blocks, rows_dev, _ = placed_s.shape
    live_rows = SPAN - BLK
    lead = 8
    state_rows = HEAD_DIM // piece_count
    channels = HEAD_DIM + 2 * STATE
    row_width = HEAD_DIM + channels
    piece_channels = channels // piece_count
    blocks_req = blocks // REQS

    chip_count = blocks // 2
    half = chip_count // 2
    my_index = scalar_ref[0]
    core = my_index % 2
    place = place_of(my_index // 2, chip_count)
    owner_at = 1 + REQS

    def device_at(distance, flip):
        onto = place + jnp.where(core == 0, distance, -distance) + chip_count
        chip = chip_at(lax.rem(onto, chip_count), chip_count)
        return 2 * chip + (core if flip == 0 else 1 - core)

    def clear(holder, _):
        used_s[holder] = 0
        return 0

    lax.fori_loop(0, blocks, clear, 0)

    def invert(block, _):
        inverse_s[scalar_ref[owner_at + block]] = block
        return 0

    lax.fori_loop(0, blocks, invert, 0)

    page_s[...] = page_ref[...].astype(jnp.float32)

    pieces_of = []
    for r in range(REQS):
        for j in range(blocks_req):
            start = j * rows_dev
            low, high = max(start, BLK), start + rows_dev
            if high > BLK:
                pieces_of.append((r, r * blocks_req + j, low - start, low - BLK, high - BLK))
    slots = gather_slots(half)
    at = 0
    for stage_ref in stage_refs:
        for top in range(0, stage_ref.shape[0], rows_dev):
            placed_s[device_at(*slots[at])] = stage_ref[top : top + rows_dev, :]
            at += 1
    for r, block, skipped, low, high in pieces_of:
        rows_s[r, lead + low : lead + high, :] = placed_s[block, skipped:, : rows_s.shape[2]]
        rate_s[r, low:high, :] = placed_s[block, skipped:, rows_s.shape[2] :]
    normed_s[...] = jnp.zeros_like(normed_s)

    wide = (live_rows, 128)
    later = lax.broadcasted_iota(jnp.int32, (live_rows, live_rows), 0)
    sooner = lax.broadcasted_iota(jnp.int32, (live_rows, live_rows), 1)
    causal = later >= sooner
    ones = causal.astype(jnp.float32)
    position = lax.broadcasted_iota(jnp.int32, wide, 0) + BLK
    lead_position = lax.broadcasted_iota(jnp.int32, (live_rows + lead, channels), 0) + BLK - lead
    spread_row = lax.broadcasted_iota(jnp.int32, (piece_count * 128, channels), 0)
    spread_col = lax.broadcasted_iota(jnp.int32, (piece_count * 128, channels), 1)
    spread = (
        ((spread_row // 128) * piece_channels + spread_row % 128 == spread_col)
        & (spread_row % 128 < piece_channels)
    ).astype(jnp.bfloat16)

    lane = lax.broadcasted_iota(jnp.int32, (1, 128), 1)
    bias_lanes = jnp.zeros((1, 128), jnp.float32)
    decay_lanes = jnp.zeros((1, 128), jnp.float32)
    for h in range(heads_dev):
        bias_lanes = jnp.where(lane == h, number_ref[h], bias_lanes)
        decay_lanes = jnp.where(lane == h, number_ref[heads_dev + h], decay_lanes)

    for r in range(REQS):
        live_start = scalar_ref[1 + r] * BLK
        live = position >= live_start
        rate = rate_s[r] + bias_lanes
        step = jnp.where(live, jax.nn.softplus(rate), 0.0)
        drop = -decay_lanes * step
        total = jnp.dot(
            ones, drop, preferred_element_type=jnp.float32, precision=lax.Precision.HIGHEST
        )
        total_t = total.T
        step_t = step.T
        from_start = jnp.exp(total)
        span_tail = total[live_rows - 1 : live_rows, :]
        to_end = jnp.exp(span_tail - total) * step
        kept = jnp.exp(span_tail)
        for h in range(heads_dev):
            lags = []
            for p in range(piece_count):
                page = page_id_ref[r, p, my_index * heads_dev + h]
                holder = lax.div(page, pool_slots)
                rank = used_s[holder]
                used_s[holder] = rank + 1
                state_at = pl.ds(pl.multiple_of(rank * state_rows, state_rows), state_rows)
                lag_at = pl.ds(pl.multiple_of(PER_PEER * state_rows + 8 * rank, 8), 8)
                initial_s[p * state_rows : (p + 1) * state_rows, :] = page_s[holder, state_at, :]
                lags.append(page_s[holder, lag_at, :].astype(jnp.bfloat16))
            initial = initial_s[...]
            lag_lanes = jnp.concatenate(lags, axis=1)
            cached = jnp.dot(lag_lanes, spread, preferred_element_type=jnp.float32)
            first = h * row_width
            c0 = h * channels
            raw = rows_s[r, :, first + HEAD_DIM : first + row_width]
            raw = raw.astype(jnp.bfloat16).astype(jnp.float32)
            inputs = jnp.where(lead_position >= live_start, raw, 0.0)
            for lag in range(CONV - 1):
                inputs = jnp.where(
                    lead_position == live_start - (CONV - 1) + lag,
                    cached[lag : lag + 1, :],
                    inputs,
                )
            input_s[...] = inputs
            conv_ref[r, :, c0 : c0 + channels] = rows_s[
                r,
                live_rows + lead - (CONV - 1) : live_rows + lead,
                first + HEAD_DIM : first + row_width,
            ].astype(jnp.bfloat16)
            summed = jnp.broadcast_to(
                conv_bias[:, c0 : c0 + channels], (live_rows, channels)
            )
            for tap in range(CONV):
                begin = lead - (CONV - 1) + tap
                summed = summed + taps_ref[tap : tap + 1, c0 : c0 + channels].astype(
                    jnp.float32
                ) * input_s[begin : begin + live_rows, :]
            mixed_in = (summed * jax.nn.sigmoid(summed)).astype(jnp.bfloat16)
            x_part = mixed_in[:, :HEAD_DIM]
            b_part = mixed_in[:, HEAD_DIM : HEAD_DIM + STATE]
            c_part = mixed_in[:, HEAD_DIM + STATE :]
            x_float = x_part.astype(jnp.float32)
            last = (((1,), (1,)), ((), ()))
            scores = lax.dot_general(c_part, b_part, last, preferred_element_type=jnp.float32)
            gaps = jnp.where(causal, total[:, h : h + 1] - total_t[h : h + 1, :], 0.0)
            weights = jnp.where(causal, jnp.exp(gaps) * scores * step_t[h : h + 1, :], 0.0)
            outputs = jnp.dot(
                weights.astype(jnp.bfloat16), x_part, preferred_element_type=jnp.float32
            )
            reader = (c_part.astype(jnp.float32) * from_start[:, h : h + 1]).astype(jnp.bfloat16)
            outputs = outputs + lax.dot_general(
                reader, initial.astype(jnp.bfloat16), last, preferred_element_type=jnp.float32
            )
            outputs = outputs + number_ref[2 * heads_dev + h] * x_float
            entering = (x_float * to_end[:, h : h + 1]).astype(jnp.bfloat16)
            added = lax.dot_general(
                entering,
                b_part,
                (((0,), (0,)), ((), ())),
                preferred_element_type=jnp.float32,
            )
            state_ref[r, h] = kept[:, h : h + 1] * initial + added
            gate = rows_s[r, lead:, first : first + HEAD_DIM]
            gate = gate.astype(jnp.bfloat16).astype(jnp.float32)
            gated = outputs * (gate * jax.nn.sigmoid(gate))
            scale = lax.rsqrt(jnp.mean(gated * gated, axis=1, keepdims=True) + EPSILON)
            gain = gains[:, h * HEAD_DIM : (h + 1) * HEAD_DIM]
            normed = jnp.where(live, gated * scale * gain, 0.0)
            for rr, block, skipped, low, high in pieces_of:
                if rr == r:
                    normed_s[block, skipped:, h * HEAD_DIM : (h + 1) * HEAD_DIM] = normed[low:high]

    for at, (distance, flip) in enumerate(send_slots(half)):
        rows = slice(at * rows_dev, (at + 1) * rows_dev)
        mine_ref[rows, :] = normed_s[inverse_s[device_at(distance, flip)]].astype(jnp.bfloat16)
        theirs_ref[rows, :] = normed_s[inverse_s[device_at(-distance, 1 - flip)]].astype(
            jnp.bfloat16
        )


def body(
    hidden,
    in_weight,
    dt_weight,
    dt_bias,
    decay_rate,
    conv_weight,
    conv_bias,
    skip,
    norm_gain,
    out_weight,
    state_pool,
    conv_pool,
    hit_page,
    prefix_blocks,
    owners,
):
    device_count = lax.axis_size("dp")
    my_index = lax.axis_index("dp").astype(jnp.int32).reshape(1)
    heads_dev = dt_weight.shape[0]
    piece_count = hit_page.shape[2]
    row_width = 2 * HEAD_DIM + 2 * STATE
    channels = HEAD_DIM + 2 * STATE
    rows_dev = hidden.shape[0]
    pool_slots, state_rows, _ = state_pool.shape
    chip_count = device_count // 2
    half = chip_count // 2
    page_ids = jnp.swapaxes(hit_page, 1, 2)

    other_type = other_core(hidden, chip_count)
    page_rows = PER_PEER * state_rows + 8 * PER_PEER
    entries = REQS * heads_dev * piece_count
    offered = kernel_call(
        functools.partial(offer_kernel, entries),
        jax.ShapeDtypeStruct((device_count, page_rows, STATE), state_pool.dtype),
        [
            my_index,
            page_ids,
            from_hbm(state_pool),
            from_hbm(jnp.swapaxes(conv_pool, 0, 1)),
        ],
        [
            pltpu.SMEM((entries + 1,), jnp.int32),
            pltpu.VMEM((CONV - 1, pool_slots, STATE), jnp.float32),
            pltpu.VMEM((device_count, 8 * PER_PEER, STATE), jnp.float32),
        ],
        "offer_pages",
        smem=2,
        limit=VMEM_ALL,
    )
    first_other = other_type
    own_type = stream(hidden, chip_count)
    other_type = stream(other_type, chip_count)
    scalars = jnp.concatenate([my_index, prefix_blocks, owners])
    numbers = jnp.concatenate([dt_bias, decay_rate, skip])
    offered, own_type, other_type, scalars, numbers, held = lax.optimization_barrier(
        (offered, own_type, other_type, scalars, numbers, out_weight)
    )
    held = other_core(held, chip_count)
    received = lax.all_to_all(offered, "dp", split_axis=0, concat_axis=0, tiled=True)
    crossed = other_core(own_type, chip_count)
    received, hidden, in_weight, dt_weight = lax.optimization_barrier(
        (received, hidden, in_weight, dt_weight)
    )
    rate_weight = from_hbm(dt_weight)
    blocks = [from_hbm(hidden), first_other, own_type, other_type, crossed]
    blocks.append(other_core(other_type, chip_count))
    out, weight_here = stage(blocks, in_weight, rate_weight, first=True)
    staged = [out]
    pending = []
    for step in range(2, half):
        own_type = stream(own_type, chip_count)
        other_type = stream(other_type, chip_count)
        if step == half - 1:
            own_type, staged[0] = lax.optimization_barrier((own_type, staged[0]))
        pending += [
            own_type,
            other_type,
            other_core(own_type, chip_count),
            other_core(other_type, chip_count),
        ]
        if len(pending) >= 6 or step == half - 1:
            staged.append(stage(pending, weight_here, rate_weight))
            pending = []
    own_type = stream(own_type, chip_count)
    last = [own_type, other_core(own_type, chip_count)]
    staged.append(stage(last, weight_here, rate_weight))

    live_rows = SPAN - BLK
    normed_rows = jax.ShapeDtypeStruct((chip_count * rows_dev, heads_dev * HEAD_DIM), jnp.bfloat16)
    final_state, final_conv, mine, theirs = kernel_call(
        functools.partial(mix_kernel, (heads_dev, piece_count, pool_slots, len(staged))),
        [
            jax.ShapeDtypeStruct((REQS, heads_dev, HEAD_DIM, STATE), jnp.float32),
            jax.ShapeDtypeStruct((REQS, CONV - 1, heads_dev * channels), jnp.bfloat16),
            normed_rows,
            normed_rows,
        ],
        [
            scalars,
            page_ids,
            numbers,
            received,
            conv_weight,
            conv_bias,
            norm_gain,
            *staged,
        ],
        [
            pltpu.VMEM((device_count, rows_dev, heads_dev * row_width + 128), jnp.float32),
            pltpu.VMEM((REQS, live_rows + 8, heads_dev * row_width), jnp.float32),
            pltpu.VMEM((REQS, live_rows, 128), jnp.float32),
            pltpu.VMEM((live_rows + 8, channels), jnp.float32),
            pltpu.VMEM((device_count, rows_dev, heads_dev * HEAD_DIM), jnp.float32),
            pltpu.VMEM((HEAD_DIM, STATE), jnp.float32),
            pltpu.VMEM(received.shape, jnp.float32),
            pltpu.SMEM((device_count,), jnp.int32),
            pltpu.SMEM((device_count,), jnp.int32),
        ],
        "mixer",
        flops=1 << 30,
        smem=3,
    )

    theirs = other_core(theirs, chip_count)
    width = out_weight.shape[1]
    total_rows = chip_count * rows_dev
    block = jax.ShapeDtypeStruct((rows_dev, width), jnp.bfloat16)
    part = kernel_call(
        part_kernel,
        jax.ShapeDtypeStruct((total_rows, width), jnp.float32),
        [mine, out_weight],
        [],
        "sums_part",
        flops=1 << 30,
    )
    first, second = kernel_call(
        functools.partial(first_kernel, rows_dev),
        [block, block],
        [part, theirs, held],
        [],
        "sums_first",
        flops=1 << 30,
    )
    own_sum = stream(first, chip_count)
    other_sum = stream(second, chip_count)
    shares = kernel_call(
        functools.partial(rest_kernel, rows_dev),
        jax.ShapeDtypeStruct((total_rows - 2 * rows_dev, width), jnp.float32),
        [part, theirs, held],
        [],
        "sums_rest",
        flops=1 << 30,
    )

    def onward(at, *arrived):
        top = (at - 2) * rows_dev
        return kernel_call(
            functools.partial(add_kernel, top), block, [shares, *arrived], [], "onward"
        )

    slots = send_slots(half)
    for at in range(2, len(slots) - 1):
        if slots[at][1] == 0:
            own_sum = stream(onward(at, own_sum), chip_count)
        else:
            other_sum = stream(onward(at, other_sum), chip_count)
    crossed = other_core(other_sum, chip_count)
    mixed = onward(len(slots) - 1, own_sum, crossed)
    return (mixed, final_state, final_conv)


def solution(mesh):
    return jax.shard_map(
        body,
        mesh=mesh,
        in_specs=(
            P(("groups", "dp"), None),
            P(None, "dp"),
            P("dp", None),
            P("dp"),
            P("dp"),
            P(None, "dp"),
            P("dp"),
            P("dp"),
            P("dp"),
            P("dp", None),
            P(("groups", "dp"), None, None),
            P(("groups", "dp"), None, None),
            P("groups", None, None),
            P("groups"),
            P("groups"),
        ),
        out_specs=(
            P(("groups", "dp"), None),
            P("groups", "dp", None, None),
            P("groups", None, "dp"),
        ),
        check_vma=False,
    )
```

```python
import functools

import jax
import jax.numpy as jnp
from jax import lax
from jax.experimental import pallas as pl
from jax.experimental.pallas import tpu as pltpu
from jax.sharding import PartitionSpec as P

HEAD_DIM = 128
STATE = 128
CONV = 4
REQS = 2
SPAN = 192
BLK = 64


EPSILON = 1e-05
PER_PEER = 2
VMEM_LIMIT = 16 * 1024 * 1024
VMEM_ALL = 60 * 1024 * 1024


def folded(chip_count):
    return chip_count <= 8


def chip_at(place, chip_count):
    if not folded(chip_count):
        return place
    back = 2 * (chip_count - 1 - place) + 1
    if isinstance(place, int):
        return 2 * place if place < chip_count // 2 else back
    return jnp.where(place < chip_count // 2, 2 * place, back)


def place_of(chip, chip_count):
    if not folded(chip_count):
        return chip
    return jnp.where(chip % 2 == 0, chip // 2, chip_count - 1 - chip // 2)


def stream(array, chip_count):
    pairs = []
    for place in range(chip_count):
        for core in range(2):
            onto = (place + 1 - 2 * core) % chip_count
            pairs.append((2 * chip_at(place, chip_count) + core, 2 * chip_at(onto, chip_count) + core))
    return lax.ppermute(array, "dp", pairs)


def other_core(array, chip_count):
    return lax.ppermute(array, "dp", [(d, d ^ 1) for d in range(2 * chip_count)])


def kernel_call(kernel, outs, operands, scratch, name, flops=0, smem=0, limit=VMEM_LIMIT):
    several = isinstance(outs, list)
    whole = pl.BlockSpec(memory_space=pltpu.VMEM)
    scalars = pl.BlockSpec(memory_space=pltpu.SMEM)
    return pl.pallas_call(
        kernel,
        out_shape=outs,
        in_specs=[scalars] * smem + [whole] * (len(operands) - smem),
        out_specs=[whole] * len(outs) if several else whole,
        scratch_shapes=scratch,
        compiler_params=pltpu.CompilerParams(vmem_limit_bytes=limit),
        cost_estimate=pl.CostEstimate(flops=flops, bytes_accessed=8 << 20, transcendentals=0),
        name=name,
    )(*operands)


def offer_kernel(entries, my_ref, ids_ref, state_ref, conv_ref, out_ref, slot_s, conv_s, lag_s):
    pool_slots, state_rows, _ = state_ref.shape
    lag_rows = conv_ref.shape[0]
    piece_channels = conv_ref.shape[2]
    receivers = out_ref.shape[0]
    heads_dev = ids_ref.shape[2] // receivers
    first = my_ref[0] * pool_slots
    conv_s[...] = jnp.zeros_like(conv_s)
    conv_s[:, :, :piece_channels] = conv_ref[...].astype(jnp.float32)
    lag_s[...] = jnp.zeros_like(lag_s)

    def one_receiver(receiver, _):
        used = jnp.int32(0)
        for r in range(REQS):
            for h in range(heads_dev):
                for p in range(ids_ref.shape[1]):
                    slot = ids_ref[r, p, receiver * heads_dev + h] - first
                    slot_s[used] = slot
                    held = jnp.logical_and(slot >= 0, slot < pool_slots)
                    used = used + held.astype(jnp.int32)
        for place in range(PER_PEER):
            slot = jnp.clip(slot_s[place], 0, pool_slots - 1)
            out_ref[receiver, place * state_rows : (place + 1) * state_rows, :] = state_ref[slot]
            for lag in range(lag_rows):
                row = 8 * place + lag
                lag_s[receiver, row : row + 1, :] = conv_s[lag, pl.ds(slot, 1), :]
        return 0

    lax.fori_loop(0, receivers, one_receiver, 0)
    out_ref[:, PER_PEER * state_rows :, :] = lag_s[...].astype(out_ref.dtype)


def column_tiles(width, body):
    tile = min(512, width)

    def one_tile(index, _):
        body(pl.ds(pl.multiple_of(index * tile, tile), tile))
        return 0

    lax.fori_loop(0, width // tile, one_tile, 0)


def rate_columns(joined_s, rate_weight_ref, out_ref, width):
    rates = rate_weight_ref.shape[0]
    out_ref[:, width:] = jnp.zeros((out_ref.shape[0], out_ref.shape[1] - width), jnp.float32)
    out_ref[:, width : width + rates] = lax.dot_general(
        joined_s[...],
        rate_weight_ref[...],
        (((1,), (1,)), ((), ())),
        preferred_element_type=jnp.float32,
    )


def stage_kernel(count, *refs):
    block_refs = refs[:count]
    weight_ref, rate_weight_ref, out_ref, joined_s = refs[count:]
    rows = block_refs[0].shape[0]
    width = weight_ref.shape[1]
    for at, block_ref in enumerate(block_refs):
        joined_s[at * rows : (at + 1) * rows, :] = block_ref[...]
    rate_columns(joined_s, rate_weight_ref, out_ref, width)

    def body(columns):
        out_ref[:, columns] = jnp.dot(
            joined_s[...], weight_ref[:, columns], preferred_element_type=jnp.float32
        )

    column_tiles(width, body)


def first_stage_kernel(count, tile, *refs):
    block_refs = refs[:count]
    weight_ref, rate_weight_ref, out_ref, held_ref, fetched_s, joined_s, sems = refs[count:]
    rows = block_refs[0].shape[0]
    width = weight_ref.shape[1]
    lefts = range(0, width, tile)
    fetches = [
        pltpu.make_async_copy(block_ref, fetched_s.at[at], sems.at[at])
        for at, block_ref in enumerate(block_refs)
    ]
    loads = [
        pltpu.make_async_copy(
            weight_ref.at[:, pl.ds(left, tile)],
            held_ref.at[:, pl.ds(left, tile)],
            sems.at[count + at],
        )
        for at, left in enumerate(lefts)
    ]
    for copy in fetches + loads:
        copy.start()
    for at, copy in enumerate(fetches):
        copy.wait()
        joined_s[at * rows : (at + 1) * rows, :] = fetched_s[at]
    rate_columns(joined_s, rate_weight_ref, out_ref, width)
    for left, copy in zip(lefts, loads, strict=True):
        copy.wait()
        out_ref[:, left : left + tile] = jnp.dot(
            joined_s[...], held_ref[:, left : left + tile], preferred_element_type=jnp.float32
        )


def from_hbm(array):
    return pltpu.with_memory_space_constraint(array, pltpu.HBM)


def stage(blocks, weight, rate_weight, first=False):
    rows, depth = blocks[0].shape
    count = len(blocks)
    total = rows * count
    width = weight.shape[1]
    out = jax.ShapeDtypeStruct((total, width + 128), jnp.float32)
    joined = pltpu.VMEM((total, depth), jnp.bfloat16)
    flops = 2 * 256 * depth * width
    if not first:
        return kernel_call(
            functools.partial(stage_kernel, count),
            out,
            [*blocks, weight, rate_weight],
            [joined],
            "stage",
            flops=flops,
        )
    whole = pl.BlockSpec(memory_space=pltpu.VMEM)
    tile = min(256, width)
    return pl.pallas_call(
        functools.partial(first_stage_kernel, count, tile),
        out_shape=[out, jax.ShapeDtypeStruct(weight.shape, weight.dtype)],
        in_specs=[pl.BlockSpec(memory_space=pl.ANY)] * count
        + [pl.BlockSpec(memory_space=pltpu.HBM), whole],
        out_specs=[whole] * 2,
        scratch_shapes=[
            pltpu.VMEM((count, rows, depth), jnp.bfloat16),
            joined,
            pltpu.SemaphoreType.DMA((count + width // tile,)),
        ],
        compiler_params=pltpu.CompilerParams(vmem_limit_bytes=VMEM_LIMIT),
        cost_estimate=pl.CostEstimate(
            flops=3 * flops, bytes_accessed=16 << 20, transcendentals=0
        ),
        name="first_stage",
    )(*blocks, from_hbm(weight), rate_weight)


def part_kernel(mine_ref, weight_ref, out_ref):
    def body(columns):
        out_ref[:, columns] = jnp.dot(
            mine_ref[...], weight_ref[:, columns], preferred_element_type=jnp.float32
        )

    column_tiles(out_ref.shape[1], body)


def first_kernel(rows, part_ref, theirs_ref, held_ref, first_ref, second_ref):
    def body(columns):
        total = part_ref[: 2 * rows, columns] + jnp.dot(
            theirs_ref[: 2 * rows, :], held_ref[:, columns], preferred_element_type=jnp.float32
        )
        first_ref[:, columns] = total[:rows].astype(first_ref.dtype)
        second_ref[:, columns] = total[rows:].astype(second_ref.dtype)

    column_tiles(held_ref.shape[1], body)


def rest_kernel(rows, part_ref, theirs_ref, held_ref, out_ref):
    def body(columns):
        out_ref[:, columns] = part_ref[2 * rows :, columns] + jnp.dot(
            theirs_ref[2 * rows :, :], held_ref[:, columns], preferred_element_type=jnp.float32
        )

    column_tiles(held_ref.shape[1], body)


def add_kernel(top, share_ref, *refs):
    out_ref = refs[-1]
    total = share_ref[top : top + out_ref.shape[0], :]
    for arrived_ref in refs[:-1]:
        total = total + arrived_ref[...].astype(jnp.float32)
    out_ref[...] = total.astype(out_ref.dtype)


def gather_slots(half):
    slots = [(0, 0), (0, 1)]
    for step in range(1, half):
        slots += [(-step, 0), (-step, 1), (step, 1), (step, 0)]
    return slots + [(-half, 0), (half, 1)]


def send_slots(half):
    slots = []
    for step in range(half, 0, -1):
        slots.append((step, 0))
        if step > 1:
            slots.append((step - 1, 1))
    return slots + [(0, 0)]


def mix_kernel(sizes, scalar_ref, page_id_ref, number_ref, page_ref, *rest):
    heads_dev, piece_count, pool_slots, stages = sizes
    taps_ref, conv_bias_ref, gain_ref = rest[:3]
    stage_refs, rest = rest[3 : 3 + stages], rest[3 + stages :]
    conv_bias = conv_bias_ref[...].astype(jnp.float32).reshape(1, -1)
    gains = gain_ref[...].astype(jnp.float32).reshape(1, -1)
    state_ref, conv_ref, mine_ref, theirs_ref = rest[:4]
    placed_s, rows_s, rate_s, input_s, normed_s, initial_s, page_s, inverse_s, used_s = rest[4:]
    blocks, rows_dev, _ = placed_s.shape
    live_rows = SPAN - BLK
    lead = 8
    state_rows = HEAD_DIM // piece_count
    channels = HEAD_DIM + 2 * STATE
    row_width = HEAD_DIM + channels
    piece_channels = channels // piece_count
    blocks_req = blocks // REQS

    chip_count = blocks // 2
    half = chip_count // 2
    my_index = scalar_ref[0]
    core = my_index % 2
    place = place_of(my_index // 2, chip_count)
    owner_at = 1 + REQS

    def device_at(distance, flip):
        onto = place + jnp.where(core == 0, distance, -distance) + chip_count
        chip = chip_at(lax.rem(onto, chip_count), chip_count)
        return 2 * chip + (core if flip == 0 else 1 - core)

    def clear(holder, _):
        used_s[holder] = 0
        return 0

    lax.fori_loop(0, blocks, clear, 0)

    def invert(block, _):
        inverse_s[scalar_ref[owner_at + block]] = block
        return 0

    lax.fori_loop(0, blocks, invert, 0)

    page_s[...] = page_ref[...].astype(jnp.float32)

    pieces_of = []
    for r in range(REQS):
        for j in range(blocks_req):
            start = j * rows_dev
            low, high = max(start, BLK), start + rows_dev
            if high > BLK:
                pieces_of.append((r, r * blocks_req + j, low - start, low - BLK, high - BLK))
    slots = gather_slots(half)
    at = 0
    for stage_ref in stage_refs:
        for top in range(0, stage_ref.shape[0], rows_dev):
            placed_s[device_at(*slots[at])] = stage_ref[top : top + rows_dev, :]
            at += 1
    for r, block, skipped, low, high in pieces_of:
        rows_s[r, lead + low : lead + high, :] = placed_s[block, skipped:, : rows_s.shape[2]]
        rate_s[r, low:high, :] = placed_s[block, skipped:, rows_s.shape[2] :]
    normed_s[...] = jnp.zeros_like(normed_s)

    wide = (live_rows, 128)
    later = lax.broadcasted_iota(jnp.int32, (live_rows, live_rows), 0)
    sooner = lax.broadcasted_iota(jnp.int32, (live_rows, live_rows), 1)
    causal = later >= sooner
    ones = causal.astype(jnp.float32)
    position = lax.broadcasted_iota(jnp.int32, wide, 0) + BLK
    lead_position = lax.broadcasted_iota(jnp.int32, (live_rows + lead, channels), 0) + BLK - lead
    spread_row = lax.broadcasted_iota(jnp.int32, (piece_count * 128, channels), 0)
    spread_col = lax.broadcasted_iota(jnp.int32, (piece_count * 128, channels), 1)
    spread = (
        ((spread_row // 128) * piece_channels + spread_row % 128 == spread_col)
        & (spread_row % 128 < piece_channels)
    ).astype(jnp.bfloat16)

    lane = lax.broadcasted_iota(jnp.int32, (1, 128), 1)
    bias_lanes = jnp.zeros((1, 128), jnp.float32)
    decay_lanes = jnp.zeros((1, 128), jnp.float32)
    for h in range(heads_dev):
        bias_lanes = jnp.where(lane == h, number_ref[h], bias_lanes)
        decay_lanes = jnp.where(lane == h, number_ref[heads_dev + h], decay_lanes)

    for r in range(REQS):
        live_start = scalar_ref[1 + r] * BLK
        live = position >= live_start
        rate = rate_s[r] + bias_lanes
        step = jnp.where(live, jax.nn.softplus(rate), 0.0)
        drop = -decay_lanes * step
        total = jnp.dot(
            ones, drop, preferred_element_type=jnp.float32, precision=lax.Precision.HIGHEST
        )
        total_t = total.T
        step_t = step.T
        from_start = jnp.exp(total)
        span_tail = total[live_rows - 1 : live_rows, :]
        to_end = jnp.exp(span_tail - total) * step
        kept = jnp.exp(span_tail)
        for h in range(heads_dev):
            lags = []
            for p in range(piece_count):
                page = page_id_ref[r, p, my_index * heads_dev + h]
                holder = lax.div(page, pool_slots)
                rank = used_s[holder]
                used_s[holder] = rank + 1
                state_at = pl.ds(pl.multiple_of(rank * state_rows, state_rows), state_rows)
                lag_at = pl.ds(pl.multiple_of(PER_PEER * state_rows + 8 * rank, 8), 8)
                initial_s[p * state_rows : (p + 1) * state_rows, :] = page_s[holder, state_at, :]
                lags.append(page_s[holder, lag_at, :].astype(jnp.bfloat16))
            initial = initial_s[...]
            lag_lanes = jnp.concatenate(lags, axis=1)
            cached = jnp.dot(lag_lanes, spread, preferred_element_type=jnp.float32)
            first = h * row_width
            c0 = h * channels
            raw = rows_s[r, :, first + HEAD_DIM : first + row_width]
            raw = raw.astype(jnp.bfloat16).astype(jnp.float32)
            inputs = jnp.where(lead_position >= live_start, raw, 0.0)
            for lag in range(CONV - 1):
                inputs = jnp.where(
                    lead_position == live_start - (CONV - 1) + lag,
                    cached[lag : lag + 1, :],
                    inputs,
                )
            input_s[...] = inputs
            conv_ref[r, :, c0 : c0 + channels] = rows_s[
                r,
                live_rows + lead - (CONV - 1) : live_rows + lead,
                first + HEAD_DIM : first + row_width,
            ].astype(jnp.bfloat16)
            summed = jnp.broadcast_to(
                conv_bias[:, c0 : c0 + channels], (live_rows, channels)
            )
            for tap in range(CONV):
                begin = lead - (CONV - 1) + tap
                summed = summed + taps_ref[tap : tap + 1, c0 : c0 + channels].astype(
                    jnp.float32
                ) * input_s[begin : begin + live_rows, :]
            mixed_in = (summed * jax.nn.sigmoid(summed)).astype(jnp.bfloat16)
            x_part = mixed_in[:, :HEAD_DIM]
            b_part = mixed_in[:, HEAD_DIM : HEAD_DIM + STATE]
            c_part = mixed_in[:, HEAD_DIM + STATE :]
            x_float = x_part.astype(jnp.float32)
            last = (((1,), (1,)), ((), ()))
            scores = lax.dot_general(c_part, b_part, last, preferred_element_type=jnp.float32)
            gaps = jnp.where(causal, total[:, h : h + 1] - total_t[h : h + 1, :], 0.0)
            weights = jnp.where(causal, jnp.exp(gaps) * scores * step_t[h : h + 1, :], 0.0)
            outputs = jnp.dot(
                weights.astype(jnp.bfloat16), x_part, preferred_element_type=jnp.float32
            )
            reader = (c_part.astype(jnp.float32) * from_start[:, h : h + 1]).astype(jnp.bfloat16)
            outputs = outputs + lax.dot_general(
                reader, initial.astype(jnp.bfloat16), last, preferred_element_type=jnp.float32
            )
            outputs = outputs + number_ref[2 * heads_dev + h] * x_float
            entering = (x_float * to_end[:, h : h + 1]).astype(jnp.bfloat16)
            added = lax.dot_general(
                entering,
                b_part,
                (((0,), (0,)), ((), ())),
                preferred_element_type=jnp.float32,
            )
            state_ref[r, h] = kept[:, h : h + 1] * initial + added
            gate = rows_s[r, lead:, first : first + HEAD_DIM]
            gate = gate.astype(jnp.bfloat16).astype(jnp.float32)
            gated = outputs * (gate * jax.nn.sigmoid(gate))
            scale = lax.rsqrt(jnp.mean(gated * gated, axis=1, keepdims=True) + EPSILON)
            gain = gains[:, h * HEAD_DIM : (h + 1) * HEAD_DIM]
            normed = jnp.where(live, gated * scale * gain, 0.0)
            for rr, block, skipped, low, high in pieces_of:
                if rr == r:
                    normed_s[block, skipped:, h * HEAD_DIM : (h + 1) * HEAD_DIM] = normed[low:high]

    for at, (distance, flip) in enumerate(send_slots(half)):
        rows = slice(at * rows_dev, (at + 1) * rows_dev)
        mine_ref[rows, :] = normed_s[inverse_s[device_at(distance, flip)]].astype(jnp.bfloat16)
        theirs_ref[rows, :] = normed_s[inverse_s[device_at(-distance, 1 - flip)]].astype(
            jnp.bfloat16
        )


def body(
    hidden,
    in_weight,
    dt_weight,
    dt_bias,
    decay_rate,
    conv_weight,
    conv_bias,
    skip,
    norm_gain,
    out_weight,
    state_pool,
    conv_pool,
    hit_page,
    prefix_blocks,
    owners,
):
    device_count = lax.axis_size("dp")
    my_index = lax.axis_index("dp").astype(jnp.int32).reshape(1)
    heads_dev = dt_weight.shape[0]
    piece_count = hit_page.shape[2]
    row_width = 2 * HEAD_DIM + 2 * STATE
    channels = HEAD_DIM + 2 * STATE
    rows_dev = hidden.shape[0]
    pool_slots, state_rows, _ = state_pool.shape
    chip_count = device_count // 2
    half = chip_count // 2
    page_ids = jnp.swapaxes(hit_page, 1, 2)

    other_type = other_core(hidden, chip_count)
    page_rows = PER_PEER * state_rows + 8 * PER_PEER
    entries = REQS * heads_dev * piece_count
    offered = kernel_call(
        functools.partial(offer_kernel, entries),
        jax.ShapeDtypeStruct((device_count, page_rows, STATE), state_pool.dtype),
        [
            my_index,
            page_ids,
            from_hbm(state_pool),
            from_hbm(jnp.swapaxes(conv_pool, 0, 1)),
        ],
        [
            pltpu.SMEM((entries + 1,), jnp.int32),
            pltpu.VMEM((CONV - 1, pool_slots, STATE), jnp.float32),
            pltpu.VMEM((device_count, 8 * PER_PEER, STATE), jnp.float32),
        ],
        "offer_pages",
        smem=2,
        limit=VMEM_ALL,
    )
    scalars = jnp.concatenate([my_index, prefix_blocks, owners])
    numbers = jnp.concatenate([dt_bias, decay_rate, skip])
    own_type = hidden
    blocks = [hidden, other_type]
    for step in range(1, half):
        own_type = stream(own_type, chip_count)
        other_type = stream(other_type, chip_count)
        if step == 1:
            offered, scalars, numbers, own_type, held = lax.optimization_barrier(
                (offered, scalars, numbers, own_type, out_weight)
            )
            held = other_core(held, chip_count)
        crossed = other_core(own_type, chip_count)
        blocks += [own_type, other_type, crossed, other_core(other_type, chip_count)]
    own_type = stream(own_type, chip_count)
    offered, blocks[-1], blocks[-2] = lax.optimization_barrier((offered, blocks[-1], blocks[-2]))
    received = lax.all_to_all(offered, "dp", split_axis=0, concat_axis=0, tiled=True)
    rate_weight = from_hbm(dt_weight)
    out, weight_here = stage(blocks, in_weight, rate_weight, first=True)
    last = [own_type, other_core(own_type, chip_count)]
    staged = [out, stage(last, weight_here, rate_weight)]

    live_rows = SPAN - BLK
    normed_rows = jax.ShapeDtypeStruct((chip_count * rows_dev, heads_dev * HEAD_DIM), jnp.bfloat16)
    final_state, final_conv, mine, theirs = kernel_call(
        functools.partial(mix_kernel, (heads_dev, piece_count, pool_slots, len(staged))),
        [
            jax.ShapeDtypeStruct((REQS, heads_dev, HEAD_DIM, STATE), jnp.float32),
            jax.ShapeDtypeStruct((REQS, CONV - 1, heads_dev * channels), jnp.bfloat16),
            normed_rows,
            normed_rows,
        ],
        [
            scalars,
            page_ids,
            numbers,
            received,
            conv_weight,
            conv_bias,
            norm_gain,
            *staged,
        ],
        [
            pltpu.VMEM((device_count, rows_dev, heads_dev * row_width + 128), jnp.float32),
            pltpu.VMEM((REQS, live_rows + 8, heads_dev * row_width), jnp.float32),
            pltpu.VMEM((REQS, live_rows, 128), jnp.float32),
            pltpu.VMEM((live_rows + 8, channels), jnp.float32),
            pltpu.VMEM((device_count, rows_dev, heads_dev * HEAD_DIM), jnp.float32),
            pltpu.VMEM((HEAD_DIM, STATE), jnp.float32),
            pltpu.VMEM(received.shape, jnp.float32),
            pltpu.SMEM((device_count,), jnp.int32),
            pltpu.SMEM((device_count,), jnp.int32),
        ],
        "mixer",
        flops=1 << 30,
        smem=3,
    )

    theirs = other_core(theirs, chip_count)
    width = out_weight.shape[1]
    total_rows = chip_count * rows_dev
    block = jax.ShapeDtypeStruct((rows_dev, width), jnp.bfloat16)
    part = kernel_call(
        part_kernel,
        jax.ShapeDtypeStruct((total_rows, width), jnp.float32),
        [mine, out_weight],
        [],
        "sums_part",
        flops=1 << 30,
    )
    first, second = kernel_call(
        functools.partial(first_kernel, rows_dev),
        [block, block],
        [part, theirs, held],
        [],
        "sums_first",
        flops=1 << 30,
    )
    own_sum = stream(first, chip_count)
    other_sum = stream(second, chip_count)
    shares = kernel_call(
        functools.partial(rest_kernel, rows_dev),
        jax.ShapeDtypeStruct((total_rows - 2 * rows_dev, width), jnp.float32),
        [part, theirs, held],
        [],
        "sums_rest",
        flops=1 << 30,
    )

    def onward(at, *arrived):
        top = (at - 2) * rows_dev
        return kernel_call(
            functools.partial(add_kernel, top), block, [shares, *arrived], [], "onward"
        )

    slots = send_slots(half)
    for at in range(2, len(slots) - 1):
        if slots[at][1] == 0:
            own_sum = stream(onward(at, own_sum), chip_count)
        else:
            other_sum = stream(onward(at, other_sum), chip_count)
    crossed = other_core(other_sum, chip_count)
    mixed = onward(len(slots) - 1, own_sum, crossed)
    return (mixed, final_state, final_conv)


def solution(mesh):
    return jax.shard_map(
        body,
        mesh=mesh,
        in_specs=(
            P(("groups", "dp"), None),
            P(None, "dp"),
            P("dp", None),
            P("dp"),
            P("dp"),
            P(None, "dp"),
            P("dp"),
            P("dp"),
            P("dp"),
            P("dp", None),
            P(("groups", "dp"), None, None),
            P(("groups", "dp"), None, None),
            P("groups", None, None),
            P("groups"),
            P("groups"),
        ),
        out_specs=(
            P(("groups", "dp"), None),
            P("groups", "dp", None, None),
            P("groups", None, "dp"),
        ),
        check_vma=False,
    )
```

```python
import functools

import jax
import jax.numpy as jnp
from jax import lax
from jax.experimental import pallas as pl
from jax.experimental.pallas import tpu as pltpu
from jax.sharding import PartitionSpec as P

HEAD_DIM = 128
STATE = 128
CONV = 4
REQS = 2
SPAN = 192
BLK = 64


EPSILON = 1e-05
PER_PEER = 2
VMEM_LIMIT = 16 * 1024 * 1024
VMEM_ALL = 60 * 1024 * 1024


def folded(chip_count):
    return chip_count <= 8


def chip_at(place, chip_count):
    if not folded(chip_count):
        return place
    back = 2 * (chip_count - 1 - place) + 1
    if isinstance(place, int):
        return 2 * place if place < chip_count // 2 else back
    return jnp.where(place < chip_count // 2, 2 * place, back)


def place_of(chip, chip_count):
    if not folded(chip_count):
        return chip
    return jnp.where(chip % 2 == 0, chip // 2, chip_count - 1 - chip // 2)


def stream(array, chip_count):
    pairs = []
    for place in range(chip_count):
        for core in range(2):
            onto = (place + 1 - 2 * core) % chip_count
            pairs.append((2 * chip_at(place, chip_count) + core, 2 * chip_at(onto, chip_count) + core))
    return lax.ppermute(array, "dp", pairs)


def stream_other(array, chip_count):
    pairs = []
    for place in range(chip_count):
        for core in range(2):
            onto = (place + 1 - 2 * core) % chip_count
            pairs.append(
                (2 * chip_at(place, chip_count) + 1 - core, 2 * chip_at(onto, chip_count) + core)
            )
    return lax.ppermute(array, "dp", pairs)


def other_core(array, chip_count):
    return lax.ppermute(array, "dp", [(d, d ^ 1) for d in range(2 * chip_count)])


def kernel_call(kernel, outs, operands, scratch, name, flops=0, smem=0, limit=VMEM_LIMIT):
    several = isinstance(outs, list)
    whole = pl.BlockSpec(memory_space=pltpu.VMEM)
    scalars = pl.BlockSpec(memory_space=pltpu.SMEM)
    return pl.pallas_call(
        kernel,
        out_shape=outs,
        in_specs=[scalars] * smem + [whole] * (len(operands) - smem),
        out_specs=[whole] * len(outs) if several else whole,
        scratch_shapes=scratch,
        compiler_params=pltpu.CompilerParams(vmem_limit_bytes=limit),
        cost_estimate=pl.CostEstimate(flops=flops, bytes_accessed=8 << 20, transcendentals=0),
        name=name,
    )(*operands)


def offer_kernel(entries, my_ref, ids_ref, state_ref, conv_ref, out_ref, slot_s, conv_s, lag_s):
    pool_slots, state_rows, _ = state_ref.shape
    lag_rows = conv_ref.shape[0]
    piece_channels = conv_ref.shape[2]
    receivers = out_ref.shape[0]
    heads_dev = ids_ref.shape[2] // receivers
    first = my_ref[0] * pool_slots
    conv_s[...] = jnp.zeros_like(conv_s)
    conv_s[:, :, :piece_channels] = conv_ref[...].astype(jnp.float32)
    lag_s[...] = jnp.zeros_like(lag_s)

    def one_receiver(receiver, _):
        used = jnp.int32(0)
        for r in range(REQS):
            for h in range(heads_dev):
                for p in range(ids_ref.shape[1]):
                    slot = ids_ref[r, p, receiver * heads_dev + h] - first
                    slot_s[used] = slot
                    held = jnp.logical_and(slot >= 0, slot < pool_slots)
                    used = used + held.astype(jnp.int32)
        for place in range(PER_PEER):
            slot = jnp.clip(slot_s[place], 0, pool_slots - 1)
            out_ref[receiver, place * state_rows : (place + 1) * state_rows, :] = state_ref[slot]
            for lag in range(lag_rows):
                row = 8 * place + lag
                lag_s[receiver, row : row + 1, :] = conv_s[lag, pl.ds(slot, 1), :]
        return 0

    lax.fori_loop(0, receivers, one_receiver, 0)
    out_ref[:, PER_PEER * state_rows :, :] = lag_s[...].astype(out_ref.dtype)


def column_tiles(width, body):
    tile = min(512, width)

    def one_tile(index, _):
        body(pl.ds(pl.multiple_of(index * tile, tile), tile))
        return 0

    lax.fori_loop(0, width // tile, one_tile, 0)


def from_hbm(array):
    return pltpu.with_memory_space_constraint(array, pltpu.HBM)


def load_kernel(*refs):
    count = (len(refs) - 1) // 2
    sems = refs[-1]
    copies = [
        pltpu.make_async_copy(refs[at], refs[count + at], sems.at[at]) for at in range(count)
    ]
    for copy in copies:
        copy.start()
    for copy in copies:
        copy.wait()


def load(*arrays):
    return pl.pallas_call(
        load_kernel,
        out_shape=[jax.ShapeDtypeStruct(a.shape, a.dtype) for a in arrays],
        in_specs=[pl.BlockSpec(memory_space=pltpu.HBM)] * len(arrays),
        out_specs=[pl.BlockSpec(memory_space=pltpu.VMEM)] * len(arrays),
        scratch_shapes=[pltpu.SemaphoreType.DMA((len(arrays),))],
        compiler_params=pltpu.CompilerParams(vmem_limit_bytes=VMEM_LIMIT),
        cost_estimate=pl.CostEstimate(flops=0, bytes_accessed=8 << 20, transcendentals=0),
        name="load",
    )(*[from_hbm(a) for a in arrays])


def stage_kernel(count, *refs):
    block_refs = refs[:count]
    weight_ref, rate_weight_ref, out_ref, joined_s = refs[count:]
    rows = block_refs[0].shape[0]
    width = weight_ref.shape[1]
    for at, block_ref in enumerate(block_refs):
        joined_s[at * rows : (at + 1) * rows, :] = block_ref[...]
    rates = rate_weight_ref.shape[0]
    out_ref[:, width:] = jnp.zeros((out_ref.shape[0], out_ref.shape[1] - width), jnp.float32)
    out_ref[:, width : width + rates] = lax.dot_general(
        joined_s[...],
        rate_weight_ref[...],
        (((1,), (1,)), ((), ())),
        preferred_element_type=jnp.float32,
    )

    def body(columns):
        out_ref[:, columns] = jnp.dot(
            joined_s[...], weight_ref[:, columns], preferred_element_type=jnp.float32
        )

    column_tiles(width, body)


def stage(blocks, weight, rate_weight):
    rows, depth = blocks[0].shape
    total = rows * len(blocks)
    width = weight.shape[1] + 128
    return kernel_call(
        functools.partial(stage_kernel, len(blocks)),
        jax.ShapeDtypeStruct((total, width), jnp.float32),
        [*blocks, weight, rate_weight],
        [pltpu.VMEM((total, depth), jnp.bfloat16)],
        "stage",
        flops=2 * 256 * depth * width,
    )


def part_kernel(mine_ref, weight_ref, out_ref):
    def body(columns):
        out_ref[:, columns] = jnp.dot(
            mine_ref[...], weight_ref[:, columns], preferred_element_type=jnp.float32
        )

    column_tiles(out_ref.shape[1], body)


def first_kernel(rows, part_ref, theirs_ref, held_ref, first_ref, second_ref):
    def body(columns):
        total = part_ref[: 2 * rows, columns] + jnp.dot(
            theirs_ref[: 2 * rows, :], held_ref[:, columns], preferred_element_type=jnp.float32
        )
        first_ref[:, columns] = total[:rows].astype(first_ref.dtype)
        second_ref[:, columns] = total[rows:].astype(second_ref.dtype)

    column_tiles(held_ref.shape[1], body)


def rest_kernel(rows, part_ref, theirs_ref, held_ref, out_ref):
    def body(columns):
        out_ref[:, columns] = part_ref[2 * rows :, columns] + jnp.dot(
            theirs_ref[2 * rows :, :], held_ref[:, columns], preferred_element_type=jnp.float32
        )

    column_tiles(held_ref.shape[1], body)


def add_kernel(top, share_ref, *refs):
    out_ref = refs[-1]
    total = share_ref[top : top + out_ref.shape[0], :]
    for arrived_ref in refs[:-1]:
        total = total + arrived_ref[...].astype(jnp.float32)
    out_ref[...] = total.astype(out_ref.dtype)


def gather_slots(half):
    slots = [(0, 0), (0, 1)]
    for step in range(1, half):
        slots += [(-step, 0), (-step, 1), (step, 1), (step, 0)]
    return slots + [(-half, 0), (half, 1)]


def send_slots(half):
    slots = []
    for step in range(half, 0, -1):
        slots.append((step, 0))
        if step > 1:
            slots.append((step - 1, 1))
    return slots + [(0, 0)]


def mix_kernel(sizes, scalar_ref, page_id_ref, number_ref, page_ref, *rest):
    heads_dev, piece_count, pool_slots, stages = sizes
    taps_ref, conv_bias_ref, gain_ref = rest[:3]
    stage_refs, rest = rest[3 : 3 + stages], rest[3 + stages :]
    conv_bias = conv_bias_ref[...].astype(jnp.float32).reshape(1, -1)
    gains = gain_ref[...].astype(jnp.float32).reshape(1, -1)
    state_ref, conv_ref, mine_ref, theirs_ref = rest[:4]
    placed_s, rows_s, rate_s, input_s, normed_s, initial_s, page_s, inverse_s, used_s = rest[4:]
    blocks, rows_dev, _ = placed_s.shape
    live_rows = SPAN - BLK
    lead = 8
    state_rows = HEAD_DIM // piece_count
    channels = HEAD_DIM + 2 * STATE
    row_width = HEAD_DIM + channels
    piece_channels = channels // piece_count
    blocks_req = blocks // REQS

    chip_count = blocks // 2
    half = chip_count // 2
    my_index = scalar_ref[0]
    core = my_index % 2
    place = place_of(my_index // 2, chip_count)
    owner_at = 1 + REQS

    def device_at(distance, flip):
        onto = place + jnp.where(core == 0, distance, -distance) + chip_count
        chip = chip_at(lax.rem(onto, chip_count), chip_count)
        return 2 * chip + (core if flip == 0 else 1 - core)

    def clear(holder, _):
        used_s[holder] = 0
        return 0

    lax.fori_loop(0, blocks, clear, 0)

    def invert(block, _):
        inverse_s[scalar_ref[owner_at + block]] = block
        return 0

    lax.fori_loop(0, blocks, invert, 0)

    page_s[...] = page_ref[...].astype(jnp.float32)

    pieces_of = []
    for r in range(REQS):
        for j in range(blocks_req):
            start = j * rows_dev
            low, high = max(start, BLK), start + rows_dev
            if high > BLK:
                pieces_of.append((r, r * blocks_req + j, low - start, low - BLK, high - BLK))
    slots = gather_slots(half)
    at = 0
    for stage_ref in stage_refs:
        for top in range(0, stage_ref.shape[0], rows_dev):
            placed_s[device_at(*slots[at])] = stage_ref[top : top + rows_dev, :]
            at += 1
    for r, block, skipped, low, high in pieces_of:
        rows_s[r, lead + low : lead + high, :] = placed_s[block, skipped:, : rows_s.shape[2]]
        rate_s[r, low:high, :] = placed_s[block, skipped:, rows_s.shape[2] :]
    normed_s[...] = jnp.zeros_like(normed_s)

    wide = (live_rows, 128)
    later = lax.broadcasted_iota(jnp.int32, (live_rows, live_rows), 0)
    sooner = lax.broadcasted_iota(jnp.int32, (live_rows, live_rows), 1)
    causal = later >= sooner
    ones = causal.astype(jnp.float32)
    position = lax.broadcasted_iota(jnp.int32, wide, 0) + BLK
    lead_position = lax.broadcasted_iota(jnp.int32, (live_rows + lead, channels), 0) + BLK - lead
    spread_row = lax.broadcasted_iota(jnp.int32, (piece_count * 128, channels), 0)
    spread_col = lax.broadcasted_iota(jnp.int32, (piece_count * 128, channels), 1)
    spread = (
        ((spread_row // 128) * piece_channels + spread_row % 128 == spread_col)
        & (spread_row % 128 < piece_channels)
    ).astype(jnp.bfloat16)

    lane = lax.broadcasted_iota(jnp.int32, (1, 128), 1)
    bias_lanes = jnp.zeros((1, 128), jnp.float32)
    decay_lanes = jnp.zeros((1, 128), jnp.float32)
    for h in range(heads_dev):
        bias_lanes = jnp.where(lane == h, number_ref[h], bias_lanes)
        decay_lanes = jnp.where(lane == h, number_ref[heads_dev + h], decay_lanes)

    for r in range(REQS):
        live_start = scalar_ref[1 + r] * BLK
        live = position >= live_start
        rate = rate_s[r] + bias_lanes
        step = jnp.where(live, jax.nn.softplus(rate), 0.0)
        drop = -decay_lanes * step
        total = jnp.dot(
            ones, drop, preferred_element_type=jnp.float32, precision=lax.Precision.HIGHEST
        )
        total_t = total.T
        step_t = step.T
        from_start = jnp.exp(total)
        span_tail = total[live_rows - 1 : live_rows, :]
        to_end = jnp.exp(span_tail - total) * step
        kept = jnp.exp(span_tail)
        for h in range(heads_dev):
            lags = []
            for p in range(piece_count):
                page = page_id_ref[r, p, my_index * heads_dev + h]
                holder = lax.div(page, pool_slots)
                rank = used_s[holder]
                used_s[holder] = rank + 1
                state_at = pl.ds(pl.multiple_of(rank * state_rows, state_rows), state_rows)
                lag_at = pl.ds(pl.multiple_of(PER_PEER * state_rows + 8 * rank, 8), 8)
                initial_s[p * state_rows : (p + 1) * state_rows, :] = page_s[holder, state_at, :]
                lags.append(page_s[holder, lag_at, :].astype(jnp.bfloat16))
            initial = initial_s[...]
            lag_lanes = jnp.concatenate(lags, axis=1)
            cached = jnp.dot(lag_lanes, spread, preferred_element_type=jnp.float32)
            first = h * row_width
            c0 = h * channels
            raw = rows_s[r, :, first + HEAD_DIM : first + row_width]
            raw = raw.astype(jnp.bfloat16).astype(jnp.float32)
            inputs = jnp.where(lead_position >= live_start, raw, 0.0)
            for lag in range(CONV - 1):
                inputs = jnp.where(
                    lead_position == live_start - (CONV - 1) + lag,
                    cached[lag : lag + 1, :],
                    inputs,
                )
            input_s[...] = inputs
            conv_ref[r, :, c0 : c0 + channels] = rows_s[
                r,
                live_rows + lead - (CONV - 1) : live_rows + lead,
                first + HEAD_DIM : first + row_width,
            ].astype(jnp.bfloat16)
            summed = jnp.broadcast_to(
                conv_bias[:, c0 : c0 + channels], (live_rows, channels)
            )
            for tap in range(CONV):
                begin = lead - (CONV - 1) + tap
                summed = summed + taps_ref[tap : tap + 1, c0 : c0 + channels].astype(
                    jnp.float32
                ) * input_s[begin : begin + live_rows, :]
            mixed_in = (summed * jax.nn.sigmoid(summed)).astype(jnp.bfloat16)
            x_part = mixed_in[:, :HEAD_DIM]
            b_part = mixed_in[:, HEAD_DIM : HEAD_DIM + STATE]
            c_part = mixed_in[:, HEAD_DIM + STATE :]
            x_float = x_part.astype(jnp.float32)
            last = (((1,), (1,)), ((), ()))
            scores = lax.dot_general(c_part, b_part, last, preferred_element_type=jnp.float32)
            gaps = jnp.where(causal, total[:, h : h + 1] - total_t[h : h + 1, :], 0.0)
            weights = jnp.where(causal, jnp.exp(gaps) * scores * step_t[h : h + 1, :], 0.0)
            outputs = jnp.dot(
                weights.astype(jnp.bfloat16), x_part, preferred_element_type=jnp.float32
            )
            reader = (c_part.astype(jnp.float32) * from_start[:, h : h + 1]).astype(jnp.bfloat16)
            outputs = outputs + lax.dot_general(
                reader, initial.astype(jnp.bfloat16), last, preferred_element_type=jnp.float32
            )
            outputs = outputs + number_ref[2 * heads_dev + h] * x_float
            entering = (x_float * to_end[:, h : h + 1]).astype(jnp.bfloat16)
            added = lax.dot_general(
                entering,
                b_part,
                (((0,), (0,)), ((), ())),
                preferred_element_type=jnp.float32,
            )
            state_ref[r, h] = kept[:, h : h + 1] * initial + added
            gate = rows_s[r, lead:, first : first + HEAD_DIM]
            gate = gate.astype(jnp.bfloat16).astype(jnp.float32)
            gated = outputs * (gate * jax.nn.sigmoid(gate))
            scale = lax.rsqrt(jnp.mean(gated * gated, axis=1, keepdims=True) + EPSILON)
            gain = gains[:, h * HEAD_DIM : (h + 1) * HEAD_DIM]
            normed = jnp.where(live, gated * scale * gain, 0.0)
            for rr, block, skipped, low, high in pieces_of:
                if rr == r:
                    normed_s[block, skipped:, h * HEAD_DIM : (h + 1) * HEAD_DIM] = normed[low:high]

    for at, (distance, flip) in enumerate(send_slots(half)):
        rows = slice(at * rows_dev, (at + 1) * rows_dev)
        mine_ref[rows, :] = normed_s[inverse_s[device_at(distance, flip)]].astype(jnp.bfloat16)
        theirs_ref[rows, :] = normed_s[inverse_s[device_at(-distance, 1 - flip)]].astype(
            jnp.bfloat16
        )


def body(
    hidden,
    in_weight,
    dt_weight,
    dt_bias,
    decay_rate,
    conv_weight,
    conv_bias,
    skip,
    norm_gain,
    out_weight,
    state_pool,
    conv_pool,
    hit_page,
    prefix_blocks,
    owners,
):
    device_count = lax.axis_size("dp")
    my_index = lax.axis_index("dp").astype(jnp.int32).reshape(1)
    heads_dev = dt_weight.shape[0]
    piece_count = hit_page.shape[2]
    row_width = 2 * HEAD_DIM + 2 * STATE
    channels = HEAD_DIM + 2 * STATE
    rows_dev = hidden.shape[0]
    pool_slots, state_rows, _ = state_pool.shape
    chip_count = device_count // 2
    half = chip_count // 2
    page_ids = jnp.swapaxes(hit_page, 1, 2)

    other_type = other_core(hidden, chip_count)
    page_rows = PER_PEER * state_rows + 8 * PER_PEER
    entries = REQS * heads_dev * piece_count
    offered = kernel_call(
        functools.partial(offer_kernel, entries),
        jax.ShapeDtypeStruct((device_count, page_rows, STATE), state_pool.dtype),
        [
            my_index,
            page_ids,
            from_hbm(state_pool),
            from_hbm(jnp.swapaxes(conv_pool, 0, 1)),
        ],
        [
            pltpu.SMEM((entries + 1,), jnp.int32),
            pltpu.VMEM((CONV - 1, pool_slots, STATE), jnp.float32),
            pltpu.VMEM((device_count, 8 * PER_PEER, STATE), jnp.float32),
        ],
        "offer_pages",
        smem=2,
        limit=VMEM_ALL,
    )
    own_type = stream(hidden, chip_count)
    first_other = other_type
    other_type = stream_other(hidden, chip_count)
    scalars = jnp.concatenate([my_index, prefix_blocks, owners])
    numbers = jnp.concatenate([dt_bias, decay_rate, skip])
    offered, own_type, other_type, scalars, numbers, held = lax.optimization_barrier(
        (offered, own_type, other_type, scalars, numbers, out_weight)
    )
    received = lax.all_to_all(offered, "dp", split_axis=0, concat_axis=0, tiled=True)
    held = other_core(held, chip_count)
    staged = []
    pending = []
    for step in range(1, half):
        if step > 1:
            own_type = stream(own_type, chip_count)
            other_type = stream(other_type, chip_count)
        crossed = other_core(own_type, chip_count)
        if step == 1:
            received, own_here, weight_here, rates_here, crossed = lax.optimization_barrier(
                (received, hidden, in_weight, dt_weight, crossed)
            )
            own_here, weight_here, rates_here = load(own_here, weight_here, rates_here)
            pending = [own_here, first_other]
        pending += [own_type, other_type, crossed, other_core(other_type, chip_count)]
        if len(pending) >= 6 or step == half - 1:
            staged.append(stage(pending, weight_here, rates_here))
            pending = []
    own_type = stream(own_type, chip_count)
    last = [own_type, other_core(own_type, chip_count)]
    staged.append(stage(last, weight_here, rates_here))

    live_rows = SPAN - BLK
    normed_rows = jax.ShapeDtypeStruct((chip_count * rows_dev, heads_dev * HEAD_DIM), jnp.bfloat16)
    final_state, final_conv, mine, theirs = kernel_call(
        functools.partial(mix_kernel, (heads_dev, piece_count, pool_slots, len(staged))),
        [
            jax.ShapeDtypeStruct((REQS, heads_dev, HEAD_DIM, STATE), jnp.float32),
            jax.ShapeDtypeStruct((REQS, CONV - 1, heads_dev * channels), jnp.bfloat16),
            normed_rows,
            normed_rows,
        ],
        [
            scalars,
            page_ids,
            numbers,
            received,
            conv_weight,
            conv_bias,
            norm_gain,
            *staged,
        ],
        [
            pltpu.VMEM((device_count, rows_dev, heads_dev * row_width + 128), jnp.float32),
            pltpu.VMEM((REQS, live_rows + 8, heads_dev * row_width), jnp.float32),
            pltpu.VMEM((REQS, live_rows, 128), jnp.float32),
            pltpu.VMEM((live_rows + 8, channels), jnp.float32),
            pltpu.VMEM((device_count, rows_dev, heads_dev * HEAD_DIM), jnp.float32),
            pltpu.VMEM((HEAD_DIM, STATE), jnp.float32),
            pltpu.VMEM(received.shape, jnp.float32),
            pltpu.SMEM((device_count,), jnp.int32),
            pltpu.SMEM((device_count,), jnp.int32),
        ],
        "mixer",
        flops=1 << 30,
        smem=3,
    )

    theirs = other_core(theirs, chip_count)
    width = out_weight.shape[1]
    total_rows = chip_count * rows_dev
    block = jax.ShapeDtypeStruct((rows_dev, width), jnp.bfloat16)
    part = kernel_call(
        part_kernel,
        jax.ShapeDtypeStruct((total_rows, width), jnp.float32),
        [mine, out_weight],
        [],
        "sums_part",
        flops=1 << 30,
    )
    first, second = kernel_call(
        functools.partial(first_kernel, rows_dev),
        [block, block],
        [part, theirs, held],
        [],
        "sums_first",
        flops=1 << 30,
    )
    own_sum = stream(first, chip_count)
    other_sum = stream(second, chip_count)
    shares = kernel_call(
        functools.partial(rest_kernel, rows_dev),
        jax.ShapeDtypeStruct((total_rows - 2 * rows_dev, width), jnp.float32),
        [part, theirs, held],
        [],
        "sums_rest",
        flops=1 << 30,
    )

    def onward(at, *arrived):
        top = (at - 2) * rows_dev
        return kernel_call(
            functools.partial(add_kernel, top), block, [shares, *arrived], [], "onward"
        )

    slots = send_slots(half)
    for at in range(2, len(slots) - 1):
        if slots[at][1] == 0:
            own_sum = stream(onward(at, own_sum), chip_count)
        else:
            other_sum = stream(onward(at, other_sum), chip_count)
    crossed = other_core(other_sum, chip_count)
    mixed = onward(len(slots) - 1, own_sum, crossed)
    return (mixed, final_state, final_conv)


def solution(mesh):
    return jax.shard_map(
        body,
        mesh=mesh,
        in_specs=(
            P(("groups", "dp"), None),
            P(None, "dp"),
            P("dp", None),
            P("dp"),
            P("dp"),
            P(None, "dp"),
            P("dp"),
            P("dp"),
            P("dp"),
            P("dp", None),
            P(("groups", "dp"), None, None),
            P(("groups", "dp"), None, None),
            P("groups", None, None),
            P("groups"),
            P("groups"),
        ),
        out_specs=(
            P(("groups", "dp"), None),
            P("groups", "dp", None, None),
            P("groups", None, "dp"),
        ),
        check_vma=False,
    )
```

```python
import functools

import jax
import jax.numpy as jnp
from jax import lax
from jax.experimental import pallas as pl
from jax.experimental.pallas import tpu as pltpu
from jax.sharding import PartitionSpec as P

HEAD_DIM = 128
STATE = 128
CONV = 4
REQS = 2
SPAN = 192
BLK = 64


EPSILON = 1e-05
PER_PEER = 2
VMEM_LIMIT = 16 * 1024 * 1024
VMEM_ALL = 60 * 1024 * 1024


def folded(chip_count):
    return chip_count <= 8


def chip_at(place, chip_count):
    if not folded(chip_count):
        return place
    back = 2 * (chip_count - 1 - place) + 1
    if isinstance(place, int):
        return 2 * place if place < chip_count // 2 else back
    return jnp.where(place < chip_count // 2, 2 * place, back)


def place_of(chip, chip_count):
    if not folded(chip_count):
        return chip
    return jnp.where(chip % 2 == 0, chip // 2, chip_count - 1 - chip // 2)


def stream(array, chip_count):
    pairs = []
    for place in range(chip_count):
        for core in range(2):
            onto = (place + 1 - 2 * core) % chip_count
            pairs.append((2 * chip_at(place, chip_count) + core, 2 * chip_at(onto, chip_count) + core))
    return lax.ppermute(array, "dp", pairs)


def stream_other(array, chip_count):
    pairs = []
    for place in range(chip_count):
        for core in range(2):
            onto = (place + 1 - 2 * core) % chip_count
            pairs.append(
                (2 * chip_at(place, chip_count) + 1 - core, 2 * chip_at(onto, chip_count) + core)
            )
    return lax.ppermute(array, "dp", pairs)


def other_core(array, chip_count):
    return lax.ppermute(array, "dp", [(d, d ^ 1) for d in range(2 * chip_count)])


def kernel_call(kernel, outs, operands, scratch, name, flops=0, smem=0, limit=VMEM_LIMIT):
    several = isinstance(outs, list)
    whole = pl.BlockSpec(memory_space=pltpu.VMEM)
    scalars = pl.BlockSpec(memory_space=pltpu.SMEM)
    return pl.pallas_call(
        kernel,
        out_shape=outs,
        in_specs=[scalars] * smem + [whole] * (len(operands) - smem),
        out_specs=[whole] * len(outs) if several else whole,
        scratch_shapes=scratch,
        compiler_params=pltpu.CompilerParams(vmem_limit_bytes=limit),
        cost_estimate=pl.CostEstimate(flops=flops, bytes_accessed=8 << 20, transcendentals=0),
        name=name,
    )(*operands)


def offer_kernel(entries, my_ref, ids_ref, state_ref, conv_ref, out_ref, slot_s, conv_s, lag_s):
    pool_slots, state_rows, _ = state_ref.shape
    lag_rows = conv_ref.shape[0]
    piece_channels = conv_ref.shape[2]
    receivers = out_ref.shape[0]
    heads_dev = ids_ref.shape[2] // receivers
    first = my_ref[0] * pool_slots
    conv_s[...] = jnp.zeros_like(conv_s)
    conv_s[:, :, :piece_channels] = conv_ref[...].astype(jnp.float32)
    lag_s[...] = jnp.zeros_like(lag_s)

    def one_receiver(receiver, _):
        used = jnp.int32(0)
        for r in range(REQS):
            for h in range(heads_dev):
                for p in range(ids_ref.shape[1]):
                    slot = ids_ref[r, p, receiver * heads_dev + h] - first
                    slot_s[used] = slot
                    held = jnp.logical_and(slot >= 0, slot < pool_slots)
                    used = used + held.astype(jnp.int32)
        for place in range(PER_PEER):
            slot = jnp.clip(slot_s[place], 0, pool_slots - 1)
            out_ref[receiver, place * state_rows : (place + 1) * state_rows, :] = state_ref[slot]
            for lag in range(lag_rows):
                row = 8 * place + lag
                lag_s[receiver, row : row + 1, :] = conv_s[lag, pl.ds(slot, 1), :]
        return 0

    lax.fori_loop(0, receivers, one_receiver, 0)
    out_ref[:, PER_PEER * state_rows :, :] = lag_s[...].astype(out_ref.dtype)


def column_tiles(width, body):
    tile = min(512, width)

    def one_tile(index, _):
        body(pl.ds(pl.multiple_of(index * tile, tile), tile))
        return 0

    lax.fori_loop(0, width // tile, one_tile, 0)


def from_hbm(array):
    return pltpu.with_memory_space_constraint(array, pltpu.HBM)


def load_kernel(*refs):
    count = (len(refs) - 1) // 2
    sems = refs[-1]
    copies = [
        pltpu.make_async_copy(refs[at], refs[count + at], sems.at[at]) for at in range(count)
    ]
    for copy in copies:
        copy.start()
    for copy in copies:
        copy.wait()


def load(*arrays):
    return pl.pallas_call(
        load_kernel,
        out_shape=[jax.ShapeDtypeStruct(a.shape, a.dtype) for a in arrays],
        in_specs=[pl.BlockSpec(memory_space=pltpu.HBM)] * len(arrays),
        out_specs=[pl.BlockSpec(memory_space=pltpu.VMEM)] * len(arrays),
        scratch_shapes=[pltpu.SemaphoreType.DMA((len(arrays),))],
        compiler_params=pltpu.CompilerParams(vmem_limit_bytes=VMEM_LIMIT),
        cost_estimate=pl.CostEstimate(flops=0, bytes_accessed=8 << 20, transcendentals=0),
        name="load",
    )(*[from_hbm(a) for a in arrays])


def stage_kernel(count, *refs):
    block_refs = refs[:count]
    weight_ref, rate_weight_ref, out_ref, joined_s = refs[count:]
    rows = block_refs[0].shape[0]
    width = weight_ref.shape[1]
    for at, block_ref in enumerate(block_refs):
        joined_s[at * rows : (at + 1) * rows, :] = block_ref[...]
    rates = rate_weight_ref.shape[0]
    out_ref[:, width:] = jnp.zeros((out_ref.shape[0], out_ref.shape[1] - width), jnp.float32)
    out_ref[:, width : width + rates] = lax.dot_general(
        joined_s[...],
        rate_weight_ref[...],
        (((1,), (1,)), ((), ())),
        preferred_element_type=jnp.float32,
    )

    def body(columns):
        out_ref[:, columns] = jnp.dot(
            joined_s[...], weight_ref[:, columns], preferred_element_type=jnp.float32
        )

    column_tiles(width, body)


def stage(blocks, weight, rate_weight):
    rows, depth = blocks[0].shape
    total = rows * len(blocks)
    width = weight.shape[1] + 128
    return kernel_call(
        functools.partial(stage_kernel, len(blocks)),
        jax.ShapeDtypeStruct((total, width), jnp.float32),
        [*blocks, weight, rate_weight],
        [pltpu.VMEM((total, depth), jnp.bfloat16)],
        "stage",
        flops=2 * 256 * depth * width,
    )


def early_kernel(count, tile, *refs):
    block_refs = refs[:count]
    weight_ref, rate_weight_ref, out_hbm, held_s, joined_s, out_ref, sems = refs[count:]
    rows = block_refs[0].shape[0]
    width = weight_ref.shape[1]
    lefts = range(0, width, tile)
    loads = [
        pltpu.make_async_copy(
            weight_ref.at[:, pl.ds(left, tile)], held_s.at[:, pl.ds(left, tile)], sems.at[at]
        )
        for at, left in enumerate(lefts)
    ]
    for copy in loads:
        copy.start()
    for at, block_ref in enumerate(block_refs):
        joined_s[at * rows : (at + 1) * rows, :] = block_ref[...]
    rates = rate_weight_ref.shape[0]
    out_ref[:, width:] = jnp.zeros((out_ref.shape[0], out_ref.shape[1] - width), jnp.float32)
    out_ref[:, width : width + rates] = lax.dot_general(
        joined_s[...],
        rate_weight_ref[...],
        (((1,), (1,)), ((), ())),
        preferred_element_type=jnp.float32,
    )
    for left, copy in zip(lefts, loads, strict=True):
        copy.wait()
        out_ref[:, left : left + tile] = jnp.dot(
            joined_s[...], held_s[:, left : left + tile], preferred_element_type=jnp.float32
        )
    store = pltpu.make_async_copy(out_ref, out_hbm, sems.at[len(loads)])
    store.start()
    store.wait()


def early_stage(blocks, weight, rate_weight):
    rows, depth = blocks[0].shape
    count = len(blocks)
    width = weight.shape[1]
    tile = min(256, width)
    whole = pl.BlockSpec(memory_space=pltpu.VMEM)
    hbm = pl.BlockSpec(memory_space=pltpu.HBM)
    return pl.pallas_call(
        functools.partial(early_kernel, count, tile),
        out_shape=jax.ShapeDtypeStruct((rows * count, width + 128), jnp.float32),
        in_specs=[whole] * count + [hbm, whole],
        out_specs=hbm,
        scratch_shapes=[
            pltpu.VMEM((depth, width), jnp.bfloat16),
            pltpu.VMEM((rows * count, depth), jnp.bfloat16),
            pltpu.VMEM((rows * count, width + 128), jnp.float32),
            pltpu.SemaphoreType.DMA((width // tile + 1,)),
        ],
        compiler_params=pltpu.CompilerParams(vmem_limit_bytes=VMEM_LIMIT),
        cost_estimate=pl.CostEstimate(
            flops=2 * 256 * depth * width, bytes_accessed=8 << 20, transcendentals=0
        ),
        name="early_stage",
    )(*blocks, from_hbm(weight), rate_weight)


def part_kernel(mine_ref, weight_ref, out_ref):
    def body(columns):
        out_ref[:, columns] = jnp.dot(
            mine_ref[...], weight_ref[:, columns], preferred_element_type=jnp.float32
        )

    column_tiles(out_ref.shape[1], body)


def first_kernel(rows, part_ref, theirs_ref, held_ref, first_ref, second_ref):
    def body(columns):
        total = part_ref[: 2 * rows, columns] + jnp.dot(
            theirs_ref[: 2 * rows, :], held_ref[:, columns], preferred_element_type=jnp.float32
        )
        first_ref[:, columns] = total[:rows].astype(first_ref.dtype)
        second_ref[:, columns] = total[rows:].astype(second_ref.dtype)

    column_tiles(held_ref.shape[1], body)


def rest_kernel(rows, part_ref, theirs_ref, held_ref, out_ref):
    def body(columns):
        out_ref[:, columns] = part_ref[2 * rows :, columns] + jnp.dot(
            theirs_ref[2 * rows :, :], held_ref[:, columns], preferred_element_type=jnp.float32
        )

    column_tiles(held_ref.shape[1], body)


def add_kernel(top, share_ref, *refs):
    out_ref = refs[-1]
    total = share_ref[top : top + out_ref.shape[0], :]
    for arrived_ref in refs[:-1]:
        total = total + arrived_ref[...].astype(jnp.float32)
    out_ref[...] = total.astype(out_ref.dtype)


def gather_slots(half):
    slots = [(0, 0), (0, 1)]
    for step in range(1, half):
        slots += [(-step, 0), (-step, 1), (step, 1), (step, 0)]
    return slots + [(-half, 0), (half, 1)]


def send_slots(half):
    slots = []
    for step in range(half, 0, -1):
        slots.append((step, 0))
        if step > 1:
            slots.append((step - 1, 1))
    return slots + [(0, 0)]


def mix_kernel(sizes, scalar_ref, page_id_ref, number_ref, page_ref, *rest):
    heads_dev, piece_count, pool_slots, stages = sizes
    taps_ref, conv_bias_ref, gain_ref = rest[:3]
    stage_refs, rest = rest[3 : 3 + stages], rest[3 + stages :]
    conv_bias = conv_bias_ref[...].astype(jnp.float32).reshape(1, -1)
    gains = gain_ref[...].astype(jnp.float32).reshape(1, -1)
    state_ref, conv_ref, mine_ref, theirs_ref = rest[:4]
    placed_s, rows_s, rate_s, input_s, normed_s, initial_s, page_s, inverse_s, used_s = rest[4:]
    blocks, rows_dev, _ = placed_s.shape
    live_rows = SPAN - BLK
    lead = 8
    state_rows = HEAD_DIM // piece_count
    channels = HEAD_DIM + 2 * STATE
    row_width = HEAD_DIM + channels
    piece_channels = channels // piece_count
    blocks_req = blocks // REQS

    chip_count = blocks // 2
    half = chip_count // 2
    my_index = scalar_ref[0]
    core = my_index % 2
    place = place_of(my_index // 2, chip_count)
    owner_at = 1 + REQS

    def device_at(distance, flip):
        onto = place + jnp.where(core == 0, distance, -distance) + chip_count
        chip = chip_at(lax.rem(onto, chip_count), chip_count)
        return 2 * chip + (core if flip == 0 else 1 - core)

    def clear(holder, _):
        used_s[holder] = 0
        return 0

    lax.fori_loop(0, blocks, clear, 0)

    def invert(block, _):
        inverse_s[scalar_ref[owner_at + block]] = block
        return 0

    lax.fori_loop(0, blocks, invert, 0)

    page_s[...] = page_ref[...].astype(jnp.float32)

    pieces_of = []
    for r in range(REQS):
        for j in range(blocks_req):
            start = j * rows_dev
            low, high = max(start, BLK), start + rows_dev
            if high > BLK:
                pieces_of.append((r, r * blocks_req + j, low - start, low - BLK, high - BLK))
    slots = gather_slots(half)
    at = 0
    for stage_ref in stage_refs:
        for top in range(0, stage_ref.shape[0], rows_dev):
            placed_s[device_at(*slots[at])] = stage_ref[top : top + rows_dev, :]
            at += 1
    for r, block, skipped, low, high in pieces_of:
        rows_s[r, lead + low : lead + high, :] = placed_s[block, skipped:, : rows_s.shape[2]]
        rate_s[r, low:high, :] = placed_s[block, skipped:, rows_s.shape[2] :]
    normed_s[...] = jnp.zeros_like(normed_s)

    wide = (live_rows, 128)
    later = lax.broadcasted_iota(jnp.int32, (live_rows, live_rows), 0)
    sooner = lax.broadcasted_iota(jnp.int32, (live_rows, live_rows), 1)
    causal = later >= sooner
    ones = causal.astype(jnp.float32)
    position = lax.broadcasted_iota(jnp.int32, wide, 0) + BLK
    lead_position = lax.broadcasted_iota(jnp.int32, (live_rows + lead, channels), 0) + BLK - lead
    spread_row = lax.broadcasted_iota(jnp.int32, (piece_count * 128, channels), 0)
    spread_col = lax.broadcasted_iota(jnp.int32, (piece_count * 128, channels), 1)
    spread = (
        ((spread_row // 128) * piece_channels + spread_row % 128 == spread_col)
        & (spread_row % 128 < piece_channels)
    ).astype(jnp.bfloat16)

    lane = lax.broadcasted_iota(jnp.int32, (1, 128), 1)
    bias_lanes = jnp.zeros((1, 128), jnp.float32)
    decay_lanes = jnp.zeros((1, 128), jnp.float32)
    for h in range(heads_dev):
        bias_lanes = jnp.where(lane == h, number_ref[h], bias_lanes)
        decay_lanes = jnp.where(lane == h, number_ref[heads_dev + h], decay_lanes)

    for r in range(REQS):
        live_start = scalar_ref[1 + r] * BLK
        live = position >= live_start
        rate = rate_s[r] + bias_lanes
        step = jnp.where(live, jax.nn.softplus(rate), 0.0)
        drop = -decay_lanes * step
        total = jnp.dot(
            ones, drop, preferred_element_type=jnp.float32, precision=lax.Precision.HIGHEST
        )
        total_t = total.T
        step_t = step.T
        from_start = jnp.exp(total)
        span_tail = total[live_rows - 1 : live_rows, :]
        to_end = jnp.exp(span_tail - total) * step
        kept = jnp.exp(span_tail)
        for h in range(heads_dev):
            lags = []
            for p in range(piece_count):
                page = page_id_ref[r, p, my_index * heads_dev + h]
                holder = lax.div(page, pool_slots)
                rank = used_s[holder]
                used_s[holder] = rank + 1
                state_at = pl.ds(pl.multiple_of(rank * state_rows, state_rows), state_rows)
                lag_at = pl.ds(pl.multiple_of(PER_PEER * state_rows + 8 * rank, 8), 8)
                initial_s[p * state_rows : (p + 1) * state_rows, :] = page_s[holder, state_at, :]
                lags.append(page_s[holder, lag_at, :].astype(jnp.bfloat16))
            initial = initial_s[...]
            lag_lanes = jnp.concatenate(lags, axis=1)
            cached = jnp.dot(lag_lanes, spread, preferred_element_type=jnp.float32)
            first = h * row_width
            c0 = h * channels
            raw = rows_s[r, :, first + HEAD_DIM : first + row_width]
            raw = raw.astype(jnp.bfloat16).astype(jnp.float32)
            inputs = jnp.where(lead_position >= live_start, raw, 0.0)
            for lag in range(CONV - 1):
                inputs = jnp.where(
                    lead_position == live_start - (CONV - 1) + lag,
                    cached[lag : lag + 1, :],
                    inputs,
                )
            input_s[...] = inputs
            conv_ref[r, :, c0 : c0 + channels] = rows_s[
                r,
                live_rows + lead - (CONV - 1) : live_rows + lead,
                first + HEAD_DIM : first + row_width,
            ].astype(jnp.bfloat16)
            summed = jnp.broadcast_to(
                conv_bias[:, c0 : c0 + channels], (live_rows, channels)
            )
            for tap in range(CONV):
                begin = lead - (CONV - 1) + tap
                summed = summed + taps_ref[tap : tap + 1, c0 : c0 + channels].astype(
                    jnp.float32
                ) * input_s[begin : begin + live_rows, :]
            mixed_in = (summed * jax.nn.sigmoid(summed)).astype(jnp.bfloat16)
            x_part = mixed_in[:, :HEAD_DIM]
            b_part = mixed_in[:, HEAD_DIM : HEAD_DIM + STATE]
            c_part = mixed_in[:, HEAD_DIM + STATE :]
            x_float = x_part.astype(jnp.float32)
            last = (((1,), (1,)), ((), ()))
            scores = lax.dot_general(c_part, b_part, last, preferred_element_type=jnp.float32)
            gaps = jnp.where(causal, total[:, h : h + 1] - total_t[h : h + 1, :], 0.0)
            weights = jnp.where(causal, jnp.exp(gaps) * scores * step_t[h : h + 1, :], 0.0)
            outputs = jnp.dot(
                weights.astype(jnp.bfloat16), x_part, preferred_element_type=jnp.float32
            )
            reader = (c_part.astype(jnp.float32) * from_start[:, h : h + 1]).astype(jnp.bfloat16)
            outputs = outputs + lax.dot_general(
                reader, initial.astype(jnp.bfloat16), last, preferred_element_type=jnp.float32
            )
            outputs = outputs + number_ref[2 * heads_dev + h] * x_float
            entering = (x_float * to_end[:, h : h + 1]).astype(jnp.bfloat16)
            added = lax.dot_general(
                entering,
                b_part,
                (((0,), (0,)), ((), ())),
                preferred_element_type=jnp.float32,
            )
            state_ref[r, h] = kept[:, h : h + 1] * initial + added
            gate = rows_s[r, lead:, first : first + HEAD_DIM]
            gate = gate.astype(jnp.bfloat16).astype(jnp.float32)
            gated = outputs * (gate * jax.nn.sigmoid(gate))
            scale = lax.rsqrt(jnp.mean(gated * gated, axis=1, keepdims=True) + EPSILON)
            gain = gains[:, h * HEAD_DIM : (h + 1) * HEAD_DIM]
            normed = jnp.where(live, gated * scale * gain, 0.0)
            for rr, block, skipped, low, high in pieces_of:
                if rr == r:
                    normed_s[block, skipped:, h * HEAD_DIM : (h + 1) * HEAD_DIM] = normed[low:high]

    for at, (distance, flip) in enumerate(send_slots(half)):
        rows = slice(at * rows_dev, (at + 1) * rows_dev)
        mine_ref[rows, :] = normed_s[inverse_s[device_at(distance, flip)]].astype(jnp.bfloat16)
        theirs_ref[rows, :] = normed_s[inverse_s[device_at(-distance, 1 - flip)]].astype(
            jnp.bfloat16
        )


def body(
    hidden,
    in_weight,
    dt_weight,
    dt_bias,
    decay_rate,
    conv_weight,
    conv_bias,
    skip,
    norm_gain,
    out_weight,
    state_pool,
    conv_pool,
    hit_page,
    prefix_blocks,
    owners,
):
    device_count = lax.axis_size("dp")
    my_index = lax.axis_index("dp").astype(jnp.int32).reshape(1)
    heads_dev = dt_weight.shape[0]
    piece_count = hit_page.shape[2]
    row_width = 2 * HEAD_DIM + 2 * STATE
    channels = HEAD_DIM + 2 * STATE
    rows_dev = hidden.shape[0]
    pool_slots, state_rows, _ = state_pool.shape
    chip_count = device_count // 2
    half = chip_count // 2
    page_ids = jnp.swapaxes(hit_page, 1, 2)

    other_type = other_core(hidden, chip_count)
    page_rows = PER_PEER * state_rows + 8 * PER_PEER
    entries = REQS * heads_dev * piece_count
    offered = kernel_call(
        functools.partial(offer_kernel, entries),
        jax.ShapeDtypeStruct((device_count, page_rows, STATE), state_pool.dtype),
        [
            my_index,
            page_ids,
            from_hbm(state_pool),
            from_hbm(jnp.swapaxes(conv_pool, 0, 1)),
        ],
        [
            pltpu.SMEM((entries + 1,), jnp.int32),
            pltpu.VMEM((CONV - 1, pool_slots, STATE), jnp.float32),
            pltpu.VMEM((device_count, 8 * PER_PEER, STATE), jnp.float32),
        ],
        "offer_pages",
        smem=2,
        limit=VMEM_ALL,
    )
    own_type = stream(hidden, chip_count)
    first_other = other_type
    other_type = stream_other(hidden, chip_count)
    scalars = jnp.concatenate([my_index, prefix_blocks, owners])
    numbers = jnp.concatenate([dt_bias, decay_rate, skip])
    offered, own_type, other_type, scalars, numbers, held = lax.optimization_barrier(
        (offered, own_type, other_type, scalars, numbers, out_weight)
    )
    received = lax.all_to_all(offered, "dp", split_axis=0, concat_axis=0, tiled=True)
    held = other_core(held, chip_count)
    blocks = [from_hbm(hidden), first_other, own_type, other_type]
    blocks += [other_core(own_type, chip_count), other_core(other_type, chip_count)]
    early = early_stage(blocks, in_weight, from_hbm(dt_weight))
    pending = []
    for step in range(2, half):
        own_type = stream(own_type, chip_count)
        other_type = stream(other_type, chip_count)
        if step == 2:
            own_type, early = lax.optimization_barrier((own_type, early))
            staged = [from_hbm(early)]
        crossed = other_core(own_type, chip_count)
        if step == 2:
            received, weight_here, rates_here, crossed = lax.optimization_barrier(
                (received, in_weight, dt_weight, crossed)
            )
            weight_here, rates_here = load(weight_here, rates_here)
        pending += [own_type, other_type, crossed, other_core(other_type, chip_count)]
        if len(pending) >= 6 or step == half - 1:
            staged.append(stage(pending, weight_here, rates_here))
            pending = []
    own_type = stream(own_type, chip_count)
    last = [own_type, other_core(own_type, chip_count)]
    staged.append(stage(last, weight_here, rates_here))

    live_rows = SPAN - BLK
    normed_rows = jax.ShapeDtypeStruct((chip_count * rows_dev, heads_dev * HEAD_DIM), jnp.bfloat16)
    final_state, final_conv, mine, theirs = kernel_call(
        functools.partial(mix_kernel, (heads_dev, piece_count, pool_slots, len(staged))),
        [
            jax.ShapeDtypeStruct((REQS, heads_dev, HEAD_DIM, STATE), jnp.float32),
            jax.ShapeDtypeStruct((REQS, CONV - 1, heads_dev * channels), jnp.bfloat16),
            normed_rows,
            normed_rows,
        ],
        [
            scalars,
            page_ids,
            numbers,
            received,
            conv_weight,
            conv_bias,
            norm_gain,
            *staged,
        ],
        [
            pltpu.VMEM((device_count, rows_dev, heads_dev * row_width + 128), jnp.float32),
            pltpu.VMEM((REQS, live_rows + 8, heads_dev * row_width), jnp.float32),
            pltpu.VMEM((REQS, live_rows, 128), jnp.float32),
            pltpu.VMEM((live_rows + 8, channels), jnp.float32),
            pltpu.VMEM((device_count, rows_dev, heads_dev * HEAD_DIM), jnp.float32),
            pltpu.VMEM((HEAD_DIM, STATE), jnp.float32),
            pltpu.VMEM(received.shape, jnp.float32),
            pltpu.SMEM((device_count,), jnp.int32),
            pltpu.SMEM((device_count,), jnp.int32),
        ],
        "mixer",
        flops=1 << 30,
        smem=3,
    )

    theirs = other_core(theirs, chip_count)
    width = out_weight.shape[1]
    total_rows = chip_count * rows_dev
    block = jax.ShapeDtypeStruct((rows_dev, width), jnp.bfloat16)
    part = kernel_call(
        part_kernel,
        jax.ShapeDtypeStruct((total_rows, width), jnp.float32),
        [mine, out_weight],
        [],
        "sums_part",
        flops=1 << 30,
    )
    first, second = kernel_call(
        functools.partial(first_kernel, rows_dev),
        [block, block],
        [part, theirs, held],
        [],
        "sums_first",
        flops=1 << 30,
    )
    own_sum = stream(first, chip_count)
    other_sum = stream(second, chip_count)
    shares = kernel_call(
        functools.partial(rest_kernel, rows_dev),
        jax.ShapeDtypeStruct((total_rows - 2 * rows_dev, width), jnp.float32),
        [part, theirs, held],
        [],
        "sums_rest",
        flops=1 << 30,
    )

    def onward(at, *arrived):
        top = (at - 2) * rows_dev
        return kernel_call(
            functools.partial(add_kernel, top), block, [shares, *arrived], [], "onward"
        )

    slots = send_slots(half)
    for at in range(2, len(slots) - 1):
        if slots[at][1] == 0:
            own_sum = stream(onward(at, own_sum), chip_count)
        else:
            other_sum = stream(onward(at, other_sum), chip_count)
    crossed = other_core(other_sum, chip_count)
    mixed = onward(len(slots) - 1, own_sum, crossed)
    return (mixed, final_state, final_conv)


def solution(mesh):
    return jax.shard_map(
        body,
        mesh=mesh,
        in_specs=(
            P(("groups", "dp"), None),
            P(None, "dp"),
            P("dp", None),
            P("dp"),
            P("dp"),
            P(None, "dp"),
            P("dp"),
            P("dp"),
            P("dp"),
            P("dp", None),
            P(("groups", "dp"), None, None),
            P(("groups", "dp"), None, None),
            P("groups", None, None),
            P("groups"),
            P("groups"),
        ),
        out_specs=(
            P(("groups", "dp"), None),
            P("groups", "dp", None, None),
            P("groups", None, "dp"),
        ),
        check_vma=False,
    )
```

```python
import functools

import jax
import jax.numpy as jnp
from jax import lax
from jax.experimental import pallas as pl
from jax.experimental.pallas import tpu as pltpu
from jax.sharding import PartitionSpec as P

HEAD_DIM = 128
STATE = 128
CONV = 4
REQS = 2
SPAN = 192
BLK = 64


EPSILON = 1e-05
PER_PEER = 2
VMEM_LIMIT = 16 * 1024 * 1024
VMEM_ALL = 60 * 1024 * 1024


def folded(chip_count):
    return chip_count <= 8


def chip_at(place, chip_count):
    if not folded(chip_count):
        return place
    back = 2 * (chip_count - 1 - place) + 1
    if isinstance(place, int):
        return 2 * place if place < chip_count // 2 else back
    return jnp.where(place < chip_count // 2, 2 * place, back)


def place_of(chip, chip_count):
    if not folded(chip_count):
        return chip
    return jnp.where(chip % 2 == 0, chip // 2, chip_count - 1 - chip // 2)


def stream(array, chip_count):
    pairs = []
    for place in range(chip_count):
        for core in range(2):
            onto = (place + 1 - 2 * core) % chip_count
            pairs.append((2 * chip_at(place, chip_count) + core, 2 * chip_at(onto, chip_count) + core))
    return lax.ppermute(array, "dp", pairs)


def stream_other(array, chip_count):
    pairs = []
    for place in range(chip_count):
        for core in range(2):
            onto = (place + 1 - 2 * core) % chip_count
            pairs.append(
                (2 * chip_at(place, chip_count) + 1 - core, 2 * chip_at(onto, chip_count) + core)
            )
    return lax.ppermute(array, "dp", pairs)


def other_core(array, chip_count):
    return lax.ppermute(array, "dp", [(d, d ^ 1) for d in range(2 * chip_count)])


def kernel_call(kernel, outs, operands, scratch, name, flops=0, smem=0, limit=VMEM_LIMIT):
    several = isinstance(outs, list)
    whole = pl.BlockSpec(memory_space=pltpu.VMEM)
    scalars = pl.BlockSpec(memory_space=pltpu.SMEM)
    return pl.pallas_call(
        kernel,
        out_shape=outs,
        in_specs=[scalars] * smem + [whole] * (len(operands) - smem),
        out_specs=[whole] * len(outs) if several else whole,
        scratch_shapes=scratch,
        compiler_params=pltpu.CompilerParams(vmem_limit_bytes=limit),
        cost_estimate=pl.CostEstimate(flops=flops, bytes_accessed=8 << 20, transcendentals=0),
        name=name,
    )(*operands)


def offer_kernel(entries, my_ref, ids_ref, state_ref, conv_ref, out_ref, slot_s, conv_s, lag_s):
    pool_slots, state_rows, _ = state_ref.shape
    lag_rows = conv_ref.shape[0]
    piece_channels = conv_ref.shape[2]
    receivers = out_ref.shape[0]
    heads_dev = ids_ref.shape[2] // receivers
    first = my_ref[0] * pool_slots
    conv_s[...] = jnp.zeros_like(conv_s)
    conv_s[:, :, :piece_channels] = conv_ref[...].astype(jnp.float32)
    lag_s[...] = jnp.zeros_like(lag_s)

    def one_receiver(receiver, _):
        used = jnp.int32(0)
        for r in range(REQS):
            for h in range(heads_dev):
                for p in range(ids_ref.shape[1]):
                    slot = ids_ref[r, p, receiver * heads_dev + h] - first
                    slot_s[used] = slot
                    held = jnp.logical_and(slot >= 0, slot < pool_slots)
                    used = used + held.astype(jnp.int32)
        for place in range(PER_PEER):
            slot = jnp.clip(slot_s[place], 0, pool_slots - 1)
            out_ref[receiver, place * state_rows : (place + 1) * state_rows, :] = state_ref[slot]
            for lag in range(lag_rows):
                row = 8 * place + lag
                lag_s[receiver, row : row + 1, :] = conv_s[lag, pl.ds(slot, 1), :]
        return 0

    lax.fori_loop(0, receivers, one_receiver, 0)
    out_ref[:, PER_PEER * state_rows :, :] = lag_s[...].astype(out_ref.dtype)


def column_tiles(width, body):
    tile = min(512, width)

    def one_tile(index, _):
        body(pl.ds(pl.multiple_of(index * tile, tile), tile))
        return 0

    lax.fori_loop(0, width // tile, one_tile, 0)


def from_hbm(array):
    return pltpu.with_memory_space_constraint(array, pltpu.HBM)


def load_kernel(*refs):
    count = (len(refs) - 1) // 2
    sems = refs[-1]
    copies = [
        pltpu.make_async_copy(refs[at], refs[count + at], sems.at[at]) for at in range(count)
    ]
    for copy in copies:
        copy.start()
    for copy in copies:
        copy.wait()


def load(*arrays):
    return pl.pallas_call(
        load_kernel,
        out_shape=[jax.ShapeDtypeStruct(a.shape, a.dtype) for a in arrays],
        in_specs=[pl.BlockSpec(memory_space=pltpu.HBM)] * len(arrays),
        out_specs=[pl.BlockSpec(memory_space=pltpu.VMEM)] * len(arrays),
        scratch_shapes=[pltpu.SemaphoreType.DMA((len(arrays),))],
        compiler_params=pltpu.CompilerParams(vmem_limit_bytes=VMEM_LIMIT),
        cost_estimate=pl.CostEstimate(flops=0, bytes_accessed=8 << 20, transcendentals=0),
        name="load",
    )(*[from_hbm(a) for a in arrays])


def stage_kernel(count, *refs):
    block_refs = refs[:count]
    weight_ref, rate_weight_ref, out_ref, joined_s = refs[count:]
    rows = block_refs[0].shape[0]
    width = weight_ref.shape[1]
    for at, block_ref in enumerate(block_refs):
        joined_s[at * rows : (at + 1) * rows, :] = block_ref[...]
    rates = rate_weight_ref.shape[0]
    out_ref[:, width:] = jnp.zeros((out_ref.shape[0], out_ref.shape[1] - width), jnp.float32)
    out_ref[:, width : width + rates] = lax.dot_general(
        joined_s[...],
        rate_weight_ref[...],
        (((1,), (1,)), ((), ())),
        preferred_element_type=jnp.float32,
    )

    def body(columns):
        out_ref[:, columns] = jnp.dot(
            joined_s[...], weight_ref[:, columns], preferred_element_type=jnp.float32
        )

    column_tiles(width, body)


def stage(blocks, weight, rate_weight):
    rows, depth = blocks[0].shape
    total = rows * len(blocks)
    width = weight.shape[1] + 128
    return kernel_call(
        functools.partial(stage_kernel, len(blocks)),
        jax.ShapeDtypeStruct((total, width), jnp.float32),
        [*blocks, weight, rate_weight],
        [pltpu.VMEM((total, depth), jnp.bfloat16)],
        "stage",
        flops=2 * 256 * depth * width,
    )


def early_kernel(count, tile, *refs):
    block_refs = refs[:count]
    weight_ref, rate_weight_ref, out_hbm, held_s, joined_s, out_ref, sems = refs[count:]
    rows = block_refs[0].shape[0]
    width = weight_ref.shape[1]
    lefts = range(0, width, tile)
    loads = [
        pltpu.make_async_copy(
            weight_ref.at[:, pl.ds(left, tile)], held_s.at[:, pl.ds(left, tile)], sems.at[at]
        )
        for at, left in enumerate(lefts)
    ]
    for copy in loads:
        copy.start()
    for at, block_ref in enumerate(block_refs):
        joined_s[at * rows : (at + 1) * rows, :] = block_ref[...]
    rates = rate_weight_ref.shape[0]
    out_ref[:, width:] = jnp.zeros((out_ref.shape[0], out_ref.shape[1] - width), jnp.float32)
    out_ref[:, width : width + rates] = lax.dot_general(
        joined_s[...],
        rate_weight_ref[...],
        (((1,), (1,)), ((), ())),
        preferred_element_type=jnp.float32,
    )
    for left, copy in zip(lefts, loads, strict=True):
        copy.wait()
        out_ref[:, left : left + tile] = jnp.dot(
            joined_s[...], held_s[:, left : left + tile], preferred_element_type=jnp.float32
        )
    store = pltpu.make_async_copy(out_ref, out_hbm, sems.at[len(loads)])
    store.start()
    store.wait()


def early_stage(blocks, weight, rate_weight):
    rows, depth = blocks[0].shape
    count = len(blocks)
    width = weight.shape[1]
    tile = min(256, width)
    whole = pl.BlockSpec(memory_space=pltpu.VMEM)
    hbm = pl.BlockSpec(memory_space=pltpu.HBM)
    return pl.pallas_call(
        functools.partial(early_kernel, count, tile),
        out_shape=jax.ShapeDtypeStruct((rows * count, width + 128), jnp.float32),
        in_specs=[whole] * count + [hbm, whole],
        out_specs=hbm,
        scratch_shapes=[
            pltpu.VMEM((depth, width), jnp.bfloat16),
            pltpu.VMEM((rows * count, depth), jnp.bfloat16),
            pltpu.VMEM((rows * count, width + 128), jnp.float32),
            pltpu.SemaphoreType.DMA((width // tile + 1,)),
        ],
        compiler_params=pltpu.CompilerParams(vmem_limit_bytes=VMEM_LIMIT),
        cost_estimate=pl.CostEstimate(
            flops=2 * 256 * depth * width, bytes_accessed=8 << 20, transcendentals=0
        ),
        name="early_stage",
    )(*blocks, from_hbm(weight), rate_weight)


def part_kernel(mine_ref, weight_ref, out_ref):
    def body(columns):
        out_ref[:, columns] = jnp.dot(
            mine_ref[...], weight_ref[:, columns], preferred_element_type=jnp.float32
        )

    column_tiles(out_ref.shape[1], body)


def first_kernel(rows, part_ref, theirs_ref, held_ref, first_ref, second_ref):
    def body(columns):
        total = part_ref[: 2 * rows, columns] + jnp.dot(
            theirs_ref[: 2 * rows, :], held_ref[:, columns], preferred_element_type=jnp.float32
        )
        first_ref[:, columns] = total[:rows].astype(first_ref.dtype)
        second_ref[:, columns] = total[rows:].astype(second_ref.dtype)

    column_tiles(held_ref.shape[1], body)


def rest_kernel(rows, part_ref, theirs_ref, held_ref, out_ref):
    def body(columns):
        out_ref[:, columns] = part_ref[2 * rows :, columns] + jnp.dot(
            theirs_ref[2 * rows :, :], held_ref[:, columns], preferred_element_type=jnp.float32
        )

    column_tiles(held_ref.shape[1], body)


def add_kernel(top, share_ref, *refs):
    out_ref = refs[-1]
    total = share_ref[top : top + out_ref.shape[0], :]
    for arrived_ref in refs[:-1]:
        total = total + arrived_ref[...].astype(jnp.float32)
    out_ref[...] = total.astype(out_ref.dtype)


def gather_slots(half):
    slots = [(0, 0), (0, 1)]
    for step in range(1, half):
        slots += [(-step, 0), (-step, 1), (step, 1), (step, 0)]
    return slots + [(-half, 0), (half, 1)]


def send_slots(half):
    slots = []
    for step in range(half, 0, -1):
        slots.append((step, 0))
        if step > 1:
            slots.append((step - 1, 1))
    return slots + [(0, 0)]


def mix_kernel(sizes, scalar_ref, page_id_ref, number_ref, page_ref, *rest):
    heads_dev, piece_count, pool_slots, stages = sizes
    taps_ref, conv_bias_ref, gain_ref = rest[:3]
    stage_refs, rest = rest[3 : 3 + stages], rest[3 + stages :]
    conv_bias = conv_bias_ref[...].astype(jnp.float32).reshape(1, -1)
    gains = gain_ref[...].astype(jnp.float32).reshape(1, -1)
    state_ref, conv_ref, mine_ref, theirs_ref = rest[:4]
    placed_s, rows_s, rate_s, input_s, normed_s, initial_s, page_s, inverse_s, used_s = rest[4:]
    blocks, rows_dev, _ = placed_s.shape
    live_rows = SPAN - BLK
    lead = 8
    state_rows = HEAD_DIM // piece_count
    channels = HEAD_DIM + 2 * STATE
    row_width = HEAD_DIM + channels
    piece_channels = channels // piece_count
    blocks_req = blocks // REQS

    chip_count = blocks // 2
    half = chip_count // 2
    my_index = scalar_ref[0]
    core = my_index % 2
    place = place_of(my_index // 2, chip_count)
    owner_at = 1 + REQS

    def device_at(distance, flip):
        onto = place + jnp.where(core == 0, distance, -distance) + chip_count
        chip = chip_at(lax.rem(onto, chip_count), chip_count)
        return 2 * chip + (core if flip == 0 else 1 - core)

    def clear(holder, _):
        used_s[holder] = 0
        return 0

    lax.fori_loop(0, blocks, clear, 0)

    def invert(block, _):
        inverse_s[scalar_ref[owner_at + block]] = block
        return 0

    lax.fori_loop(0, blocks, invert, 0)

    page_s[...] = page_ref[...].astype(jnp.float32)

    pieces_of = []
    for r in range(REQS):
        for j in range(blocks_req):
            start = j * rows_dev
            low, high = max(start, BLK), start + rows_dev
            if high > BLK:
                pieces_of.append((r, r * blocks_req + j, low - start, low - BLK, high - BLK))
    slots = gather_slots(half)
    at = 0
    for stage_ref in stage_refs:
        for top in range(0, stage_ref.shape[0], rows_dev):
            placed_s[device_at(*slots[at])] = stage_ref[top : top + rows_dev, :]
            at += 1
    for r, block, skipped, low, high in pieces_of:
        rows_s[r, lead + low : lead + high, :] = placed_s[block, skipped:, : rows_s.shape[2]]
        rate_s[r, low:high, :] = placed_s[block, skipped:, rows_s.shape[2] :]
    normed_s[...] = jnp.zeros_like(normed_s)

    wide = (live_rows, 128)
    later = lax.broadcasted_iota(jnp.int32, (live_rows, live_rows), 0)
    sooner = lax.broadcasted_iota(jnp.int32, (live_rows, live_rows), 1)
    causal = later >= sooner
    ones = causal.astype(jnp.float32)
    position = lax.broadcasted_iota(jnp.int32, wide, 0) + BLK
    lead_position = lax.broadcasted_iota(jnp.int32, (live_rows + lead, channels), 0) + BLK - lead
    spread_row = lax.broadcasted_iota(jnp.int32, (piece_count * 128, channels), 0)
    spread_col = lax.broadcasted_iota(jnp.int32, (piece_count * 128, channels), 1)
    spread = (
        ((spread_row // 128) * piece_channels + spread_row % 128 == spread_col)
        & (spread_row % 128 < piece_channels)
    ).astype(jnp.bfloat16)

    lane = lax.broadcasted_iota(jnp.int32, (1, 128), 1)
    bias_lanes = jnp.zeros((1, 128), jnp.float32)
    decay_lanes = jnp.zeros((1, 128), jnp.float32)
    for h in range(heads_dev):
        bias_lanes = jnp.where(lane == h, number_ref[h], bias_lanes)
        decay_lanes = jnp.where(lane == h, number_ref[heads_dev + h], decay_lanes)

    for r in range(REQS):
        live_start = scalar_ref[1 + r] * BLK
        live = position >= live_start
        rate = rate_s[r] + bias_lanes
        step = jnp.where(live, jax.nn.softplus(rate), 0.0)
        drop = -decay_lanes * step
        total = jnp.dot(
            ones, drop, preferred_element_type=jnp.float32, precision=lax.Precision.HIGHEST
        )
        total_t = total.T
        step_t = step.T
        from_start = jnp.exp(total)
        span_tail = total[live_rows - 1 : live_rows, :]
        to_end = jnp.exp(span_tail - total) * step
        kept = jnp.exp(span_tail)
        for h in range(heads_dev):
            lags = []
            for p in range(piece_count):
                page = page_id_ref[r, p, my_index * heads_dev + h]
                holder = lax.div(page, pool_slots)
                rank = used_s[holder]
                used_s[holder] = rank + 1
                state_at = pl.ds(pl.multiple_of(rank * state_rows, state_rows), state_rows)
                lag_at = pl.ds(pl.multiple_of(PER_PEER * state_rows + 8 * rank, 8), 8)
                initial_s[p * state_rows : (p + 1) * state_rows, :] = page_s[holder, state_at, :]
                lags.append(page_s[holder, lag_at, :].astype(jnp.bfloat16))
            initial = initial_s[...]
            lag_lanes = jnp.concatenate(lags, axis=1)
            cached = jnp.dot(lag_lanes, spread, preferred_element_type=jnp.float32)
            first = h * row_width
            c0 = h * channels
            raw = rows_s[r, :, first + HEAD_DIM : first + row_width]
            raw = raw.astype(jnp.bfloat16).astype(jnp.float32)
            inputs = jnp.where(lead_position >= live_start, raw, 0.0)
            for lag in range(CONV - 1):
                inputs = jnp.where(
                    lead_position == live_start - (CONV - 1) + lag,
                    cached[lag : lag + 1, :],
                    inputs,
                )
            input_s[...] = inputs
            conv_ref[r, :, c0 : c0 + channels] = rows_s[
                r,
                live_rows + lead - (CONV - 1) : live_rows + lead,
                first + HEAD_DIM : first + row_width,
            ].astype(jnp.bfloat16)
            summed = jnp.broadcast_to(
                conv_bias[:, c0 : c0 + channels], (live_rows, channels)
            )
            for tap in range(CONV):
                begin = lead - (CONV - 1) + tap
                summed = summed + taps_ref[tap : tap + 1, c0 : c0 + channels].astype(
                    jnp.float32
                ) * input_s[begin : begin + live_rows, :]
            mixed_in = (summed * jax.nn.sigmoid(summed)).astype(jnp.bfloat16)
            x_part = mixed_in[:, :HEAD_DIM]
            b_part = mixed_in[:, HEAD_DIM : HEAD_DIM + STATE]
            c_part = mixed_in[:, HEAD_DIM + STATE :]
            x_float = x_part.astype(jnp.float32)
            last = (((1,), (1,)), ((), ()))
            scores = lax.dot_general(c_part, b_part, last, preferred_element_type=jnp.float32)
            gaps = jnp.where(causal, total[:, h : h + 1] - total_t[h : h + 1, :], 0.0)
            weights = jnp.where(causal, jnp.exp(gaps) * scores * step_t[h : h + 1, :], 0.0)
            outputs = jnp.dot(
                weights.astype(jnp.bfloat16), x_part, preferred_element_type=jnp.float32
            )
            reader = (c_part.astype(jnp.float32) * from_start[:, h : h + 1]).astype(jnp.bfloat16)
            outputs = outputs + lax.dot_general(
                reader, initial.astype(jnp.bfloat16), last, preferred_element_type=jnp.float32
            )
            outputs = outputs + number_ref[2 * heads_dev + h] * x_float
            entering = (x_float * to_end[:, h : h + 1]).astype(jnp.bfloat16)
            added = lax.dot_general(
                entering,
                b_part,
                (((0,), (0,)), ((), ())),
                preferred_element_type=jnp.float32,
            )
            state_ref[r, h] = kept[:, h : h + 1] * initial + added
            gate = rows_s[r, lead:, first : first + HEAD_DIM]
            gate = gate.astype(jnp.bfloat16).astype(jnp.float32)
            gated = outputs * (gate * jax.nn.sigmoid(gate))
            scale = lax.rsqrt(jnp.mean(gated * gated, axis=1, keepdims=True) + EPSILON)
            gain = gains[:, h * HEAD_DIM : (h + 1) * HEAD_DIM]
            normed = jnp.where(live, gated * scale * gain, 0.0)
            for rr, block, skipped, low, high in pieces_of:
                if rr == r:
                    normed_s[block, skipped:, h * HEAD_DIM : (h + 1) * HEAD_DIM] = normed[low:high]

    for at, (distance, flip) in enumerate(send_slots(half)):
        rows = slice(at * rows_dev, (at + 1) * rows_dev)
        mine_ref[rows, :] = normed_s[inverse_s[device_at(distance, flip)]].astype(jnp.bfloat16)
        theirs_ref[rows, :] = normed_s[inverse_s[device_at(-distance, 1 - flip)]].astype(
            jnp.bfloat16
        )


def body(
    hidden,
    in_weight,
    dt_weight,
    dt_bias,
    decay_rate,
    conv_weight,
    conv_bias,
    skip,
    norm_gain,
    out_weight,
    state_pool,
    conv_pool,
    hit_page,
    prefix_blocks,
    owners,
):
    device_count = lax.axis_size("dp")
    my_index = lax.axis_index("dp").astype(jnp.int32).reshape(1)
    heads_dev = dt_weight.shape[0]
    piece_count = hit_page.shape[2]
    row_width = 2 * HEAD_DIM + 2 * STATE
    channels = HEAD_DIM + 2 * STATE
    rows_dev = hidden.shape[0]
    pool_slots, state_rows, _ = state_pool.shape
    chip_count = device_count // 2
    half = chip_count // 2
    page_ids = jnp.swapaxes(hit_page, 1, 2)

    other_type = other_core(hidden, chip_count)
    page_rows = PER_PEER * state_rows + 8 * PER_PEER
    entries = REQS * heads_dev * piece_count
    offered = kernel_call(
        functools.partial(offer_kernel, entries),
        jax.ShapeDtypeStruct((device_count, page_rows, STATE), state_pool.dtype),
        [
            my_index,
            page_ids,
            from_hbm(state_pool),
            from_hbm(jnp.swapaxes(conv_pool, 0, 1)),
        ],
        [
            pltpu.SMEM((entries + 1,), jnp.int32),
            pltpu.VMEM((CONV - 1, pool_slots, STATE), jnp.float32),
            pltpu.VMEM((device_count, 8 * PER_PEER, STATE), jnp.float32),
        ],
        "offer_pages",
        smem=2,
        limit=VMEM_ALL,
    )
    own_type = stream(hidden, chip_count)
    first_other = other_type
    other_type = stream_other(hidden, chip_count)
    scalars = jnp.concatenate([my_index, prefix_blocks, owners])
    numbers = jnp.concatenate([dt_bias, decay_rate, skip])
    offered, own_type, other_type, scalars, numbers, held = lax.optimization_barrier(
        (offered, own_type, other_type, scalars, numbers, out_weight)
    )
    received = lax.all_to_all(offered, "dp", split_axis=0, concat_axis=0, tiled=True)
    held = other_core(held, chip_count)
    blocks = [from_hbm(hidden), first_other, own_type, other_type]
    blocks += [other_core(own_type, chip_count), other_core(other_type, chip_count)]
    early = early_stage(blocks, in_weight, from_hbm(dt_weight))
    pending = []
    for step in range(2, half):
        own_type = stream(own_type, chip_count)
        other_type = stream(other_type, chip_count)
        if step == 2:
            own_type, early = lax.optimization_barrier((own_type, early))
            staged = [from_hbm(early)]
            received, weight_here, rates_here = lax.optimization_barrier(
                (received, in_weight, dt_weight)
            )
            weight_here, rates_here = load(weight_here, rates_here)
        if step == half - 1:
            own_type, weight_here = lax.optimization_barrier((own_type, weight_here))
        pending += [
            own_type,
            other_type,
            other_core(own_type, chip_count),
            other_core(other_type, chip_count),
        ]
        if len(pending) >= 6 or step == half - 1:
            staged.append(stage(pending, weight_here, rates_here))
            pending = []
    own_type = stream(own_type, chip_count)
    last = [own_type, other_core(own_type, chip_count)]
    staged.append(stage(last, weight_here, rates_here))

    live_rows = SPAN - BLK
    normed_rows = jax.ShapeDtypeStruct((chip_count * rows_dev, heads_dev * HEAD_DIM), jnp.bfloat16)
    final_state, final_conv, mine, theirs = kernel_call(
        functools.partial(mix_kernel, (heads_dev, piece_count, pool_slots, len(staged))),
        [
            jax.ShapeDtypeStruct((REQS, heads_dev, HEAD_DIM, STATE), jnp.float32),
            jax.ShapeDtypeStruct((REQS, CONV - 1, heads_dev * channels), jnp.bfloat16),
            normed_rows,
            normed_rows,
        ],
        [
            scalars,
            page_ids,
            numbers,
            received,
            conv_weight,
            conv_bias,
            norm_gain,
            *staged,
        ],
        [
            pltpu.VMEM((device_count, rows_dev, heads_dev * row_width + 128), jnp.float32),
            pltpu.VMEM((REQS, live_rows + 8, heads_dev * row_width), jnp.float32),
            pltpu.VMEM((REQS, live_rows, 128), jnp.float32),
            pltpu.VMEM((live_rows + 8, channels), jnp.float32),
            pltpu.VMEM((device_count, rows_dev, heads_dev * HEAD_DIM), jnp.float32),
            pltpu.VMEM((HEAD_DIM, STATE), jnp.float32),
            pltpu.VMEM(received.shape, jnp.float32),
            pltpu.SMEM((device_count,), jnp.int32),
            pltpu.SMEM((device_count,), jnp.int32),
        ],
        "mixer",
        flops=1 << 30,
        smem=3,
    )

    theirs = other_core(theirs, chip_count)
    width = out_weight.shape[1]
    total_rows = chip_count * rows_dev
    block = jax.ShapeDtypeStruct((rows_dev, width), jnp.bfloat16)
    part = kernel_call(
        part_kernel,
        jax.ShapeDtypeStruct((total_rows, width), jnp.float32),
        [mine, out_weight],
        [],
        "sums_part",
        flops=1 << 30,
    )
    first, second = kernel_call(
        functools.partial(first_kernel, rows_dev),
        [block, block],
        [part, theirs, held],
        [],
        "sums_first",
        flops=1 << 30,
    )
    own_sum = stream(first, chip_count)
    other_sum = stream(second, chip_count)
    shares = kernel_call(
        functools.partial(rest_kernel, rows_dev),
        jax.ShapeDtypeStruct((total_rows - 2 * rows_dev, width), jnp.float32),
        [part, theirs, held],
        [],
        "sums_rest",
        flops=1 << 30,
    )

    def onward(at, *arrived):
        top = (at - 2) * rows_dev
        return kernel_call(
            functools.partial(add_kernel, top), block, [shares, *arrived], [], "onward"
        )

    slots = send_slots(half)
    for at in range(2, len(slots) - 1):
        if slots[at][1] == 0:
            own_sum = stream(onward(at, own_sum), chip_count)
        else:
            other_sum = stream(onward(at, other_sum), chip_count)
    crossed = other_core(other_sum, chip_count)
    mixed = onward(len(slots) - 1, own_sum, crossed)
    return (mixed, final_state, final_conv)


def solution(mesh):
    return jax.shard_map(
        body,
        mesh=mesh,
        in_specs=(
            P(("groups", "dp"), None),
            P(None, "dp"),
            P("dp", None),
            P("dp"),
            P("dp"),
            P(None, "dp"),
            P("dp"),
            P("dp"),
            P("dp"),
            P("dp", None),
            P(("groups", "dp"), None, None),
            P(("groups", "dp"), None, None),
            P("groups", None, None),
            P("groups"),
            P("groups"),
        ),
        out_specs=(
            P(("groups", "dp"), None),
            P("groups", "dp", None, None),
            P("groups", None, "dp"),
        ),
        check_vma=False,
    )
```

```python
import functools

import jax
import jax.numpy as jnp
from jax import lax
from jax.experimental import pallas as pl
from jax.experimental.pallas import tpu as pltpu
from jax.sharding import PartitionSpec as P

HEAD_DIM = 128
STATE = 128
CONV = 4
REQS = 2
SPAN = 192
BLK = 64


EPSILON = 1e-05
PER_PEER = 2
VMEM_LIMIT = 16 * 1024 * 1024
VMEM_ALL = 60 * 1024 * 1024


def folded(chip_count):
    return chip_count <= 8


def chip_at(place, chip_count):
    if not folded(chip_count):
        return place
    back = 2 * (chip_count - 1 - place) + 1
    if isinstance(place, int):
        return 2 * place if place < chip_count // 2 else back
    return jnp.where(place < chip_count // 2, 2 * place, back)


def place_of(chip, chip_count):
    if not folded(chip_count):
        return chip
    return jnp.where(chip % 2 == 0, chip // 2, chip_count - 1 - chip // 2)


def stream(array, chip_count):
    pairs = []
    for place in range(chip_count):
        for core in range(2):
            onto = (place + 1 - 2 * core) % chip_count
            pairs.append((2 * chip_at(place, chip_count) + core, 2 * chip_at(onto, chip_count) + core))
    return lax.ppermute(array, "dp", pairs)


def stream_other(array, chip_count):
    pairs = []
    for place in range(chip_count):
        for core in range(2):
            onto = (place + 1 - 2 * core) % chip_count
            pairs.append(
                (2 * chip_at(place, chip_count) + 1 - core, 2 * chip_at(onto, chip_count) + core)
            )
    return lax.ppermute(array, "dp", pairs)


def other_core(array, chip_count):
    return lax.ppermute(array, "dp", [(d, d ^ 1) for d in range(2 * chip_count)])


def kernel_call(kernel, outs, operands, scratch, name, flops=0, smem=0, limit=VMEM_LIMIT):
    several = isinstance(outs, list)
    whole = pl.BlockSpec(memory_space=pltpu.VMEM)
    scalars = pl.BlockSpec(memory_space=pltpu.SMEM)
    return pl.pallas_call(
        kernel,
        out_shape=outs,
        in_specs=[scalars] * smem + [whole] * (len(operands) - smem),
        out_specs=[whole] * len(outs) if several else whole,
        scratch_shapes=scratch,
        compiler_params=pltpu.CompilerParams(vmem_limit_bytes=limit),
        cost_estimate=pl.CostEstimate(flops=flops, bytes_accessed=8 << 20, transcendentals=0),
        name=name,
    )(*operands)


def offer_kernel(entries, my_ref, ids_ref, state_ref, conv_ref, out_ref, slot_s, conv_s, lag_s):
    pool_slots, state_rows, _ = state_ref.shape
    lag_rows = conv_ref.shape[0]
    piece_channels = conv_ref.shape[2]
    receivers = out_ref.shape[0]
    heads_dev = ids_ref.shape[2] // receivers
    first = my_ref[0] * pool_slots
    conv_s[...] = jnp.zeros_like(conv_s)
    conv_s[:, :, :piece_channels] = conv_ref[...].astype(jnp.float32)
    lag_s[...] = jnp.zeros_like(lag_s)

    def one_receiver(receiver, _):
        used = jnp.int32(0)
        for r in range(REQS):
            for h in range(heads_dev):
                for p in range(ids_ref.shape[1]):
                    slot = ids_ref[r, p, receiver * heads_dev + h] - first
                    slot_s[used] = slot
                    held = jnp.logical_and(slot >= 0, slot < pool_slots)
                    used = used + held.astype(jnp.int32)
        for place in range(PER_PEER):
            slot = jnp.clip(slot_s[place], 0, pool_slots - 1)
            out_ref[receiver, place * state_rows : (place + 1) * state_rows, :] = state_ref[slot]
            for lag in range(lag_rows):
                row = 8 * place + lag
                lag_s[receiver, row : row + 1, :] = conv_s[lag, pl.ds(slot, 1), :]
        return 0

    lax.fori_loop(0, receivers, one_receiver, 0)
    out_ref[:, PER_PEER * state_rows :, :] = lag_s[...].astype(out_ref.dtype)


def column_tiles(width, body):
    tile = min(512, width)

    def one_tile(index, _):
        body(pl.ds(pl.multiple_of(index * tile, tile), tile))
        return 0

    lax.fori_loop(0, width // tile, one_tile, 0)


def from_hbm(array):
    return pltpu.with_memory_space_constraint(array, pltpu.HBM)


def load_kernel(*refs):
    count = (len(refs) - 1) // 2
    sems = refs[-1]
    copies = [
        pltpu.make_async_copy(refs[at], refs[count + at], sems.at[at]) for at in range(count)
    ]
    for copy in copies:
        copy.start()
    for copy in copies:
        copy.wait()


def load(*arrays):
    return pl.pallas_call(
        load_kernel,
        out_shape=[jax.ShapeDtypeStruct(a.shape, a.dtype) for a in arrays],
        in_specs=[pl.BlockSpec(memory_space=pltpu.HBM)] * len(arrays),
        out_specs=[pl.BlockSpec(memory_space=pltpu.VMEM)] * len(arrays),
        scratch_shapes=[pltpu.SemaphoreType.DMA((len(arrays),))],
        compiler_params=pltpu.CompilerParams(vmem_limit_bytes=VMEM_LIMIT),
        cost_estimate=pl.CostEstimate(flops=0, bytes_accessed=8 << 20, transcendentals=0),
        name="load",
    )(*[from_hbm(a) for a in arrays])


def stage_kernel(count, *refs):
    block_refs = refs[:count]
    weight_ref, rate_weight_ref, out_ref, joined_s = refs[count:]
    rows = block_refs[0].shape[0]
    width = weight_ref.shape[1]
    for at, block_ref in enumerate(block_refs):
        joined_s[at * rows : (at + 1) * rows, :] = block_ref[...]
    rates = rate_weight_ref.shape[0]
    out_ref[:, width:] = jnp.zeros((out_ref.shape[0], out_ref.shape[1] - width), jnp.float32)
    out_ref[:, width : width + rates] = lax.dot_general(
        joined_s[...],
        rate_weight_ref[...],
        (((1,), (1,)), ((), ())),
        preferred_element_type=jnp.float32,
    )

    def body(columns):
        out_ref[:, columns] = jnp.dot(
            joined_s[...], weight_ref[:, columns], preferred_element_type=jnp.float32
        )

    column_tiles(width, body)


def stage(blocks, weight, rate_weight):
    rows, depth = blocks[0].shape
    total = rows * len(blocks)
    width = weight.shape[1] + 128
    return kernel_call(
        functools.partial(stage_kernel, len(blocks)),
        jax.ShapeDtypeStruct((total, width), jnp.float32),
        [*blocks, weight, rate_weight],
        [pltpu.VMEM((total, depth), jnp.bfloat16)],
        "stage",
        flops=2 * 256 * depth * width,
    )


def early_kernel(count, tile, *refs):
    block_refs = refs[:count]
    weight_ref, rate_weight_ref, out_hbm, held_s, joined_s, out_ref, sems = refs[count:]
    rows = block_refs[0].shape[0]
    width = weight_ref.shape[1]
    lefts = range(0, width, tile)
    loads = [
        pltpu.make_async_copy(
            weight_ref.at[:, pl.ds(left, tile)], held_s.at[:, pl.ds(left, tile)], sems.at[at]
        )
        for at, left in enumerate(lefts)
    ]
    for copy in loads:
        copy.start()
    for at, block_ref in enumerate(block_refs):
        joined_s[at * rows : (at + 1) * rows, :] = block_ref[...]
    rates = rate_weight_ref.shape[0]
    out_ref[:, width:] = jnp.zeros((out_ref.shape[0], out_ref.shape[1] - width), jnp.float32)
    out_ref[:, width : width + rates] = lax.dot_general(
        joined_s[...],
        rate_weight_ref[...],
        (((1,), (1,)), ((), ())),
        preferred_element_type=jnp.float32,
    )
    for left, copy in zip(lefts, loads, strict=True):
        copy.wait()
        out_ref[:, left : left + tile] = jnp.dot(
            joined_s[...], held_s[:, left : left + tile], preferred_element_type=jnp.float32
        )
    store = pltpu.make_async_copy(out_ref, out_hbm, sems.at[len(loads)])
    store.start()
    store.wait()


def early_stage(blocks, weight, rate_weight):
    rows, depth = blocks[0].shape
    count = len(blocks)
    width = weight.shape[1]
    tile = min(256, width)
    whole = pl.BlockSpec(memory_space=pltpu.VMEM)
    hbm = pl.BlockSpec(memory_space=pltpu.HBM)
    return pl.pallas_call(
        functools.partial(early_kernel, count, tile),
        out_shape=jax.ShapeDtypeStruct((rows * count, width + 128), jnp.float32),
        in_specs=[whole] * count + [hbm, whole],
        out_specs=hbm,
        scratch_shapes=[
            pltpu.VMEM((depth, width), jnp.bfloat16),
            pltpu.VMEM((rows * count, depth), jnp.bfloat16),
            pltpu.VMEM((rows * count, width + 128), jnp.float32),
            pltpu.SemaphoreType.DMA((width // tile + 1,)),
        ],
        compiler_params=pltpu.CompilerParams(vmem_limit_bytes=VMEM_LIMIT),
        cost_estimate=pl.CostEstimate(
            flops=2 * 256 * depth * width, bytes_accessed=8 << 20, transcendentals=0
        ),
        name="early_stage",
    )(*blocks, from_hbm(weight), rate_weight)


def part_kernel(mine_ref, weight_ref, out_ref):
    def body(columns):
        out_ref[:, columns] = jnp.dot(
            mine_ref[...], weight_ref[:, columns], preferred_element_type=jnp.float32
        )

    column_tiles(out_ref.shape[1], body)


def first_kernel(rows, part_ref, theirs_ref, held_ref, first_ref, second_ref):
    def body(columns):
        total = part_ref[: 2 * rows, columns] + jnp.dot(
            theirs_ref[: 2 * rows, :], held_ref[:, columns], preferred_element_type=jnp.float32
        )
        first_ref[:, columns] = total[:rows].astype(first_ref.dtype)
        second_ref[:, columns] = total[rows:].astype(second_ref.dtype)

    column_tiles(held_ref.shape[1], body)


def rest_kernel(rows, part_ref, theirs_ref, held_ref, out_ref):
    def body(columns):
        out_ref[:, columns] = part_ref[2 * rows :, columns] + jnp.dot(
            theirs_ref[2 * rows :, :], held_ref[:, columns], preferred_element_type=jnp.float32
        )

    column_tiles(held_ref.shape[1], body)


def add_kernel(top, share_ref, *refs):
    out_ref = refs[-1]
    total = share_ref[top : top + out_ref.shape[0], :]
    for arrived_ref in refs[:-1]:
        total = total + arrived_ref[...].astype(jnp.float32)
    out_ref[...] = total.astype(out_ref.dtype)


def gather_slots(half):
    slots = [(0, 0), (0, 1)]
    for step in range(1, half):
        slots += [(-step, 0), (-step, 1), (step, 1), (step, 0)]
    return slots + [(-half, 0), (half, 1)]


def send_slots(half):
    slots = []
    for step in range(half, 0, -1):
        slots.append((step, 0))
        if step > 1:
            slots.append((step - 1, 1))
    return slots + [(0, 0)]


def mix_kernel(sizes, scalar_ref, page_id_ref, number_ref, page_ref, *rest):
    heads_dev, piece_count, pool_slots, stages = sizes
    taps_ref, conv_bias_ref, gain_ref = rest[:3]
    stage_refs, rest = rest[3 : 3 + stages], rest[3 + stages :]
    conv_bias = conv_bias_ref[...].astype(jnp.float32).reshape(1, -1)
    gains = gain_ref[...].astype(jnp.float32).reshape(1, -1)
    state_ref, conv_ref, mine_ref, theirs_ref = rest[:4]
    placed_s, rows_s, rate_s, input_s, normed_s, initial_s, page_s, inverse_s, used_s = rest[4:]
    blocks, rows_dev, _ = placed_s.shape
    live_rows = SPAN - BLK
    lead = 8
    state_rows = HEAD_DIM // piece_count
    channels = HEAD_DIM + 2 * STATE
    row_width = HEAD_DIM + channels
    piece_channels = channels // piece_count
    blocks_req = blocks // REQS

    chip_count = blocks // 2
    half = chip_count // 2
    my_index = scalar_ref[0]
    core = my_index % 2
    place = place_of(my_index // 2, chip_count)
    owner_at = 1 + REQS

    def device_at(distance, flip):
        onto = place + jnp.where(core == 0, distance, -distance) + chip_count
        chip = chip_at(lax.rem(onto, chip_count), chip_count)
        return 2 * chip + (core if flip == 0 else 1 - core)

    def clear(holder, _):
        used_s[holder] = 0
        return 0

    lax.fori_loop(0, blocks, clear, 0)

    def invert(block, _):
        inverse_s[scalar_ref[owner_at + block]] = block
        return 0

    lax.fori_loop(0, blocks, invert, 0)

    page_s[...] = page_ref[...].astype(jnp.float32)

    pieces_of = []
    for r in range(REQS):
        for j in range(blocks_req):
            start = j * rows_dev
            low, high = max(start, BLK), start + rows_dev
            if high > BLK:
                pieces_of.append((r, r * blocks_req + j, low - start, low - BLK, high - BLK))
    slots = gather_slots(half)
    at = 0
    for stage_ref in stage_refs:
        for top in range(0, stage_ref.shape[0], rows_dev):
            placed_s[device_at(*slots[at])] = stage_ref[top : top + rows_dev, :]
            at += 1
    for r, block, skipped, low, high in pieces_of:
        rows_s[r, lead + low : lead + high, :] = placed_s[block, skipped:, : rows_s.shape[2]]
        rate_s[r, low:high, :] = placed_s[block, skipped:, rows_s.shape[2] :]
    normed_s[...] = jnp.zeros_like(normed_s)

    wide = (live_rows, 128)
    later = lax.broadcasted_iota(jnp.int32, (live_rows, live_rows), 0)
    sooner = lax.broadcasted_iota(jnp.int32, (live_rows, live_rows), 1)
    causal = later >= sooner
    ones = causal.astype(jnp.float32)
    position = lax.broadcasted_iota(jnp.int32, wide, 0) + BLK
    lead_position = lax.broadcasted_iota(jnp.int32, (live_rows + lead, channels), 0) + BLK - lead
    spread_row = lax.broadcasted_iota(jnp.int32, (piece_count * 128, channels), 0)
    spread_col = lax.broadcasted_iota(jnp.int32, (piece_count * 128, channels), 1)
    spread = (
        ((spread_row // 128) * piece_channels + spread_row % 128 == spread_col)
        & (spread_row % 128 < piece_channels)
    ).astype(jnp.bfloat16)

    lane = lax.broadcasted_iota(jnp.int32, (1, 128), 1)
    bias_lanes = jnp.zeros((1, 128), jnp.float32)
    decay_lanes = jnp.zeros((1, 128), jnp.float32)
    for h in range(heads_dev):
        bias_lanes = jnp.where(lane == h, number_ref[h], bias_lanes)
        decay_lanes = jnp.where(lane == h, number_ref[heads_dev + h], decay_lanes)

    for r in range(REQS):
        live_start = scalar_ref[1 + r] * BLK
        live = position >= live_start
        rate = rate_s[r] + bias_lanes
        step = jnp.where(live, jax.nn.softplus(rate), 0.0)
        drop = -decay_lanes * step
        total = jnp.dot(
            ones, drop, preferred_element_type=jnp.float32, precision=lax.Precision.HIGHEST
        )
        total_t = total.T
        step_t = step.T
        from_start = jnp.exp(total)
        span_tail = total[live_rows - 1 : live_rows, :]
        to_end = jnp.exp(span_tail - total) * step
        kept = jnp.exp(span_tail)
        for h in range(heads_dev):
            lags = []
            for p in range(piece_count):
                page = page_id_ref[r, p, my_index * heads_dev + h]
                holder = lax.div(page, pool_slots)
                rank = used_s[holder]
                used_s[holder] = rank + 1
                state_at = pl.ds(pl.multiple_of(rank * state_rows, state_rows), state_rows)
                lag_at = pl.ds(pl.multiple_of(PER_PEER * state_rows + 8 * rank, 8), 8)
                initial_s[p * state_rows : (p + 1) * state_rows, :] = page_s[holder, state_at, :]
                lags.append(page_s[holder, lag_at, :].astype(jnp.bfloat16))
            initial = initial_s[...]
            lag_lanes = jnp.concatenate(lags, axis=1)
            cached = jnp.dot(lag_lanes, spread, preferred_element_type=jnp.float32)
            first = h * row_width
            c0 = h * channels
            raw = rows_s[r, :, first + HEAD_DIM : first + row_width]
            raw = raw.astype(jnp.bfloat16).astype(jnp.float32)
            inputs = jnp.where(lead_position >= live_start, raw, 0.0)
            for lag in range(CONV - 1):
                inputs = jnp.where(
                    lead_position == live_start - (CONV - 1) + lag,
                    cached[lag : lag + 1, :],
                    inputs,
                )
            input_s[...] = inputs
            conv_ref[r, :, c0 : c0 + channels] = rows_s[
                r,
                live_rows + lead - (CONV - 1) : live_rows + lead,
                first + HEAD_DIM : first + row_width,
            ].astype(jnp.bfloat16)
            summed = jnp.broadcast_to(
                conv_bias[:, c0 : c0 + channels], (live_rows, channels)
            )
            for tap in range(CONV):
                begin = lead - (CONV - 1) + tap
                summed = summed + taps_ref[tap : tap + 1, c0 : c0 + channels].astype(
                    jnp.float32
                ) * input_s[begin : begin + live_rows, :]
            mixed_in = (summed * jax.nn.sigmoid(summed)).astype(jnp.bfloat16)
            x_part = mixed_in[:, :HEAD_DIM]
            b_part = mixed_in[:, HEAD_DIM : HEAD_DIM + STATE]
            c_part = mixed_in[:, HEAD_DIM + STATE :]
            x_float = x_part.astype(jnp.float32)
            last = (((1,), (1,)), ((), ()))
            scores = lax.dot_general(c_part, b_part, last, preferred_element_type=jnp.float32)
            gaps = jnp.where(causal, total[:, h : h + 1] - total_t[h : h + 1, :], 0.0)
            weights = jnp.where(causal, jnp.exp(gaps) * scores * step_t[h : h + 1, :], 0.0)
            outputs = jnp.dot(
                weights.astype(jnp.bfloat16), x_part, preferred_element_type=jnp.float32
            )
            reader = (c_part.astype(jnp.float32) * from_start[:, h : h + 1]).astype(jnp.bfloat16)
            outputs = outputs + lax.dot_general(
                reader, initial.astype(jnp.bfloat16), last, preferred_element_type=jnp.float32
            )
            outputs = outputs + number_ref[2 * heads_dev + h] * x_float
            entering = (x_float * to_end[:, h : h + 1]).astype(jnp.bfloat16)
            added = lax.dot_general(
                entering,
                b_part,
                (((0,), (0,)), ((), ())),
                preferred_element_type=jnp.float32,
            )
            state_ref[r, h] = kept[:, h : h + 1] * initial + added
            gate = rows_s[r, lead:, first : first + HEAD_DIM]
            gate = gate.astype(jnp.bfloat16).astype(jnp.float32)
            gated = outputs * (gate * jax.nn.sigmoid(gate))
            scale = lax.rsqrt(jnp.mean(gated * gated, axis=1, keepdims=True) + EPSILON)
            gain = gains[:, h * HEAD_DIM : (h + 1) * HEAD_DIM]
            normed = jnp.where(live, gated * scale * gain, 0.0)
            for rr, block, skipped, low, high in pieces_of:
                if rr == r:
                    normed_s[block, skipped:, h * HEAD_DIM : (h + 1) * HEAD_DIM] = normed[low:high]

    for at, (distance, flip) in enumerate(send_slots(half)):
        rows = slice(at * rows_dev, (at + 1) * rows_dev)
        mine_ref[rows, :] = normed_s[inverse_s[device_at(distance, flip)]].astype(jnp.bfloat16)
        theirs_ref[rows, :] = normed_s[inverse_s[device_at(-distance, 1 - flip)]].astype(
            jnp.bfloat16
        )


def body(
    hidden,
    in_weight,
    dt_weight,
    dt_bias,
    decay_rate,
    conv_weight,
    conv_bias,
    skip,
    norm_gain,
    out_weight,
    state_pool,
    conv_pool,
    hit_page,
    prefix_blocks,
    owners,
):
    device_count = lax.axis_size("dp")
    my_index = lax.axis_index("dp").astype(jnp.int32).reshape(1)
    heads_dev = dt_weight.shape[0]
    piece_count = hit_page.shape[2]
    row_width = 2 * HEAD_DIM + 2 * STATE
    channels = HEAD_DIM + 2 * STATE
    rows_dev = hidden.shape[0]
    pool_slots, state_rows, _ = state_pool.shape
    chip_count = device_count // 2
    half = chip_count // 2
    page_ids = jnp.swapaxes(hit_page, 1, 2)

    other_type = other_core(hidden, chip_count)
    page_rows = PER_PEER * state_rows + 8 * PER_PEER
    entries = REQS * heads_dev * piece_count
    offered = kernel_call(
        functools.partial(offer_kernel, entries),
        jax.ShapeDtypeStruct((device_count, page_rows, STATE), state_pool.dtype),
        [
            my_index,
            page_ids,
            from_hbm(state_pool),
            from_hbm(jnp.swapaxes(conv_pool, 0, 1)),
        ],
        [
            pltpu.SMEM((entries + 1,), jnp.int32),
            pltpu.VMEM((CONV - 1, pool_slots, STATE), jnp.float32),
            pltpu.VMEM((device_count, 8 * PER_PEER, STATE), jnp.float32),
        ],
        "offer_pages",
        smem=2,
        limit=VMEM_ALL,
    )
    own_type = stream(hidden, chip_count)
    first_other = other_type
    other_type = stream_other(hidden, chip_count)
    scalars = jnp.concatenate([my_index, prefix_blocks, owners])
    numbers = jnp.concatenate([dt_bias, decay_rate, skip])
    offered, own_type, other_type, scalars, numbers, held = lax.optimization_barrier(
        (offered, own_type, other_type, scalars, numbers, out_weight)
    )
    received = lax.all_to_all(offered, "dp", split_axis=0, concat_axis=0, tiled=True)
    held = other_core(held, chip_count)
    blocks = [from_hbm(hidden), first_other, own_type, other_type]
    blocks += [other_core(own_type, chip_count), other_core(other_type, chip_count)]
    early = early_stage(blocks, in_weight, from_hbm(dt_weight))
    pending = []
    for step in range(2, half):
        own_type = stream(own_type, chip_count)
        other_type = stream(other_type, chip_count)
        if step == 2:
            own_type, early = lax.optimization_barrier((own_type, early))
            staged = [from_hbm(early)]
            received, weight_here, rates_here = lax.optimization_barrier(
                (received, in_weight, dt_weight)
            )
            weight_here, rates_here = load(weight_here, rates_here)
        if step == half - 1:
            own_type, weight_here = lax.optimization_barrier((own_type, weight_here))
        pending += [
            own_type,
            other_type,
            other_core(own_type, chip_count),
            other_core(other_type, chip_count),
        ]
        if len(pending) >= 6 or step == half - 1:
            staged.append(stage(pending, weight_here, rates_here))
            pending = []
    own_type = stream(own_type, chip_count)
    own_type, staged[-1] = lax.optimization_barrier((own_type, staged[-1]))
    last = [own_type, other_core(own_type, chip_count)]
    staged.append(stage(last, weight_here, rates_here))

    live_rows = SPAN - BLK
    normed_rows = jax.ShapeDtypeStruct((chip_count * rows_dev, heads_dev * HEAD_DIM), jnp.bfloat16)
    final_state, final_conv, mine, theirs = kernel_call(
        functools.partial(mix_kernel, (heads_dev, piece_count, pool_slots, len(staged))),
        [
            jax.ShapeDtypeStruct((REQS, heads_dev, HEAD_DIM, STATE), jnp.float32),
            jax.ShapeDtypeStruct((REQS, CONV - 1, heads_dev * channels), jnp.bfloat16),
            normed_rows,
            normed_rows,
        ],
        [
            scalars,
            page_ids,
            numbers,
            received,
            conv_weight,
            conv_bias,
            norm_gain,
            *staged,
        ],
        [
            pltpu.VMEM((device_count, rows_dev, heads_dev * row_width + 128), jnp.float32),
            pltpu.VMEM((REQS, live_rows + 8, heads_dev * row_width), jnp.float32),
            pltpu.VMEM((REQS, live_rows, 128), jnp.float32),
            pltpu.VMEM((live_rows + 8, channels), jnp.float32),
            pltpu.VMEM((device_count, rows_dev, heads_dev * HEAD_DIM), jnp.float32),
            pltpu.VMEM((HEAD_DIM, STATE), jnp.float32),
            pltpu.VMEM(received.shape, jnp.float32),
            pltpu.SMEM((device_count,), jnp.int32),
            pltpu.SMEM((device_count,), jnp.int32),
        ],
        "mixer",
        flops=1 << 30,
        smem=3,
    )

    theirs = other_core(theirs, chip_count)
    width = out_weight.shape[1]
    total_rows = chip_count * rows_dev
    block = jax.ShapeDtypeStruct((rows_dev, width), jnp.bfloat16)
    part = kernel_call(
        part_kernel,
        jax.ShapeDtypeStruct((total_rows, width), jnp.float32),
        [mine, out_weight],
        [],
        "sums_part",
        flops=1 << 30,
    )
    first, second = kernel_call(
        functools.partial(first_kernel, rows_dev),
        [block, block],
        [part, theirs, held],
        [],
        "sums_first",
        flops=1 << 30,
    )
    own_sum = stream(first, chip_count)
    other_sum = stream(second, chip_count)
    shares = kernel_call(
        functools.partial(rest_kernel, rows_dev),
        jax.ShapeDtypeStruct((total_rows - 2 * rows_dev, width), jnp.float32),
        [part, theirs, held],
        [],
        "sums_rest",
        flops=1 << 30,
    )

    def onward(at, *arrived):
        top = (at - 2) * rows_dev
        return kernel_call(
            functools.partial(add_kernel, top), block, [shares, *arrived], [], "onward"
        )

    slots = send_slots(half)
    for at in range(2, len(slots) - 1):
        if slots[at][1] == 0:
            own_sum = stream(onward(at, own_sum), chip_count)
        else:
            other_sum = stream(onward(at, other_sum), chip_count)
    crossed = other_core(other_sum, chip_count)
    mixed = onward(len(slots) - 1, own_sum, crossed)
    return (mixed, final_state, final_conv)


def solution(mesh):
    return jax.shard_map(
        body,
        mesh=mesh,
        in_specs=(
            P(("groups", "dp"), None),
            P(None, "dp"),
            P("dp", None),
            P("dp"),
            P("dp"),
            P(None, "dp"),
            P("dp"),
            P("dp"),
            P("dp"),
            P("dp", None),
            P(("groups", "dp"), None, None),
            P(("groups", "dp"), None, None),
            P("groups", None, None),
            P("groups"),
            P("groups"),
        ),
        out_specs=(
            P(("groups", "dp"), None),
            P("groups", "dp", None, None),
            P("groups", None, "dp"),
        ),
        check_vma=False,
    )
```

```python
import functools

import jax
import jax.numpy as jnp
from jax import lax
from jax.experimental import pallas as pl
from jax.experimental.pallas import tpu as pltpu
from jax.sharding import PartitionSpec as P

HEAD_DIM = 128
STATE = 128
CONV = 4
REQS = 2
SPAN = 192
BLK = 64


EPSILON = 1e-05
PER_PEER = 2
VMEM_LIMIT = 16 * 1024 * 1024
VMEM_ALL = 60 * 1024 * 1024


def folded(chip_count):
    return chip_count <= 8


def chip_at(place, chip_count):
    if not folded(chip_count):
        return place
    back = 2 * (chip_count - 1 - place) + 1
    if isinstance(place, int):
        return 2 * place if place < chip_count // 2 else back
    return jnp.where(place < chip_count // 2, 2 * place, back)


def place_of(chip, chip_count):
    if not folded(chip_count):
        return chip
    return jnp.where(chip % 2 == 0, chip // 2, chip_count - 1 - chip // 2)


def stream(array, chip_count):
    pairs = []
    for place in range(chip_count):
        for core in range(2):
            onto = (place + 1 - 2 * core) % chip_count
            pairs.append((2 * chip_at(place, chip_count) + core, 2 * chip_at(onto, chip_count) + core))
    return lax.ppermute(array, "dp", pairs)


def stream_other(array, chip_count):
    pairs = []
    for place in range(chip_count):
        for core in range(2):
            onto = (place + 1 - 2 * core) % chip_count
            pairs.append(
                (2 * chip_at(place, chip_count) + 1 - core, 2 * chip_at(onto, chip_count) + core)
            )
    return lax.ppermute(array, "dp", pairs)


def other_core(array, chip_count):
    return lax.ppermute(array, "dp", [(d, d ^ 1) for d in range(2 * chip_count)])


def kernel_call(kernel, outs, operands, scratch, name, flops=0, smem=0, limit=VMEM_LIMIT):
    several = isinstance(outs, list)
    whole = pl.BlockSpec(memory_space=pltpu.VMEM)
    scalars = pl.BlockSpec(memory_space=pltpu.SMEM)
    return pl.pallas_call(
        kernel,
        out_shape=outs,
        in_specs=[scalars] * smem + [whole] * (len(operands) - smem),
        out_specs=[whole] * len(outs) if several else whole,
        scratch_shapes=scratch,
        compiler_params=pltpu.CompilerParams(vmem_limit_bytes=limit),
        cost_estimate=pl.CostEstimate(flops=flops, bytes_accessed=8 << 20, transcendentals=0),
        name=name,
    )(*operands)


def offer_kernel(entries, my_ref, ids_ref, state_ref, conv_ref, out_ref, slot_s, conv_s, lag_s):
    pool_slots, state_rows, _ = state_ref.shape
    lag_rows = conv_ref.shape[0]
    piece_channels = conv_ref.shape[2]
    receivers = out_ref.shape[0]
    heads_dev = ids_ref.shape[2] // receivers
    first = my_ref[0] * pool_slots
    conv_s[...] = jnp.zeros_like(conv_s)
    conv_s[:, :, :piece_channels] = conv_ref[...].astype(jnp.float32)
    lag_s[...] = jnp.zeros_like(lag_s)

    def one_receiver(receiver, _):
        used = jnp.int32(0)
        for r in range(REQS):
            for h in range(heads_dev):
                for p in range(ids_ref.shape[1]):
                    slot = ids_ref[r, p, receiver * heads_dev + h] - first
                    slot_s[used] = slot
                    held = jnp.logical_and(slot >= 0, slot < pool_slots)
                    used = used + held.astype(jnp.int32)
        for place in range(PER_PEER):
            slot = jnp.clip(slot_s[place], 0, pool_slots - 1)
            out_ref[receiver, place * state_rows : (place + 1) * state_rows, :] = state_ref[slot]
            for lag in range(lag_rows):
                row = 8 * place + lag
                lag_s[receiver, row : row + 1, :] = conv_s[lag, pl.ds(slot, 1), :]
        return 0

    lax.fori_loop(0, receivers, one_receiver, 0)
    out_ref[:, PER_PEER * state_rows :, :] = lag_s[...].astype(out_ref.dtype)


def column_tiles(width, body):
    tile = min(512, width)

    def one_tile(index, _):
        body(pl.ds(pl.multiple_of(index * tile, tile), tile))
        return 0

    lax.fori_loop(0, width // tile, one_tile, 0)


def from_hbm(array):
    return pltpu.with_memory_space_constraint(array, pltpu.HBM)


def load_kernel(*refs):
    count = (len(refs) - 1) // 2
    sems = refs[-1]
    copies = [
        pltpu.make_async_copy(refs[at], refs[count + at], sems.at[at]) for at in range(count)
    ]
    for copy in copies:
        copy.start()
    for copy in copies:
        copy.wait()


def load(*arrays):
    return pl.pallas_call(
        load_kernel,
        out_shape=[jax.ShapeDtypeStruct(a.shape, a.dtype) for a in arrays],
        in_specs=[pl.BlockSpec(memory_space=pltpu.HBM)] * len(arrays),
        out_specs=[pl.BlockSpec(memory_space=pltpu.VMEM)] * len(arrays),
        scratch_shapes=[pltpu.SemaphoreType.DMA((len(arrays),))],
        compiler_params=pltpu.CompilerParams(vmem_limit_bytes=VMEM_LIMIT),
        cost_estimate=pl.CostEstimate(flops=0, bytes_accessed=8 << 20, transcendentals=0),
        name="load",
    )(*[from_hbm(a) for a in arrays])


def stage_kernel(count, *refs):
    block_refs = refs[:count]
    weight_ref, rate_weight_ref, out_ref, joined_s = refs[count:]
    rows = block_refs[0].shape[0]
    width = weight_ref.shape[1]
    for at, block_ref in enumerate(block_refs):
        joined_s[at * rows : (at + 1) * rows, :] = block_ref[...]
    rates = rate_weight_ref.shape[0]
    out_ref[:, width:] = jnp.zeros((out_ref.shape[0], out_ref.shape[1] - width), jnp.float32)
    out_ref[:, width : width + rates] = lax.dot_general(
        joined_s[...],
        rate_weight_ref[...],
        (((1,), (1,)), ((), ())),
        preferred_element_type=jnp.float32,
    )

    def body(columns):
        out_ref[:, columns] = jnp.dot(
            joined_s[...], weight_ref[:, columns], preferred_element_type=jnp.float32
        )

    column_tiles(width, body)


def stage(blocks, weight, rate_weight):
    rows, depth = blocks[0].shape
    total = rows * len(blocks)
    width = weight.shape[1] + 128
    return kernel_call(
        functools.partial(stage_kernel, len(blocks)),
        jax.ShapeDtypeStruct((total, width), jnp.float32),
        [*blocks, weight, rate_weight],
        [pltpu.VMEM((total, depth), jnp.bfloat16)],
        "stage",
        flops=2 * 256 * depth * width,
    )


def early_kernel(count, tile, *refs):
    block_refs = refs[:count]
    weight_ref, rate_weight_ref, out_hbm, held_s, joined_s, out_ref, sems = refs[count:]
    rows = block_refs[0].shape[0]
    width = weight_ref.shape[1]
    lefts = range(0, width, tile)
    loads = [
        pltpu.make_async_copy(
            weight_ref.at[:, pl.ds(left, tile)], held_s.at[:, pl.ds(left, tile)], sems.at[at]
        )
        for at, left in enumerate(lefts)
    ]
    for copy in loads:
        copy.start()
    for at, block_ref in enumerate(block_refs):
        joined_s[at * rows : (at + 1) * rows, :] = block_ref[...]
    rates = rate_weight_ref.shape[0]
    out_ref[:, width:] = jnp.zeros((out_ref.shape[0], out_ref.shape[1] - width), jnp.float32)
    out_ref[:, width : width + rates] = lax.dot_general(
        joined_s[...],
        rate_weight_ref[...],
        (((1,), (1,)), ((), ())),
        preferred_element_type=jnp.float32,
    )
    for left, copy in zip(lefts, loads, strict=True):
        copy.wait()
        out_ref[:, left : left + tile] = jnp.dot(
            joined_s[...], held_s[:, left : left + tile], preferred_element_type=jnp.float32
        )
    store = pltpu.make_async_copy(out_ref, out_hbm, sems.at[len(loads)])
    store.start()
    store.wait()


def early_stage(blocks, weight, rate_weight):
    rows, depth = blocks[0].shape
    count = len(blocks)
    width = weight.shape[1]
    tile = min(256, width)
    whole = pl.BlockSpec(memory_space=pltpu.VMEM)
    hbm = pl.BlockSpec(memory_space=pltpu.HBM)
    return pl.pallas_call(
        functools.partial(early_kernel, count, tile),
        out_shape=pltpu.HBM((rows * count, width + 128), jnp.float32),
        in_specs=[whole] * count + [hbm, whole],
        out_specs=hbm,
        scratch_shapes=[
            pltpu.VMEM((depth, width), jnp.bfloat16),
            pltpu.VMEM((rows * count, depth), jnp.bfloat16),
            pltpu.VMEM((rows * count, width + 128), jnp.float32),
            pltpu.SemaphoreType.DMA((width // tile + 1,)),
        ],
        compiler_params=pltpu.CompilerParams(vmem_limit_bytes=VMEM_LIMIT),
        cost_estimate=pl.CostEstimate(
            flops=2 * 256 * depth * width, bytes_accessed=8 << 20, transcendentals=0
        ),
        name="early_stage",
    )(*blocks, from_hbm(weight), rate_weight)


def part_kernel(mine_ref, weight_ref, out_ref):
    rows = out_ref.shape[0]

    def body(columns):
        out_ref[:, columns] = jnp.dot(
            mine_ref[:rows, :], weight_ref[:, columns], preferred_element_type=jnp.float32
        )

    column_tiles(out_ref.shape[1], body)


def first_kernel(rows, part_ref, theirs_ref, held_ref, first_ref, second_ref):
    def body(columns):
        total = part_ref[: 2 * rows, columns] + jnp.dot(
            theirs_ref[: 2 * rows, :], held_ref[:, columns], preferred_element_type=jnp.float32
        )
        first_ref[:, columns] = total[:rows].astype(first_ref.dtype)
        second_ref[:, columns] = total[rows:].astype(second_ref.dtype)

    column_tiles(held_ref.shape[1], body)


def rest_kernel(rows, mine_ref, theirs_ref, weight_ref, held_ref, out_ref):
    def body(columns):
        total = jnp.dot(
            mine_ref[2 * rows :, :], weight_ref[:, columns], preferred_element_type=jnp.float32
        )
        out_ref[:, columns] = total + jnp.dot(
            theirs_ref[2 * rows :, :], held_ref[:, columns], preferred_element_type=jnp.float32
        )

    column_tiles(held_ref.shape[1], body)


def add_kernel(top, share_ref, *refs):
    out_ref = refs[-1]
    total = share_ref[top : top + out_ref.shape[0], :]
    for arrived_ref in refs[:-1]:
        total = total + arrived_ref[...].astype(jnp.float32)
    out_ref[...] = total.astype(out_ref.dtype)


def gather_slots(half):
    slots = [(0, 0), (0, 1)]
    for step in range(1, half):
        slots += [(-step, 0), (-step, 1), (step, 1), (step, 0)]
    return slots + [(-half, 0), (half, 1)]


def send_slots(half):
    slots = []
    for step in range(half, 0, -1):
        slots.append((step, 0))
        if step > 1:
            slots.append((step - 1, 1))
    return slots + [(0, 0)]


def mix_kernel(sizes, scalar_ref, page_id_ref, number_ref, page_ref, *rest):
    heads_dev, piece_count, pool_slots, stages = sizes
    taps_ref, conv_bias_ref, gain_ref = rest[:3]
    stage_refs, rest = rest[3 : 3 + stages], rest[3 + stages :]
    conv_bias = conv_bias_ref[...].astype(jnp.float32).reshape(1, -1)
    gains = gain_ref[...].astype(jnp.float32).reshape(1, -1)
    state_ref, conv_ref, mine_ref, theirs_ref = rest[:4]
    placed_s, rows_s, rate_s, input_s, normed_s, initial_s, page_s, inverse_s, used_s = rest[4:]
    blocks, rows_dev, _ = placed_s.shape
    live_rows = SPAN - BLK
    lead = 8
    state_rows = HEAD_DIM // piece_count
    channels = HEAD_DIM + 2 * STATE
    row_width = HEAD_DIM + channels
    piece_channels = channels // piece_count
    blocks_req = blocks // REQS

    chip_count = blocks // 2
    half = chip_count // 2
    my_index = scalar_ref[0]
    core = my_index % 2
    place = place_of(my_index // 2, chip_count)
    owner_at = 1 + REQS

    def device_at(distance, flip):
        onto = place + jnp.where(core == 0, distance, -distance) + chip_count
        chip = chip_at(lax.rem(onto, chip_count), chip_count)
        return 2 * chip + (core if flip == 0 else 1 - core)

    def clear(holder, _):
        used_s[holder] = 0
        return 0

    lax.fori_loop(0, blocks, clear, 0)

    def invert(block, _):
        inverse_s[scalar_ref[owner_at + block]] = block
        return 0

    lax.fori_loop(0, blocks, invert, 0)

    page_s[...] = page_ref[...].astype(jnp.float32)

    pieces_of = []
    for r in range(REQS):
        for j in range(blocks_req):
            start = j * rows_dev
            low, high = max(start, BLK), start + rows_dev
            if high > BLK:
                pieces_of.append((r, r * blocks_req + j, low - start, low - BLK, high - BLK))
    slots = gather_slots(half)
    at = 0
    for stage_ref in stage_refs:
        for top in range(0, stage_ref.shape[0], rows_dev):
            placed_s[device_at(*slots[at])] = stage_ref[top : top + rows_dev, :]
            at += 1
    for r, block, skipped, low, high in pieces_of:
        rows_s[r, lead + low : lead + high, :] = placed_s[block, skipped:, : rows_s.shape[2]]
        rate_s[r, low:high, :] = placed_s[block, skipped:, rows_s.shape[2] :]
    normed_s[...] = jnp.zeros_like(normed_s)

    wide = (live_rows, 128)
    later = lax.broadcasted_iota(jnp.int32, (live_rows, live_rows), 0)
    sooner = lax.broadcasted_iota(jnp.int32, (live_rows, live_rows), 1)
    causal = later >= sooner
    ones = causal.astype(jnp.float32)
    position = lax.broadcasted_iota(jnp.int32, wide, 0) + BLK
    lead_position = lax.broadcasted_iota(jnp.int32, (live_rows + lead, channels), 0) + BLK - lead
    spread_row = lax.broadcasted_iota(jnp.int32, (piece_count * 128, channels), 0)
    spread_col = lax.broadcasted_iota(jnp.int32, (piece_count * 128, channels), 1)
    spread = (
        ((spread_row // 128) * piece_channels + spread_row % 128 == spread_col)
        & (spread_row % 128 < piece_channels)
    ).astype(jnp.bfloat16)

    lane = lax.broadcasted_iota(jnp.int32, (1, 128), 1)
    bias_lanes = jnp.zeros((1, 128), jnp.float32)
    decay_lanes = jnp.zeros((1, 128), jnp.float32)
    for h in range(heads_dev):
        bias_lanes = jnp.where(lane == h, number_ref[h], bias_lanes)
        decay_lanes = jnp.where(lane == h, number_ref[heads_dev + h], decay_lanes)

    for r in range(REQS):
        live_start = scalar_ref[1 + r] * BLK
        live = position >= live_start
        rate = rate_s[r] + bias_lanes
        step = jnp.where(live, jax.nn.softplus(rate), 0.0)
        drop = -decay_lanes * step
        total = jnp.dot(
            ones, drop, preferred_element_type=jnp.float32, precision=lax.Precision.HIGHEST
        )
        total_t = total.T
        step_t = step.T
        from_start = jnp.exp(total)
        span_tail = total[live_rows - 1 : live_rows, :]
        to_end = jnp.exp(span_tail - total) * step
        kept = jnp.exp(span_tail)
        for h in range(heads_dev):
            lags = []
            for p in range(piece_count):
                page = page_id_ref[r, p, my_index * heads_dev + h]
                holder = lax.div(page, pool_slots)
                rank = used_s[holder]
                used_s[holder] = rank + 1
                state_at = pl.ds(pl.multiple_of(rank * state_rows, state_rows), state_rows)
                lag_at = pl.ds(pl.multiple_of(PER_PEER * state_rows + 8 * rank, 8), 8)
                initial_s[p * state_rows : (p + 1) * state_rows, :] = page_s[holder, state_at, :]
                lags.append(page_s[holder, lag_at, :].astype(jnp.bfloat16))
            initial = initial_s[...]
            lag_lanes = jnp.concatenate(lags, axis=1)
            cached = jnp.dot(lag_lanes, spread, preferred_element_type=jnp.float32)
            first = h * row_width
            c0 = h * channels
            raw = rows_s[r, :, first + HEAD_DIM : first + row_width]
            raw = raw.astype(jnp.bfloat16).astype(jnp.float32)
            inputs = jnp.where(lead_position >= live_start, raw, 0.0)
            for lag in range(CONV - 1):
                inputs = jnp.where(
                    lead_position == live_start - (CONV - 1) + lag,
                    cached[lag : lag + 1, :],
                    inputs,
                )
            input_s[...] = inputs
            conv_ref[r, :, c0 : c0 + channels] = rows_s[
                r,
                live_rows + lead - (CONV - 1) : live_rows + lead,
                first + HEAD_DIM : first + row_width,
            ].astype(jnp.bfloat16)
            summed = jnp.broadcast_to(
                conv_bias[:, c0 : c0 + channels], (live_rows, channels)
            )
            for tap in range(CONV):
                begin = lead - (CONV - 1) + tap
                summed = summed + taps_ref[tap : tap + 1, c0 : c0 + channels].astype(
                    jnp.float32
                ) * input_s[begin : begin + live_rows, :]
            mixed_in = (summed * jax.nn.sigmoid(summed)).astype(jnp.bfloat16)
            x_part = mixed_in[:, :HEAD_DIM]
            b_part = mixed_in[:, HEAD_DIM : HEAD_DIM + STATE]
            c_part = mixed_in[:, HEAD_DIM + STATE :]
            x_float = x_part.astype(jnp.float32)
            last = (((1,), (1,)), ((), ()))
            scores = lax.dot_general(c_part, b_part, last, preferred_element_type=jnp.float32)
            gaps = jnp.where(causal, total[:, h : h + 1] - total_t[h : h + 1, :], 0.0)
            weights = jnp.where(causal, jnp.exp(gaps) * scores * step_t[h : h + 1, :], 0.0)
            outputs = jnp.dot(
                weights.astype(jnp.bfloat16), x_part, preferred_element_type=jnp.float32
            )
            reader = (c_part.astype(jnp.float32) * from_start[:, h : h + 1]).astype(jnp.bfloat16)
            outputs = outputs + lax.dot_general(
                reader, initial.astype(jnp.bfloat16), last, preferred_element_type=jnp.float32
            )
            outputs = outputs + number_ref[2 * heads_dev + h] * x_float
            entering = (x_float * to_end[:, h : h + 1]).astype(jnp.bfloat16)
            added = lax.dot_general(
                entering,
                b_part,
                (((0,), (0,)), ((), ())),
                preferred_element_type=jnp.float32,
            )
            state_ref[r, h] = kept[:, h : h + 1] * initial + added
            gate = rows_s[r, lead:, first : first + HEAD_DIM]
            gate = gate.astype(jnp.bfloat16).astype(jnp.float32)
            gated = outputs * (gate * jax.nn.sigmoid(gate))
            scale = lax.rsqrt(jnp.mean(gated * gated, axis=1, keepdims=True) + EPSILON)
            gain = gains[:, h * HEAD_DIM : (h + 1) * HEAD_DIM]
            normed = jnp.where(live, gated * scale * gain, 0.0)
            for rr, block, skipped, low, high in pieces_of:
                if rr == r:
                    normed_s[block, skipped:, h * HEAD_DIM : (h + 1) * HEAD_DIM] = normed[low:high]

    for at, (distance, flip) in enumerate(send_slots(half)):
        rows = slice(at * rows_dev, (at + 1) * rows_dev)
        mine_ref[rows, :] = normed_s[inverse_s[device_at(distance, flip)]].astype(jnp.bfloat16)
        theirs_ref[rows, :] = normed_s[inverse_s[device_at(-distance, 1 - flip)]].astype(
            jnp.bfloat16
        )


def body(
    hidden,
    in_weight,
    dt_weight,
    dt_bias,
    decay_rate,
    conv_weight,
    conv_bias,
    skip,
    norm_gain,
    out_weight,
    state_pool,
    conv_pool,
    hit_page,
    prefix_blocks,
    owners,
):
    device_count = lax.axis_size("dp")
    my_index = lax.axis_index("dp").astype(jnp.int32).reshape(1)
    heads_dev = dt_weight.shape[0]
    piece_count = hit_page.shape[2]
    row_width = 2 * HEAD_DIM + 2 * STATE
    channels = HEAD_DIM + 2 * STATE
    rows_dev = hidden.shape[0]
    pool_slots, state_rows, _ = state_pool.shape
    chip_count = device_count // 2
    half = chip_count // 2
    page_ids = jnp.swapaxes(hit_page, 1, 2)

    other_type = other_core(hidden, chip_count)
    page_rows = PER_PEER * state_rows + 8 * PER_PEER
    entries = REQS * heads_dev * piece_count
    offered = kernel_call(
        functools.partial(offer_kernel, entries),
        jax.ShapeDtypeStruct((device_count, page_rows, STATE), state_pool.dtype),
        [
            my_index,
            page_ids,
            from_hbm(state_pool),
            from_hbm(jnp.swapaxes(conv_pool, 0, 1)),
        ],
        [
            pltpu.SMEM((entries + 1,), jnp.int32),
            pltpu.VMEM((CONV - 1, pool_slots, STATE), jnp.float32),
            pltpu.VMEM((device_count, 8 * PER_PEER, STATE), jnp.float32),
        ],
        "offer_pages",
        smem=2,
        limit=VMEM_ALL,
    )
    own_type = stream(hidden, chip_count)
    first_other = other_type
    other_type = stream_other(hidden, chip_count)
    scalars = jnp.concatenate([my_index, prefix_blocks, owners])
    numbers = jnp.concatenate([dt_bias, decay_rate, skip])
    offered, own_type, other_type, scalars, numbers, held = lax.optimization_barrier(
        (offered, own_type, other_type, scalars, numbers, out_weight)
    )
    received = lax.all_to_all(offered, "dp", split_axis=0, concat_axis=0, tiled=True)
    held = other_core(held, chip_count)
    blocks = [from_hbm(hidden), first_other, own_type, other_type]
    blocks += [other_core(own_type, chip_count), other_core(other_type, chip_count)]
    early = early_stage(blocks, in_weight, from_hbm(dt_weight))
    pending = []
    for step in range(2, half):
        own_type = stream(own_type, chip_count)
        other_type = stream(other_type, chip_count)
        if step == 2:
            own_type, early = lax.optimization_barrier((own_type, early))
            staged = [from_hbm(early)]
            received, weight_here, rates_here = lax.optimization_barrier(
                (received, in_weight, dt_weight)
            )
            weight_here, rates_here = load(weight_here, rates_here)
        if step == half - 1:
            own_type, weight_here = lax.optimization_barrier((own_type, weight_here))
        pending += [
            own_type,
            other_type,
            other_core(own_type, chip_count),
            other_core(other_type, chip_count),
        ]
        if len(pending) >= 6 or step == half - 1:
            staged.append(stage(pending, weight_here, rates_here))
            pending = []
    own_type = stream(own_type, chip_count)
    last = [own_type, other_core(own_type, chip_count)]
    staged.append(stage(last, weight_here, rates_here))

    live_rows = SPAN - BLK
    normed_rows = jax.ShapeDtypeStruct((chip_count * rows_dev, heads_dev * HEAD_DIM), jnp.bfloat16)
    final_state, final_conv, mine, theirs = kernel_call(
        functools.partial(mix_kernel, (heads_dev, piece_count, pool_slots, len(staged))),
        [
            jax.ShapeDtypeStruct((REQS, heads_dev, HEAD_DIM, STATE), jnp.float32),
            jax.ShapeDtypeStruct((REQS, CONV - 1, heads_dev * channels), jnp.bfloat16),
            normed_rows,
            normed_rows,
        ],
        [
            scalars,
            page_ids,
            numbers,
            received,
            conv_weight,
            conv_bias,
            norm_gain,
            *staged,
        ],
        [
            pltpu.VMEM((device_count, rows_dev, heads_dev * row_width + 128), jnp.float32),
            pltpu.VMEM((REQS, live_rows + 8, heads_dev * row_width), jnp.float32),
            pltpu.VMEM((REQS, live_rows, 128), jnp.float32),
            pltpu.VMEM((live_rows + 8, channels), jnp.float32),
            pltpu.VMEM((device_count, rows_dev, heads_dev * HEAD_DIM), jnp.float32),
            pltpu.VMEM((HEAD_DIM, STATE), jnp.float32),
            pltpu.VMEM(received.shape, jnp.float32),
            pltpu.SMEM((device_count,), jnp.int32),
            pltpu.SMEM((device_count,), jnp.int32),
        ],
        "mixer",
        flops=1 << 30,
        smem=3,
    )

    theirs = other_core(theirs, chip_count)
    width = out_weight.shape[1]
    total_rows = chip_count * rows_dev
    block = jax.ShapeDtypeStruct((rows_dev, width), jnp.bfloat16)
    part = kernel_call(
        part_kernel,
        jax.ShapeDtypeStruct((2 * rows_dev, width), jnp.float32),
        [mine, out_weight],
        [],
        "sums_part",
        flops=1 << 30,
    )
    first, second = kernel_call(
        functools.partial(first_kernel, rows_dev),
        [block, block],
        [part, theirs, held],
        [],
        "sums_first",
        flops=1 << 30,
    )
    own_sum = stream(first, chip_count)
    other_sum = stream(second, chip_count)
    shares = kernel_call(
        functools.partial(rest_kernel, rows_dev),
        jax.ShapeDtypeStruct((total_rows - 2 * rows_dev, width), jnp.float32),
        [mine, theirs, out_weight, held],
        [],
        "sums_rest",
        flops=1 << 30,
    )

    def onward(at, *arrived):
        top = (at - 2) * rows_dev
        return kernel_call(
            functools.partial(add_kernel, top), block, [shares, *arrived], [], "onward"
        )

    slots = send_slots(half)
    for at in range(2, len(slots) - 1):
        if slots[at][1] == 0:
            own_sum = stream(onward(at, own_sum), chip_count)
        else:
            other_sum = stream(onward(at, other_sum), chip_count)
    crossed = other_core(other_sum, chip_count)
    mixed = onward(len(slots) - 1, own_sum, crossed)
    return (mixed, final_state, final_conv)


def solution(mesh):
    return jax.shard_map(
        body,
        mesh=mesh,
        in_specs=(
            P(("groups", "dp"), None),
            P(None, "dp"),
            P("dp", None),
            P("dp"),
            P("dp"),
            P(None, "dp"),
            P("dp"),
            P("dp"),
            P("dp"),
            P("dp", None),
            P(("groups", "dp"), None, None),
            P(("groups", "dp"), None, None),
            P("groups", None, None),
            P("groups"),
            P("groups"),
        ),
        out_specs=(
            P(("groups", "dp"), None),
            P("groups", "dp", None, None),
            P("groups", None, "dp"),
        ),
        check_vma=False,
    )
```

```python
import functools

import jax
import jax.numpy as jnp
from jax import lax
from jax.experimental import pallas as pl
from jax.experimental.pallas import tpu as pltpu
from jax.sharding import PartitionSpec as P

HEAD_DIM = 128
STATE = 128
CONV = 4
REQS = 2
SPAN = 192
BLK = 64


EPSILON = 1e-05
PER_PEER = 2
VMEM_LIMIT = 16 * 1024 * 1024
VMEM_ALL = 60 * 1024 * 1024


def folded(chip_count):
    return chip_count <= 8


def chip_at(place, chip_count):
    if not folded(chip_count):
        return place
    back = 2 * (chip_count - 1 - place) + 1
    if isinstance(place, int):
        return 2 * place if place < chip_count // 2 else back
    return jnp.where(place < chip_count // 2, 2 * place, back)


def place_of(chip, chip_count):
    if not folded(chip_count):
        return chip
    return jnp.where(chip % 2 == 0, chip // 2, chip_count - 1 - chip // 2)


def stream(array, chip_count):
    pairs = []
    for place in range(chip_count):
        for core in range(2):
            onto = (place + 1 - 2 * core) % chip_count
            pairs.append((2 * chip_at(place, chip_count) + core, 2 * chip_at(onto, chip_count) + core))
    return lax.ppermute(array, "dp", pairs)


def stream_other(array, chip_count):
    pairs = []
    for place in range(chip_count):
        for core in range(2):
            onto = (place + 1 - 2 * core) % chip_count
            pairs.append(
                (2 * chip_at(place, chip_count) + 1 - core, 2 * chip_at(onto, chip_count) + core)
            )
    return lax.ppermute(array, "dp", pairs)


def other_core(array, chip_count):
    return lax.ppermute(array, "dp", [(d, d ^ 1) for d in range(2 * chip_count)])


def kernel_call(kernel, outs, operands, scratch, name, flops=0, smem=0, limit=VMEM_LIMIT):
    several = isinstance(outs, list)
    whole = pl.BlockSpec(memory_space=pltpu.VMEM)
    scalars = pl.BlockSpec(memory_space=pltpu.SMEM)
    return pl.pallas_call(
        kernel,
        out_shape=outs,
        in_specs=[scalars] * smem + [whole] * (len(operands) - smem),
        out_specs=[whole] * len(outs) if several else whole,
        scratch_shapes=scratch,
        compiler_params=pltpu.CompilerParams(vmem_limit_bytes=limit),
        cost_estimate=pl.CostEstimate(flops=flops, bytes_accessed=8 << 20, transcendentals=0),
        name=name,
    )(*operands)


def offer_kernel(entries, my_ref, ids_ref, state_ref, conv_ref, out_ref, slot_s, conv_s, lag_s):
    pool_slots, state_rows, _ = state_ref.shape
    lag_rows = conv_ref.shape[0]
    piece_channels = conv_ref.shape[2]
    receivers = out_ref.shape[0]
    heads_dev = ids_ref.shape[2] // receivers
    first = my_ref[0] * pool_slots
    conv_s[...] = jnp.zeros_like(conv_s)
    conv_s[:, :, :piece_channels] = conv_ref[...].astype(jnp.float32)
    lag_s[...] = jnp.zeros_like(lag_s)

    def one_receiver(receiver, _):
        used = jnp.int32(0)
        for r in range(REQS):
            for h in range(heads_dev):
                for p in range(ids_ref.shape[1]):
                    slot = ids_ref[r, p, receiver * heads_dev + h] - first
                    slot_s[used] = slot
                    held = jnp.logical_and(slot >= 0, slot < pool_slots)
                    used = used + held.astype(jnp.int32)
        for place in range(PER_PEER):
            slot = jnp.clip(slot_s[place], 0, pool_slots - 1)
            out_ref[receiver, place * state_rows : (place + 1) * state_rows, :] = state_ref[slot]
            for lag in range(lag_rows):
                row = 8 * place + lag
                lag_s[receiver, row : row + 1, :] = conv_s[lag, pl.ds(slot, 1), :]
        return 0

    lax.fori_loop(0, receivers, one_receiver, 0)
    out_ref[:, PER_PEER * state_rows :, :] = lag_s[...].astype(out_ref.dtype)


def column_tiles(width, body):
    tile = min(512, width)

    def one_tile(index, _):
        body(pl.ds(pl.multiple_of(index * tile, tile), tile))
        return 0

    lax.fori_loop(0, width // tile, one_tile, 0)


def from_hbm(array):
    return pltpu.with_memory_space_constraint(array, pltpu.HBM)


def load_kernel(*refs):
    count = (len(refs) - 1) // 2
    sems = refs[-1]
    copies = [
        pltpu.make_async_copy(refs[at], refs[count + at], sems.at[at]) for at in range(count)
    ]
    for copy in copies:
        copy.start()
    for copy in copies:
        copy.wait()


def load(*arrays):
    return pl.pallas_call(
        load_kernel,
        out_shape=[jax.ShapeDtypeStruct(a.shape, a.dtype) for a in arrays],
        in_specs=[pl.BlockSpec(memory_space=pltpu.HBM)] * len(arrays),
        out_specs=[pl.BlockSpec(memory_space=pltpu.VMEM)] * len(arrays),
        scratch_shapes=[pltpu.SemaphoreType.DMA((len(arrays),))],
        compiler_params=pltpu.CompilerParams(vmem_limit_bytes=VMEM_LIMIT),
        cost_estimate=pl.CostEstimate(flops=0, bytes_accessed=8 << 20, transcendentals=0),
        name="load",
    )(*[from_hbm(a) for a in arrays])


def stage_kernel(count, *refs):
    block_refs = refs[:count]
    weight_ref, rate_weight_ref, out_ref, joined_s = refs[count:]
    rows = block_refs[0].shape[0]
    width = weight_ref.shape[1]
    for at, block_ref in enumerate(block_refs):
        joined_s[at * rows : (at + 1) * rows, :] = block_ref[...]
    rates = rate_weight_ref.shape[0]
    out_ref[:, width:] = jnp.zeros((out_ref.shape[0], out_ref.shape[1] - width), jnp.float32)
    out_ref[:, width : width + rates] = lax.dot_general(
        joined_s[...],
        rate_weight_ref[...],
        (((1,), (1,)), ((), ())),
        preferred_element_type=jnp.float32,
    )

    def body(columns):
        out_ref[:, columns] = jnp.dot(
            joined_s[...], weight_ref[:, columns], preferred_element_type=jnp.float32
        )

    column_tiles(width, body)


def stage(blocks, weight, rate_weight):
    rows, depth = blocks[0].shape
    total = rows * len(blocks)
    width = weight.shape[1] + 128
    return kernel_call(
        functools.partial(stage_kernel, len(blocks)),
        jax.ShapeDtypeStruct((total, width), jnp.float32),
        [*blocks, weight, rate_weight],
        [pltpu.VMEM((total, depth), jnp.bfloat16)],
        "stage",
        flops=2 * 256 * depth * width,
    )


def early_kernel(count, tile, *refs):
    block_refs = refs[:count]
    weight_ref, rate_weight_ref, out_hbm, held_s, joined_s, out_ref, sems = refs[count:]
    rows = block_refs[0].shape[0]
    width = weight_ref.shape[1]
    lefts = range(0, width, tile)
    loads = [
        pltpu.make_async_copy(
            weight_ref.at[:, pl.ds(left, tile)], held_s.at[:, pl.ds(left, tile)], sems.at[at]
        )
        for at, left in enumerate(lefts)
    ]
    for copy in loads:
        copy.start()
    for at, block_ref in enumerate(block_refs):
        joined_s[at * rows : (at + 1) * rows, :] = block_ref[...]
    rates = rate_weight_ref.shape[0]
    out_ref[:, width:] = jnp.zeros((out_ref.shape[0], out_ref.shape[1] - width), jnp.float32)
    out_ref[:, width : width + rates] = lax.dot_general(
        joined_s[...],
        rate_weight_ref[...],
        (((1,), (1,)), ((), ())),
        preferred_element_type=jnp.float32,
    )
    for left, copy in zip(lefts, loads, strict=True):
        copy.wait()
        out_ref[:, left : left + tile] = jnp.dot(
            joined_s[...], held_s[:, left : left + tile], preferred_element_type=jnp.float32
        )
    store = pltpu.make_async_copy(out_ref, out_hbm, sems.at[len(loads)])
    store.start()
    store.wait()


def early_stage(blocks, weight, rate_weight):
    rows, depth = blocks[0].shape
    count = len(blocks)
    width = weight.shape[1]
    tile = min(256, width)
    whole = pl.BlockSpec(memory_space=pltpu.VMEM)
    hbm = pl.BlockSpec(memory_space=pltpu.HBM)
    return pl.pallas_call(
        functools.partial(early_kernel, count, tile),
        out_shape=pltpu.HBM((rows * count, width + 128), jnp.float32),
        in_specs=[whole] * count + [hbm, whole],
        out_specs=hbm,
        scratch_shapes=[
            pltpu.VMEM((depth, width), jnp.bfloat16),
            pltpu.VMEM((rows * count, depth), jnp.bfloat16),
            pltpu.VMEM((rows * count, width + 128), jnp.float32),
            pltpu.SemaphoreType.DMA((width // tile + 1,)),
        ],
        compiler_params=pltpu.CompilerParams(vmem_limit_bytes=VMEM_LIMIT),
        cost_estimate=pl.CostEstimate(
            flops=2 * 256 * depth * width, bytes_accessed=8 << 20, transcendentals=0
        ),
        name="early_stage",
    )(*blocks, from_hbm(weight), rate_weight)


def part_kernel(mine_ref, weight_ref, out_ref):
    rows = out_ref.shape[0]

    def body(columns):
        out_ref[:, columns] = jnp.dot(
            mine_ref[:rows, :], weight_ref[:, columns], preferred_element_type=jnp.float32
        )

    column_tiles(out_ref.shape[1], body)


def first_kernel(rows, part_ref, theirs_ref, held_ref, first_ref, second_ref):
    def body(columns):
        total = part_ref[: 2 * rows, columns] + jnp.dot(
            theirs_ref[: 2 * rows, :], held_ref[:, columns], preferred_element_type=jnp.float32
        )
        first_ref[:, columns] = total[:rows].astype(first_ref.dtype)
        second_ref[:, columns] = total[rows:].astype(second_ref.dtype)

    column_tiles(held_ref.shape[1], body)


def rest_kernel(rows, mine_ref, theirs_ref, weight_ref, held_ref, out_ref):
    def body(columns):
        total = jnp.dot(
            mine_ref[2 * rows :, :], weight_ref[:, columns], preferred_element_type=jnp.float32
        )
        out_ref[:, columns] = total + jnp.dot(
            theirs_ref[2 * rows :, :], held_ref[:, columns], preferred_element_type=jnp.float32
        )

    column_tiles(held_ref.shape[1], body)


def add_kernel(top, share_ref, *refs):
    out_ref = refs[-1]
    total = share_ref[top : top + out_ref.shape[0], :]
    for arrived_ref in refs[:-1]:
        total = total + arrived_ref[...].astype(jnp.float32)
    out_ref[...] = total.astype(out_ref.dtype)


def gather_slots(half):
    slots = [(0, 0), (0, 1)]
    for step in range(1, half):
        slots += [(-step, 0), (-step, 1), (step, 1), (step, 0)]
    return slots + [(-half, 0), (half, 1)]


def send_slots(half):
    slots = []
    for step in range(half, 0, -1):
        slots.append((step, 0))
        if step > 1:
            slots.append((step - 1, 1))
    return slots + [(0, 0)]


def mix_kernel(sizes, scalar_ref, page_id_ref, number_ref, page_ref, *rest):
    heads_dev, piece_count, pool_slots, stages = sizes
    taps_ref, conv_bias_ref, gain_ref = rest[:3]
    stage_refs, rest = rest[3 : 3 + stages], rest[3 + stages :]
    conv_bias = conv_bias_ref[...].astype(jnp.float32).reshape(1, -1)
    gains = gain_ref[...].astype(jnp.float32).reshape(1, -1)
    state_ref, conv_ref, mine_ref, theirs_ref = rest[:4]
    placed_s, rows_s, rate_s, input_s, normed_s, initial_s, page_s, inverse_s, used_s = rest[4:]
    blocks, rows_dev, _ = placed_s.shape
    live_rows = SPAN - BLK
    lead = 8
    state_rows = HEAD_DIM // piece_count
    channels = HEAD_DIM + 2 * STATE
    row_width = HEAD_DIM + channels
    piece_channels = channels // piece_count
    blocks_req = blocks // REQS

    chip_count = blocks // 2
    half = chip_count // 2
    my_index = scalar_ref[0]
    core = my_index % 2
    place = place_of(my_index // 2, chip_count)
    owner_at = 1 + REQS

    def device_at(distance, flip):
        onto = place + jnp.where(core == 0, distance, -distance) + chip_count
        chip = chip_at(lax.rem(onto, chip_count), chip_count)
        return 2 * chip + (core if flip == 0 else 1 - core)

    def clear(holder, _):
        used_s[holder] = 0
        return 0

    lax.fori_loop(0, blocks, clear, 0)

    def invert(block, _):
        inverse_s[scalar_ref[owner_at + block]] = block
        return 0

    lax.fori_loop(0, blocks, invert, 0)

    page_s[...] = page_ref[...].astype(jnp.float32)

    pieces_of = []
    for r in range(REQS):
        for j in range(blocks_req):
            start = j * rows_dev
            low, high = max(start, BLK), start + rows_dev
            if high > BLK:
                pieces_of.append((r, r * blocks_req + j, low - start, low - BLK, high - BLK))
    slots = gather_slots(half)
    at = 0
    for stage_ref in stage_refs:
        for top in range(0, stage_ref.shape[0], rows_dev):
            placed_s[device_at(*slots[at])] = stage_ref[top : top + rows_dev, :]
            at += 1
    for r, block, skipped, low, high in pieces_of:
        rows_s[r, lead + low : lead + high, :] = placed_s[block, skipped:, : rows_s.shape[2]]
        rate_s[r, low:high, :] = placed_s[block, skipped:, rows_s.shape[2] :]
    normed_s[...] = jnp.zeros_like(normed_s)

    wide = (live_rows, 128)
    later = lax.broadcasted_iota(jnp.int32, (live_rows, live_rows), 0)
    sooner = lax.broadcasted_iota(jnp.int32, (live_rows, live_rows), 1)
    causal = later >= sooner
    ones = causal.astype(jnp.float32)
    position = lax.broadcasted_iota(jnp.int32, wide, 0) + BLK
    lead_position = lax.broadcasted_iota(jnp.int32, (live_rows + lead, channels), 0) + BLK - lead
    spread_row = lax.broadcasted_iota(jnp.int32, (piece_count * 128, channels), 0)
    spread_col = lax.broadcasted_iota(jnp.int32, (piece_count * 128, channels), 1)
    spread = (
        ((spread_row // 128) * piece_channels + spread_row % 128 == spread_col)
        & (spread_row % 128 < piece_channels)
    ).astype(jnp.bfloat16)

    lane = lax.broadcasted_iota(jnp.int32, (1, 128), 1)
    bias_lanes = jnp.zeros((1, 128), jnp.float32)
    decay_lanes = jnp.zeros((1, 128), jnp.float32)
    for h in range(heads_dev):
        bias_lanes = jnp.where(lane == h, number_ref[h], bias_lanes)
        decay_lanes = jnp.where(lane == h, number_ref[heads_dev + h], decay_lanes)

    for r in range(REQS):
        live_start = scalar_ref[1 + r] * BLK
        live = position >= live_start
        rate = rate_s[r] + bias_lanes
        step = jnp.where(live, jax.nn.softplus(rate), 0.0)
        drop = -decay_lanes * step
        total = jnp.dot(
            ones, drop, preferred_element_type=jnp.float32, precision=lax.Precision.HIGHEST
        )
        total_t = total.T
        step_t = step.T
        from_start = jnp.exp(total)
        span_tail = total[live_rows - 1 : live_rows, :]
        to_end = jnp.exp(span_tail - total) * step
        kept = jnp.exp(span_tail)
        for h in range(heads_dev):
            lags = []
            for p in range(piece_count):
                page = page_id_ref[r, p, my_index * heads_dev + h]
                holder = lax.div(page, pool_slots)
                rank = used_s[holder]
                used_s[holder] = rank + 1
                state_at = pl.ds(pl.multiple_of(rank * state_rows, state_rows), state_rows)
                lag_at = pl.ds(pl.multiple_of(PER_PEER * state_rows + 8 * rank, 8), 8)
                initial_s[p * state_rows : (p + 1) * state_rows, :] = page_s[holder, state_at, :]
                lags.append(page_s[holder, lag_at, :].astype(jnp.bfloat16))
            initial = initial_s[...]
            lag_lanes = jnp.concatenate(lags, axis=1)
            cached = jnp.dot(lag_lanes, spread, preferred_element_type=jnp.float32)
            first = h * row_width
            c0 = h * channels
            raw = rows_s[r, :, first + HEAD_DIM : first + row_width]
            raw = raw.astype(jnp.bfloat16).astype(jnp.float32)
            inputs = jnp.where(lead_position >= live_start, raw, 0.0)
            for lag in range(CONV - 1):
                inputs = jnp.where(
                    lead_position == live_start - (CONV - 1) + lag,
                    cached[lag : lag + 1, :],
                    inputs,
                )
            input_s[...] = inputs
            conv_ref[r, :, c0 : c0 + channels] = rows_s[
                r,
                live_rows + lead - (CONV - 1) : live_rows + lead,
                first + HEAD_DIM : first + row_width,
            ].astype(jnp.bfloat16)
            summed = jnp.broadcast_to(
                conv_bias[:, c0 : c0 + channels], (live_rows, channels)
            )
            for tap in range(CONV):
                begin = lead - (CONV - 1) + tap
                summed = summed + taps_ref[tap : tap + 1, c0 : c0 + channels].astype(
                    jnp.float32
                ) * input_s[begin : begin + live_rows, :]
            mixed_in = (summed * jax.nn.sigmoid(summed)).astype(jnp.bfloat16)
            x_part = mixed_in[:, :HEAD_DIM]
            b_part = mixed_in[:, HEAD_DIM : HEAD_DIM + STATE]
            c_part = mixed_in[:, HEAD_DIM + STATE :]
            x_float = x_part.astype(jnp.float32)
            last = (((1,), (1,)), ((), ()))
            scores = lax.dot_general(c_part, b_part, last, preferred_element_type=jnp.float32)
            gaps = jnp.where(causal, total[:, h : h + 1] - total_t[h : h + 1, :], 0.0)
            weights = jnp.where(causal, jnp.exp(gaps) * scores * step_t[h : h + 1, :], 0.0)
            outputs = jnp.dot(
                weights.astype(jnp.bfloat16), x_part, preferred_element_type=jnp.float32
            )
            reader = (c_part.astype(jnp.float32) * from_start[:, h : h + 1]).astype(jnp.bfloat16)
            outputs = outputs + lax.dot_general(
                reader, initial.astype(jnp.bfloat16), last, preferred_element_type=jnp.float32
            )
            outputs = outputs + number_ref[2 * heads_dev + h] * x_float
            entering = (x_float * to_end[:, h : h + 1]).astype(jnp.bfloat16)
            added = lax.dot_general(
                entering,
                b_part,
                (((0,), (0,)), ((), ())),
                preferred_element_type=jnp.float32,
            )
            state_ref[r, h] = kept[:, h : h + 1] * initial + added
            gate = rows_s[r, lead:, first : first + HEAD_DIM]
            gate = gate.astype(jnp.bfloat16).astype(jnp.float32)
            gated = outputs * (gate * jax.nn.sigmoid(gate))
            scale = lax.rsqrt(jnp.mean(gated * gated, axis=1, keepdims=True) + EPSILON)
            gain = gains[:, h * HEAD_DIM : (h + 1) * HEAD_DIM]
            normed = jnp.where(live, gated * scale * gain, 0.0)
            for rr, block, skipped, low, high in pieces_of:
                if rr == r:
                    normed_s[block, skipped:, h * HEAD_DIM : (h + 1) * HEAD_DIM] = normed[low:high]

    for at, (distance, flip) in enumerate(send_slots(half)):
        rows = slice(at * rows_dev, (at + 1) * rows_dev)
        mine_ref[rows, :] = normed_s[inverse_s[device_at(distance, flip)]].astype(jnp.bfloat16)
        theirs_ref[rows, :] = normed_s[inverse_s[device_at(-distance, 1 - flip)]].astype(
            jnp.bfloat16
        )


def body(
    hidden,
    in_weight,
    dt_weight,
    dt_bias,
    decay_rate,
    conv_weight,
    conv_bias,
    skip,
    norm_gain,
    out_weight,
    state_pool,
    conv_pool,
    hit_page,
    prefix_blocks,
    owners,
):
    device_count = lax.axis_size("dp")
    my_index = lax.axis_index("dp").astype(jnp.int32).reshape(1)
    heads_dev = dt_weight.shape[0]
    piece_count = hit_page.shape[2]
    row_width = 2 * HEAD_DIM + 2 * STATE
    channels = HEAD_DIM + 2 * STATE
    rows_dev = hidden.shape[0]
    pool_slots, state_rows, _ = state_pool.shape
    chip_count = device_count // 2
    half = chip_count // 2
    page_ids = jnp.swapaxes(hit_page, 1, 2)

    other_type = other_core(hidden, chip_count)
    page_rows = PER_PEER * state_rows + 8 * PER_PEER
    entries = REQS * heads_dev * piece_count
    offered = kernel_call(
        functools.partial(offer_kernel, entries),
        jax.ShapeDtypeStruct((device_count, page_rows, STATE), state_pool.dtype),
        [
            my_index,
            page_ids,
            from_hbm(state_pool),
            from_hbm(jnp.swapaxes(conv_pool, 0, 1)),
        ],
        [
            pltpu.SMEM((entries + 1,), jnp.int32),
            pltpu.VMEM((CONV - 1, pool_slots, STATE), jnp.float32),
            pltpu.VMEM((device_count, 8 * PER_PEER, STATE), jnp.float32),
        ],
        "offer_pages",
        smem=2,
        limit=VMEM_ALL,
    )
    own_type = stream(hidden, chip_count)
    first_other = other_type
    other_type = stream_other(hidden, chip_count)
    scalars = jnp.concatenate([my_index, prefix_blocks, owners])
    numbers = jnp.concatenate([dt_bias, decay_rate, skip])
    offered, own_type, other_type, scalars, numbers, held = lax.optimization_barrier(
        (offered, own_type, other_type, scalars, numbers, out_weight)
    )
    received = lax.all_to_all(offered, "dp", split_axis=0, concat_axis=0, tiled=True)
    held = other_core(held, chip_count)
    blocks = [from_hbm(hidden), first_other, own_type, other_type]
    blocks += [other_core(own_type, chip_count), other_core(other_type, chip_count)]
    early = early_stage(blocks, in_weight, from_hbm(dt_weight))
    pending = []
    for step in range(2, half):
        own_type = stream(own_type, chip_count)
        other_type = stream(other_type, chip_count)
        if step == 2:
            own_type, early = lax.optimization_barrier((own_type, early))
            staged = [from_hbm(early)]
            received, weight_here, rates_here = lax.optimization_barrier(
                (received, in_weight, dt_weight)
            )
            weight_here, rates_here = load(weight_here, rates_here)
        if step == half - 1:
            own_type, weight_here = lax.optimization_barrier((own_type, weight_here))
        pending += [
            own_type,
            other_type,
            other_core(own_type, chip_count),
            other_core(other_type, chip_count),
        ]
        if len(pending) >= max(4, half) and step < half - 1:
            staged.append(stage(pending, weight_here, rates_here))
            pending = []
    own_type = stream(own_type, chip_count)
    last = [own_type, other_core(own_type, chip_count)]
    staged.append(stage(pending + last, weight_here, rates_here))

    live_rows = SPAN - BLK
    normed_rows = jax.ShapeDtypeStruct((chip_count * rows_dev, heads_dev * HEAD_DIM), jnp.bfloat16)
    final_state, final_conv, mine, theirs = kernel_call(
        functools.partial(mix_kernel, (heads_dev, piece_count, pool_slots, len(staged))),
        [
            jax.ShapeDtypeStruct((REQS, heads_dev, HEAD_DIM, STATE), jnp.float32),
            jax.ShapeDtypeStruct((REQS, CONV - 1, heads_dev * channels), jnp.bfloat16),
            normed_rows,
            normed_rows,
        ],
        [
            scalars,
            page_ids,
            numbers,
            received,
            conv_weight,
            conv_bias,
            norm_gain,
            *staged,
        ],
        [
            pltpu.VMEM((device_count, rows_dev, heads_dev * row_width + 128), jnp.float32),
            pltpu.VMEM((REQS, live_rows + 8, heads_dev * row_width), jnp.float32),
            pltpu.VMEM((REQS, live_rows, 128), jnp.float32),
            pltpu.VMEM((live_rows + 8, channels), jnp.float32),
            pltpu.VMEM((device_count, rows_dev, heads_dev * HEAD_DIM), jnp.float32),
            pltpu.VMEM((HEAD_DIM, STATE), jnp.float32),
            pltpu.VMEM(received.shape, jnp.float32),
            pltpu.SMEM((device_count,), jnp.int32),
            pltpu.SMEM((device_count,), jnp.int32),
        ],
        "mixer",
        flops=1 << 30,
        smem=3,
    )

    theirs = other_core(theirs, chip_count)
    width = out_weight.shape[1]
    total_rows = chip_count * rows_dev
    block = jax.ShapeDtypeStruct((rows_dev, width), jnp.bfloat16)
    part = kernel_call(
        part_kernel,
        jax.ShapeDtypeStruct((2 * rows_dev, width), jnp.float32),
        [mine, out_weight],
        [],
        "sums_part",
        flops=1 << 30,
    )
    first, second = kernel_call(
        functools.partial(first_kernel, rows_dev),
        [block, block],
        [part, theirs, held],
        [],
        "sums_first",
        flops=1 << 30,
    )
    own_sum = stream(first, chip_count)
    other_sum = stream(second, chip_count)
    shares = kernel_call(
        functools.partial(rest_kernel, rows_dev),
        jax.ShapeDtypeStruct((total_rows - 2 * rows_dev, width), jnp.float32),
        [mine, theirs, out_weight, held],
        [],
        "sums_rest",
        flops=1 << 30,
    )

    def onward(at, *arrived):
        top = (at - 2) * rows_dev
        return kernel_call(
            functools.partial(add_kernel, top), block, [shares, *arrived], [], "onward"
        )

    slots = send_slots(half)
    for at in range(2, len(slots) - 1):
        if slots[at][1] == 0:
            own_sum = stream(onward(at, own_sum), chip_count)
        else:
            other_sum = stream(onward(at, other_sum), chip_count)
    crossed = other_core(other_sum, chip_count)
    mixed = onward(len(slots) - 1, own_sum, crossed)
    return (mixed, final_state, final_conv)


def solution(mesh):
    return jax.shard_map(
        body,
        mesh=mesh,
        in_specs=(
            P(("groups", "dp"), None),
            P(None, "dp"),
            P("dp", None),
            P("dp"),
            P("dp"),
            P(None, "dp"),
            P("dp"),
            P("dp"),
            P("dp"),
            P("dp", None),
            P(("groups", "dp"), None, None),
            P(("groups", "dp"), None, None),
            P("groups", None, None),
            P("groups"),
            P("groups"),
        ),
        out_specs=(
            P(("groups", "dp"), None),
            P("groups", "dp", None, None),
            P("groups", None, "dp"),
        ),
        check_vma=False,
    )
```

```python
import functools

import jax
import jax.numpy as jnp
from jax import lax
from jax.experimental import pallas as pl
from jax.experimental.pallas import tpu as pltpu
from jax.sharding import PartitionSpec as P

HEAD_DIM = 128
STATE = 128
CONV = 4
REQS = 2
SPAN = 192
BLK = 64


EPSILON = 1e-05
PER_PEER = 2
VMEM_LIMIT = 16 * 1024 * 1024
VMEM_ALL = 60 * 1024 * 1024


def folded(chip_count):
    return chip_count <= 8


def chip_at(place, chip_count):
    if not folded(chip_count):
        return place
    back = 2 * (chip_count - 1 - place) + 1
    if isinstance(place, int):
        return 2 * place if place < chip_count // 2 else back
    return jnp.where(place < chip_count // 2, 2 * place, back)


def place_of(chip, chip_count):
    if not folded(chip_count):
        return chip
    return jnp.where(chip % 2 == 0, chip // 2, chip_count - 1 - chip // 2)


def stream(array, chip_count):
    pairs = []
    for place in range(chip_count):
        for core in range(2):
            onto = (place + 1 - 2 * core) % chip_count
            pairs.append((2 * chip_at(place, chip_count) + core, 2 * chip_at(onto, chip_count) + core))
    return lax.ppermute(array, "dp", pairs)


def stream_other(array, chip_count):
    pairs = []
    for place in range(chip_count):
        for core in range(2):
            onto = (place + 1 - 2 * core) % chip_count
            pairs.append(
                (2 * chip_at(place, chip_count) + 1 - core, 2 * chip_at(onto, chip_count) + core)
            )
    return lax.ppermute(array, "dp", pairs)


def other_core(array, chip_count):
    return lax.ppermute(array, "dp", [(d, d ^ 1) for d in range(2 * chip_count)])


def kernel_call(kernel, outs, operands, scratch, name, flops=0, smem=0, limit=VMEM_LIMIT):
    several = isinstance(outs, list)
    whole = pl.BlockSpec(memory_space=pltpu.VMEM)
    scalars = pl.BlockSpec(memory_space=pltpu.SMEM)
    return pl.pallas_call(
        kernel,
        out_shape=outs,
        in_specs=[scalars] * smem + [whole] * (len(operands) - smem),
        out_specs=[whole] * len(outs) if several else whole,
        scratch_shapes=scratch,
        compiler_params=pltpu.CompilerParams(vmem_limit_bytes=limit),
        cost_estimate=pl.CostEstimate(flops=flops, bytes_accessed=8 << 20, transcendentals=0),
        name=name,
    )(*operands)


def offer_kernel(entries, my_ref, ids_ref, state_ref, conv_ref, out_ref, slot_s, conv_s, lag_s):
    pool_slots, state_rows, _ = state_ref.shape
    lag_rows = conv_ref.shape[0]
    piece_channels = conv_ref.shape[2]
    receivers = out_ref.shape[0]
    heads_dev = ids_ref.shape[2] // receivers
    first = my_ref[0] * pool_slots
    conv_s[...] = jnp.zeros_like(conv_s)
    conv_s[:, :, :piece_channels] = conv_ref[...].astype(jnp.float32)
    lag_s[...] = jnp.zeros_like(lag_s)

    def one_receiver(receiver, _):
        used = jnp.int32(0)
        for r in range(REQS):
            for h in range(heads_dev):
                for p in range(ids_ref.shape[1]):
                    slot = ids_ref[r, p, receiver * heads_dev + h] - first
                    slot_s[used] = slot
                    held = jnp.logical_and(slot >= 0, slot < pool_slots)
                    used = used + held.astype(jnp.int32)
        for place in range(PER_PEER):
            slot = jnp.clip(slot_s[place], 0, pool_slots - 1)
            out_ref[receiver, place * state_rows : (place + 1) * state_rows, :] = state_ref[slot]
            for lag in range(lag_rows):
                row = 8 * place + lag
                lag_s[receiver, row : row + 1, :] = conv_s[lag, pl.ds(slot, 1), :]
        return 0

    lax.fori_loop(0, receivers, one_receiver, 0)
    out_ref[:, PER_PEER * state_rows :, :] = lag_s[...].astype(out_ref.dtype)


def column_tiles(width, body):
    tile = min(512, width)

    def one_tile(index, _):
        body(pl.ds(pl.multiple_of(index * tile, tile), tile))
        return 0

    lax.fori_loop(0, width // tile, one_tile, 0)


def from_hbm(array):
    return pltpu.with_memory_space_constraint(array, pltpu.HBM)


def load_kernel(*refs):
    count = (len(refs) - 1) // 2
    sems = refs[-1]
    copies = [
        pltpu.make_async_copy(refs[at], refs[count + at], sems.at[at]) for at in range(count)
    ]
    for copy in copies:
        copy.start()
    for copy in copies:
        copy.wait()


def load(*arrays):
    return pl.pallas_call(
        load_kernel,
        out_shape=[jax.ShapeDtypeStruct(a.shape, a.dtype) for a in arrays],
        in_specs=[pl.BlockSpec(memory_space=pltpu.HBM)] * len(arrays),
        out_specs=[pl.BlockSpec(memory_space=pltpu.VMEM)] * len(arrays),
        scratch_shapes=[pltpu.SemaphoreType.DMA((len(arrays),))],
        compiler_params=pltpu.CompilerParams(vmem_limit_bytes=VMEM_LIMIT),
        cost_estimate=pl.CostEstimate(flops=0, bytes_accessed=8 << 20, transcendentals=0),
        name="load",
    )(*[from_hbm(a) for a in arrays])


def stage_kernel(count, *refs):
    block_refs = refs[:count]
    weight_ref, rate_weight_ref, out_ref, joined_s = refs[count:]
    rows = block_refs[0].shape[0]
    width = weight_ref.shape[1]
    for at, block_ref in enumerate(block_refs):
        joined_s[at * rows : (at + 1) * rows, :] = block_ref[...]
    rates = rate_weight_ref.shape[0]
    out_ref[:, width:] = jnp.zeros((out_ref.shape[0], out_ref.shape[1] - width), jnp.float32)
    out_ref[:, width : width + rates] = lax.dot_general(
        joined_s[...],
        rate_weight_ref[...],
        (((1,), (1,)), ((), ())),
        preferred_element_type=jnp.float32,
    )

    def body(columns):
        out_ref[:, columns] = jnp.dot(
            joined_s[...], weight_ref[:, columns], preferred_element_type=jnp.float32
        )

    column_tiles(width, body)


def stage(blocks, weight, rate_weight):
    rows, depth = blocks[0].shape
    total = rows * len(blocks)
    width = weight.shape[1] + 128
    return kernel_call(
        functools.partial(stage_kernel, len(blocks)),
        jax.ShapeDtypeStruct((total, width), jnp.float32),
        [*blocks, weight, rate_weight],
        [pltpu.VMEM((total, depth), jnp.bfloat16)],
        "stage",
        flops=2 * 256 * depth * width,
    )


def early_kernel(count, tile, *refs):
    block_refs = refs[:count]
    weight_ref, rate_weight_ref, out_hbm, held_s, joined_s, out_ref, sems = refs[count:]
    rows = block_refs[0].shape[0]
    width = weight_ref.shape[1]
    lefts = range(0, width, tile)
    loads = [
        pltpu.make_async_copy(
            weight_ref.at[:, pl.ds(left, tile)], held_s.at[:, pl.ds(left, tile)], sems.at[at]
        )
        for at, left in enumerate(lefts)
    ]
    for copy in loads:
        copy.start()
    for at, block_ref in enumerate(block_refs):
        joined_s[at * rows : (at + 1) * rows, :] = block_ref[...]
    rates = rate_weight_ref.shape[0]
    out_ref[:, width:] = jnp.zeros((out_ref.shape[0], out_ref.shape[1] - width), jnp.float32)
    out_ref[:, width : width + rates] = lax.dot_general(
        joined_s[...],
        rate_weight_ref[...],
        (((1,), (1,)), ((), ())),
        preferred_element_type=jnp.float32,
    )
    for left, copy in zip(lefts, loads, strict=True):
        copy.wait()
        out_ref[:, left : left + tile] = jnp.dot(
            joined_s[...], held_s[:, left : left + tile], preferred_element_type=jnp.float32
        )
    store = pltpu.make_async_copy(out_ref, out_hbm, sems.at[len(loads)])
    store.start()
    store.wait()


def early_stage(blocks, weight, rate_weight):
    rows, depth = blocks[0].shape
    count = len(blocks)
    width = weight.shape[1]
    tile = min(256, width)
    whole = pl.BlockSpec(memory_space=pltpu.VMEM)
    hbm = pl.BlockSpec(memory_space=pltpu.HBM)
    return pl.pallas_call(
        functools.partial(early_kernel, count, tile),
        out_shape=pltpu.HBM((rows * count, width + 128), jnp.float32),
        in_specs=[whole] * count + [hbm, whole],
        out_specs=hbm,
        scratch_shapes=[
            pltpu.VMEM((depth, width), jnp.bfloat16),
            pltpu.VMEM((rows * count, depth), jnp.bfloat16),
            pltpu.VMEM((rows * count, width + 128), jnp.float32),
            pltpu.SemaphoreType.DMA((width // tile + 1,)),
        ],
        compiler_params=pltpu.CompilerParams(vmem_limit_bytes=VMEM_LIMIT),
        cost_estimate=pl.CostEstimate(
            flops=2 * 256 * depth * width, bytes_accessed=8 << 20, transcendentals=0
        ),
        name="early_stage",
    )(*blocks, from_hbm(weight), rate_weight)


def part_kernel(mine_ref, weight_ref, out_ref):
    rows = out_ref.shape[0]

    def body(columns):
        out_ref[:, columns] = jnp.dot(
            mine_ref[:rows, :], weight_ref[:, columns], preferred_element_type=jnp.float32
        )

    column_tiles(out_ref.shape[1], body)


def first_kernel(rows, part_ref, theirs_ref, held_ref, first_ref, second_ref):
    def body(columns):
        total = part_ref[: 2 * rows, columns] + jnp.dot(
            theirs_ref[: 2 * rows, :], held_ref[:, columns], preferred_element_type=jnp.float32
        )
        first_ref[:, columns] = total[:rows].astype(first_ref.dtype)
        second_ref[:, columns] = total[rows:].astype(second_ref.dtype)

    column_tiles(held_ref.shape[1], body)


def rest_kernel(rows, mine_ref, theirs_ref, weight_ref, held_ref, out_ref):
    def body(columns):
        total = jnp.dot(
            mine_ref[2 * rows :, :], weight_ref[:, columns], preferred_element_type=jnp.float32
        )
        out_ref[:, columns] = total + jnp.dot(
            theirs_ref[2 * rows :, :], held_ref[:, columns], preferred_element_type=jnp.float32
        )

    column_tiles(held_ref.shape[1], body)


def add_kernel(top, share_ref, *refs):
    out_ref = refs[-1]
    total = share_ref[top : top + out_ref.shape[0], :]
    for arrived_ref in refs[:-1]:
        total = total + arrived_ref[...].astype(jnp.float32)
    out_ref[...] = total.astype(out_ref.dtype)


def gather_slots(half):
    slots = [(0, 0), (0, 1)]
    for step in range(1, half):
        slots += [(-step, 0), (-step, 1), (step, 1), (step, 0)]
    return slots + [(-half, 0), (half, 1)]


def send_slots(half):
    slots = []
    for step in range(half, 0, -1):
        slots.append((step, 0))
        if step > 1:
            slots.append((step - 1, 1))
    return slots + [(0, 0)]


def mix_kernel(sizes, scalar_ref, page_id_ref, number_ref, page_ref, *rest):
    heads_dev, piece_count, pool_slots, stages = sizes
    taps_ref, conv_bias_ref, gain_ref = rest[:3]
    stage_refs, rest = rest[3 : 3 + stages], rest[3 + stages :]
    conv_bias = conv_bias_ref[...].astype(jnp.float32).reshape(1, -1)
    gains = gain_ref[...].astype(jnp.float32).reshape(1, -1)
    state_ref, conv_ref, mine_ref, theirs_ref = rest[:4]
    placed_s, rows_s, rate_s, input_s, normed_s, initial_s, page_s, inverse_s, used_s = rest[4:]
    blocks, rows_dev, _ = placed_s.shape
    live_rows = SPAN - BLK
    lead = 8
    state_rows = HEAD_DIM // piece_count
    channels = HEAD_DIM + 2 * STATE
    row_width = HEAD_DIM + channels
    piece_channels = channels // piece_count
    blocks_req = blocks // REQS

    chip_count = blocks // 2
    half = chip_count // 2
    my_index = scalar_ref[0]
    core = my_index % 2
    place = place_of(my_index // 2, chip_count)
    owner_at = 1 + REQS

    def device_at(distance, flip):
        onto = place + jnp.where(core == 0, distance, -distance) + chip_count
        chip = chip_at(lax.rem(onto, chip_count), chip_count)
        return 2 * chip + (core if flip == 0 else 1 - core)

    def clear(holder, _):
        used_s[holder] = 0
        return 0

    lax.fori_loop(0, blocks, clear, 0)

    def invert(block, _):
        inverse_s[scalar_ref[owner_at + block]] = block
        return 0

    lax.fori_loop(0, blocks, invert, 0)

    page_s[...] = page_ref[...].astype(jnp.float32)

    pieces_of = []
    for r in range(REQS):
        for j in range(blocks_req):
            start = j * rows_dev
            low, high = max(start, BLK), start + rows_dev
            if high > BLK:
                pieces_of.append((r, r * blocks_req + j, low - start, low - BLK, high - BLK))
    slots = gather_slots(half)
    at = 0
    for stage_ref in stage_refs:
        for top in range(0, stage_ref.shape[0], rows_dev):
            placed_s[device_at(*slots[at])] = stage_ref[top : top + rows_dev, :]
            at += 1
    for r, block, skipped, low, high in pieces_of:
        rows_s[r, lead + low : lead + high, :] = placed_s[block, skipped:, : rows_s.shape[2]]
        rate_s[r, low:high, :] = placed_s[block, skipped:, rows_s.shape[2] :]
    normed_s[...] = jnp.zeros_like(normed_s)

    wide = (live_rows, 128)
    later = lax.broadcasted_iota(jnp.int32, (live_rows, live_rows), 0)
    sooner = lax.broadcasted_iota(jnp.int32, (live_rows, live_rows), 1)
    causal = later >= sooner
    ones = causal.astype(jnp.float32)
    position = lax.broadcasted_iota(jnp.int32, wide, 0) + BLK
    lead_position = lax.broadcasted_iota(jnp.int32, (live_rows + lead, channels), 0) + BLK - lead
    spread_row = lax.broadcasted_iota(jnp.int32, (piece_count * 128, channels), 0)
    spread_col = lax.broadcasted_iota(jnp.int32, (piece_count * 128, channels), 1)
    spread = (
        ((spread_row // 128) * piece_channels + spread_row % 128 == spread_col)
        & (spread_row % 128 < piece_channels)
    ).astype(jnp.bfloat16)

    lane = lax.broadcasted_iota(jnp.int32, (1, 128), 1)
    bias_lanes = jnp.zeros((1, 128), jnp.float32)
    decay_lanes = jnp.zeros((1, 128), jnp.float32)
    for h in range(heads_dev):
        bias_lanes = jnp.where(lane == h, number_ref[h], bias_lanes)
        decay_lanes = jnp.where(lane == h, number_ref[heads_dev + h], decay_lanes)

    for r in range(REQS):
        live_start = scalar_ref[1 + r] * BLK
        live = position >= live_start
        rate = rate_s[r] + bias_lanes
        step = jnp.where(live, jax.nn.softplus(rate), 0.0)
        drop = -decay_lanes * step
        total = jnp.dot(
            ones, drop, preferred_element_type=jnp.float32, precision=lax.Precision.HIGHEST
        )
        total_t = total.T
        step_t = step.T
        from_start = jnp.exp(total)
        span_tail = total[live_rows - 1 : live_rows, :]
        to_end = jnp.exp(span_tail - total) * step
        kept = jnp.exp(span_tail)
        for h in range(heads_dev):
            lags = []
            for p in range(piece_count):
                page = page_id_ref[r, p, my_index * heads_dev + h]
                holder = lax.div(page, pool_slots)
                rank = used_s[holder]
                used_s[holder] = rank + 1
                state_at = pl.ds(pl.multiple_of(rank * state_rows, state_rows), state_rows)
                lag_at = pl.ds(pl.multiple_of(PER_PEER * state_rows + 8 * rank, 8), 8)
                initial_s[p * state_rows : (p + 1) * state_rows, :] = page_s[holder, state_at, :]
                lags.append(page_s[holder, lag_at, :].astype(jnp.bfloat16))
            initial = initial_s[...]
            lag_lanes = jnp.concatenate(lags, axis=1)
            cached = jnp.dot(lag_lanes, spread, preferred_element_type=jnp.float32)
            first = h * row_width
            c0 = h * channels
            raw = rows_s[r, :, first + HEAD_DIM : first + row_width]
            raw = raw.astype(jnp.bfloat16).astype(jnp.float32)
            inputs = jnp.where(lead_position >= live_start, raw, 0.0)
            for lag in range(CONV - 1):
                inputs = jnp.where(
                    lead_position == live_start - (CONV - 1) + lag,
                    cached[lag : lag + 1, :],
                    inputs,
                )
            input_s[...] = inputs
            conv_ref[r, :, c0 : c0 + channels] = rows_s[
                r,
                live_rows + lead - (CONV - 1) : live_rows + lead,
                first + HEAD_DIM : first + row_width,
            ].astype(jnp.bfloat16)
            summed = jnp.broadcast_to(
                conv_bias[:, c0 : c0 + channels], (live_rows, channels)
            )
            for tap in range(CONV):
                begin = lead - (CONV - 1) + tap
                summed = summed + taps_ref[tap : tap + 1, c0 : c0 + channels].astype(
                    jnp.float32
                ) * input_s[begin : begin + live_rows, :]
            mixed_in = (summed * jax.nn.sigmoid(summed)).astype(jnp.bfloat16)
            x_part = mixed_in[:, :HEAD_DIM]
            b_part = mixed_in[:, HEAD_DIM : HEAD_DIM + STATE]
            c_part = mixed_in[:, HEAD_DIM + STATE :]
            x_float = x_part.astype(jnp.float32)
            last = (((1,), (1,)), ((), ()))
            scores = lax.dot_general(c_part, b_part, last, preferred_element_type=jnp.float32)
            gaps = jnp.where(causal, total[:, h : h + 1] - total_t[h : h + 1, :], 0.0)
            weights = jnp.where(causal, jnp.exp(gaps) * scores * step_t[h : h + 1, :], 0.0)
            outputs = jnp.dot(
                weights.astype(jnp.bfloat16), x_part, preferred_element_type=jnp.float32
            )
            reader = (c_part.astype(jnp.float32) * from_start[:, h : h + 1]).astype(jnp.bfloat16)
            outputs = outputs + lax.dot_general(
                reader, initial.astype(jnp.bfloat16), last, preferred_element_type=jnp.float32
            )
            outputs = outputs + number_ref[2 * heads_dev + h] * x_float
            entering = (x_float * to_end[:, h : h + 1]).astype(jnp.bfloat16)
            added = lax.dot_general(
                entering,
                b_part,
                (((0,), (0,)), ((), ())),
                preferred_element_type=jnp.float32,
            )
            state_ref[r, h] = kept[:, h : h + 1] * initial + added
            gate = rows_s[r, lead:, first : first + HEAD_DIM]
            gate = gate.astype(jnp.bfloat16).astype(jnp.float32)
            gated = outputs * (gate * jax.nn.sigmoid(gate))
            scale = lax.rsqrt(jnp.mean(gated * gated, axis=1, keepdims=True) + EPSILON)
            gain = gains[:, h * HEAD_DIM : (h + 1) * HEAD_DIM]
            normed = jnp.where(live, gated * scale * gain, 0.0)
            for rr, block, skipped, low, high in pieces_of:
                if rr == r:
                    normed_s[block, skipped:, h * HEAD_DIM : (h + 1) * HEAD_DIM] = normed[low:high]

    for at, (distance, flip) in enumerate(send_slots(half)):
        rows = slice(at * rows_dev, (at + 1) * rows_dev)
        mine_ref[rows, :] = normed_s[inverse_s[device_at(distance, flip)]].astype(jnp.bfloat16)
        theirs_ref[rows, :] = normed_s[inverse_s[device_at(-distance, 1 - flip)]].astype(
            jnp.bfloat16
        )


def body(
    hidden,
    in_weight,
    dt_weight,
    dt_bias,
    decay_rate,
    conv_weight,
    conv_bias,
    skip,
    norm_gain,
    out_weight,
    state_pool,
    conv_pool,
    hit_page,
    prefix_blocks,
    owners,
):
    device_count = lax.axis_size("dp")
    my_index = lax.axis_index("dp").astype(jnp.int32).reshape(1)
    heads_dev = dt_weight.shape[0]
    piece_count = hit_page.shape[2]
    row_width = 2 * HEAD_DIM + 2 * STATE
    channels = HEAD_DIM + 2 * STATE
    rows_dev = hidden.shape[0]
    pool_slots, state_rows, _ = state_pool.shape
    chip_count = device_count // 2
    half = chip_count // 2
    page_ids = jnp.swapaxes(hit_page, 1, 2)

    other_type = other_core(hidden, chip_count)
    page_rows = PER_PEER * state_rows + 8 * PER_PEER
    entries = REQS * heads_dev * piece_count
    offered = kernel_call(
        functools.partial(offer_kernel, entries),
        jax.ShapeDtypeStruct((device_count, page_rows, STATE), state_pool.dtype),
        [
            my_index,
            page_ids,
            from_hbm(state_pool),
            from_hbm(jnp.swapaxes(conv_pool, 0, 1)),
        ],
        [
            pltpu.SMEM((entries + 1,), jnp.int32),
            pltpu.VMEM((CONV - 1, pool_slots, STATE), jnp.float32),
            pltpu.VMEM((device_count, 8 * PER_PEER, STATE), jnp.float32),
        ],
        "offer_pages",
        smem=2,
        limit=VMEM_ALL,
    )
    own_type = stream(hidden, chip_count)
    first_other = other_type
    other_type = stream_other(hidden, chip_count)
    scalars = jnp.concatenate([my_index, prefix_blocks, owners])
    numbers = jnp.concatenate([dt_bias, decay_rate, skip])
    offered, own_type, other_type, scalars, numbers, held = lax.optimization_barrier(
        (offered, own_type, other_type, scalars, numbers, out_weight)
    )
    received = lax.all_to_all(offered, "dp", split_axis=0, concat_axis=0, tiled=True)
    held = other_core(held, chip_count)
    blocks = [from_hbm(hidden), first_other, own_type, other_type]
    blocks += [other_core(own_type, chip_count), other_core(other_type, chip_count)]
    early = early_stage(blocks, in_weight, from_hbm(dt_weight))
    pending = []
    for step in range(2, half):
        own_type = stream(own_type, chip_count)
        other_type = stream(other_type, chip_count)
        if step == 2:
            own_type, early = lax.optimization_barrier((own_type, early))
            staged = [early]
            received, weight_here, rates_here = lax.optimization_barrier(
                (received, in_weight, dt_weight)
            )
            weight_here, rates_here = load(weight_here, rates_here)
        if step == half - 1:
            own_type, weight_here = lax.optimization_barrier((own_type, weight_here))
        pending += [
            own_type,
            other_type,
            other_core(own_type, chip_count),
            other_core(other_type, chip_count),
        ]
        if len(pending) >= max(4, half) and step < half - 1:
            staged.append(stage(pending, weight_here, rates_here))
            pending = []
    own_type = stream(own_type, chip_count)
    last = [own_type, other_core(own_type, chip_count)]
    staged.append(stage(pending + last, weight_here, rates_here))

    live_rows = SPAN - BLK
    normed_rows = jax.ShapeDtypeStruct((chip_count * rows_dev, heads_dev * HEAD_DIM), jnp.bfloat16)
    final_state, final_conv, mine, theirs = kernel_call(
        functools.partial(mix_kernel, (heads_dev, piece_count, pool_slots, len(staged))),
        [
            jax.ShapeDtypeStruct((REQS, heads_dev, HEAD_DIM, STATE), jnp.float32),
            jax.ShapeDtypeStruct((REQS, CONV - 1, heads_dev * channels), jnp.bfloat16),
            normed_rows,
            normed_rows,
        ],
        [
            scalars,
            page_ids,
            numbers,
            received,
            conv_weight,
            conv_bias,
            norm_gain,
            *staged,
        ],
        [
            pltpu.VMEM((device_count, rows_dev, heads_dev * row_width + 128), jnp.float32),
            pltpu.VMEM((REQS, live_rows + 8, heads_dev * row_width), jnp.float32),
            pltpu.VMEM((REQS, live_rows, 128), jnp.float32),
            pltpu.VMEM((live_rows + 8, channels), jnp.float32),
            pltpu.VMEM((device_count, rows_dev, heads_dev * HEAD_DIM), jnp.float32),
            pltpu.VMEM((HEAD_DIM, STATE), jnp.float32),
            pltpu.VMEM(received.shape, jnp.float32),
            pltpu.SMEM((device_count,), jnp.int32),
            pltpu.SMEM((device_count,), jnp.int32),
        ],
        "mixer",
        flops=1 << 30,
        smem=3,
    )

    theirs = other_core(theirs, chip_count)
    width = out_weight.shape[1]
    total_rows = chip_count * rows_dev
    block = jax.ShapeDtypeStruct((rows_dev, width), jnp.bfloat16)
    part = kernel_call(
        part_kernel,
        jax.ShapeDtypeStruct((2 * rows_dev, width), jnp.float32),
        [mine, out_weight],
        [],
        "sums_part",
        flops=1 << 30,
    )
    first, second = kernel_call(
        functools.partial(first_kernel, rows_dev),
        [block, block],
        [part, theirs, held],
        [],
        "sums_first",
        flops=1 << 30,
    )
    own_sum = stream(first, chip_count)
    other_sum = stream(second, chip_count)
    shares = kernel_call(
        functools.partial(rest_kernel, rows_dev),
        jax.ShapeDtypeStruct((total_rows - 2 * rows_dev, width), jnp.float32),
        [mine, theirs, out_weight, held],
        [],
        "sums_rest",
        flops=1 << 30,
    )

    def onward(at, *arrived):
        top = (at - 2) * rows_dev
        return kernel_call(
            functools.partial(add_kernel, top), block, [shares, *arrived], [], "onward"
        )

    slots = send_slots(half)
    for at in range(2, len(slots) - 1):
        if slots[at][1] == 0:
            own_sum = stream(onward(at, own_sum), chip_count)
        else:
            other_sum = stream(onward(at, other_sum), chip_count)
    crossed = other_core(other_sum, chip_count)
    mixed = onward(len(slots) - 1, own_sum, crossed)
    return (mixed, final_state, final_conv)


def solution(mesh):
    return jax.shard_map(
        body,
        mesh=mesh,
        in_specs=(
            P(("groups", "dp"), None),
            P(None, "dp"),
            P("dp", None),
            P("dp"),
            P("dp"),
            P(None, "dp"),
            P("dp"),
            P("dp"),
            P("dp"),
            P("dp", None),
            P(("groups", "dp"), None, None),
            P(("groups", "dp"), None, None),
            P("groups", None, None),
            P("groups"),
            P("groups"),
        ),
        out_specs=(
            P(("groups", "dp"), None),
            P("groups", "dp", None, None),
            P("groups", None, "dp"),
        ),
        check_vma=False,
    )
```
